256 devices in a mesh: pool: 32 (over y, z_lo, core), tp: 8 (over x, z_hi).
Axes of the slice: x: 4, y: 4, z: 8 (z_hi: 2, z_lo: 4; z = z_hi * 4 + z_lo), core: 2. Of those that a mesh axis runs over, the one named last changes fastest.
Arguments:
- queries: bfloat16 [8192, 4096], P('pool', 'tp'), may hold values from -8 to 8
- new_key_values: bfloat16 [8192, 2048], P('pool', 'tp'), may hold values from -6 to 6
- key_value_store: bfloat16 [768, 256, 2048], P('pool', None, 'tp'), may hold values from -6 to 6
- o_weight: bfloat16 [4096, 8192], P('tp'), may hold values from -0.09375 to 0.09375
- residual: bfloat16 [8192, 8192], P(('pool', 'tp')), may hold values from -6 to 6
- hit_dev: int32 [64, 16], replicated, may hold values from 0 to 31, as said below
- hit_blk: int32 [64, 16], replicated, may hold values from 0 to 23
- prefix_len: int32 [64], replicated, may hold values from 3072 to 4096, as said below
Outputs:
- layer_out: bfloat16 [8192, 8192], P(('pool', 'tp'))
The draws below stay inside these ranges and needn't reach their ends.
Inputs may be any that keep to these rules, and one draw needn't show every extreme that they name: `hit_dev`: within one request the 16 pool indices are distinct. So one pool index sends at most one used block to each request, and at most 2 to the 2 requests held by any one pool index. `prefix_len`: some request has the full 16 * 256 tokens.
All inputs are finite; a program needn't handle non-finite values.
Results may differ from the reference program's by a relative error of at most 0.0085.
Values may be sent and summed in bfloat16 or wider, within the bound.
A program may use at most 128 MiB of HBM per device.

```python
import jax
import jax.numpy as jnp
from jax import lax

D = 8192
HEAD_SIZE = 128
QUERY_HEADS = 32
KEY_VALUE_HEADS = 8
NEW_TOKEN_COUNT = 128
PREFIX_BLOCK_LEN = 256
MAXB = 16
POOL_BLK = 24
REQ_DEV = 2
REQ = 64
ALL_NEW_TOKENS = 8192
STORED_BLOCK_NUM = 768
N_TP = 8


def draw_queries(key, part):
    key = jax.random.fold_in(key, 1)
    first = jax.random.fold_in(key, 0)
    array_shape = (ALL_NEW_TOKENS, QUERY_HEADS * HEAD_SIZE)
    values = jnp.clip(2.0 * jax.random.normal(first, array_shape, jnp.float32), -8.0, 8.0)
    return values.astype(jnp.bfloat16)


def draw_key_value_store(key, part):
    key = jax.random.fold_in(key, 2)
    first = jax.random.fold_in(key, 0)
    array_shape = (STORED_BLOCK_NUM, PREFIX_BLOCK_LEN, KEY_VALUE_HEADS * 2 * HEAD_SIZE)
    values = jnp.clip(jax.random.normal(first, array_shape, jnp.float32), -6.0, 6.0)
    return values.astype(jnp.bfloat16)


def draw_hit_dev(key, part):
    key = jax.random.fold_in(key, 3)
    first, second = jax.random.split(key, 2)
    npool = REQ // REQ_DEV
    keys = jax.random.split(first, REQ)
    perms = jax.vmap(lambda k: jax.random.permutation(k, npool))(keys).astype(jnp.int32)
    perms = perms.reshape(npool, REQ_DEV, npool)
    target = perms[:, 0, 0]
    where_at = jnp.argmax(perms == target[:, None, None], axis=2)
    leading = perms[:, :, 0]
    places = jnp.arange(npool, dtype=jnp.int32)
    moved = jnp.where(places[None, None, :] == where_at[:, :, None], leading[:, :, None], perms)
    moved = jnp.where(places[None, None, :] == 0, target[:, None, None], moved)
    chosen = jax.random.randint(second, (), 0, npool)
    flag = (jnp.arange(npool) == chosen)[:, None, None]
    result = jnp.where(flag, moved, perms)
    return result[:, :, :MAXB].reshape(REQ, MAXB).astype(jnp.int32)


def draw_prefix_len(key, part):
    key = jax.random.fold_in(key, 4)
    first, second = jax.random.split(key, 2)
    lengths = jax.random.randint(first, (REQ,), 3 * MAXB * PREFIX_BLOCK_LEN // 4, MAXB * PREFIX_BLOCK_LEN + 1)
    longest = jax.random.randint(second, (), 0, REQ)
    lengths = jnp.where(jnp.arange(REQ) == longest, MAXB * PREFIX_BLOCK_LEN, lengths)
    return lengths.astype(jnp.int32)


def touch_ends(entries, stream_key, smallest, high):
    spot = [jax.random.randint(jax.random.fold_in(stream_key, axis), (), 0, length) for axis, length in enumerate(entries.shape)]
    widest = entries.shape.index(max(entries.shape))
    next_to = spot[:widest] + [(spot[widest] + 1) % entries.shape[widest]] + spot[widest + 1:]
    return entries.at[tuple(spot)].set(smallest).at[tuple(next_to)].set(high)


def shard_levels(key, shape, pieces, low, largest):
    def one(axis_at, parts):
        steps = jax.random.uniform(jax.random.fold_in(jax.random.fold_in(key, 6), axis_at), (parts,), jnp.float32, low / len(pieces), largest / len(pieces))
        return jnp.repeat(jnp.exp(steps), shape[axis_at] // parts).reshape((-1,) + (1,) * (len(shape) - axis_at - 1))

    gain = one(*pieces[0])
    for cut in pieces[1:]:
        gain = gain * one(*cut)
    return gain


def normal_values(stream_key, extent, scale, bound, shards=(), kind=jnp.bfloat16):
    gain = shard_levels(stream_key, extent, shards, -0.22, 0.18) if shards else 1.0
    values = jax.random.normal(stream_key, extent, jnp.float32) * scale * gain
    return jnp.minimum(jnp.maximum(values, -bound), bound).astype(kind)


def setup_inputs(seed: int = 0) -> dict:
    key_of = jax.random.split(jax.random.key(seed), 9)
    queries = draw_queries(jax.random.fold_in(key_of[8], 71), 0)
    new_key_values = normal_values(key_of[1], (ALL_NEW_TOKENS, KEY_VALUE_HEADS * 2 * HEAD_SIZE), 1.0, 6.0, ((0, 32), (1, 8)))
    key_value_store = draw_key_value_store(jax.random.fold_in(key_of[8], 71), 0)
    o_weight = normal_values(key_of[3], (QUERY_HEADS * HEAD_SIZE, D), (QUERY_HEADS * HEAD_SIZE) ** -0.5, 0.09375, ((0, 8),))
    residual = normal_values(key_of[4], (ALL_NEW_TOKENS, D), 1.0, 6.0, ((0, 256),))
    hit_dev = draw_hit_dev(jax.random.fold_in(key_of[8], 71), 0)
    hit_blk = touch_ends(jax.random.randint(key_of[6], (REQ, MAXB), 0, POOL_BLK), jax.random.fold_in(key_of[6], 1), 0, POOL_BLK - 1).astype(jnp.int32)
    prefix_len = draw_prefix_len(jax.random.fold_in(key_of[8], 71), 0)
    return {"queries": queries, "new_key_values": new_key_values, "key_value_store": key_value_store, "o_weight": o_weight, "residual": residual, "hit_dev": hit_dev, "hit_blk": hit_blk, "prefix_len": prefix_len}


def reference(queries, new_key_values, key_value_store, o_weight, residual, hit_dev, hit_blk, prefix_len):
    query_group = QUERY_HEADS // KEY_VALUE_HEADS
    token_span = MAXB * PREFIX_BLOCK_LEN

    def one(request_index):
        block_index = hit_dev[request_index] * POOL_BLK + hit_blk[request_index]
        prefix_blocks = jnp.take(key_value_store, block_index, axis=0).reshape(token_span, KEY_VALUE_HEADS, 2, HEAD_SIZE)
        fresh_tokens = lax.dynamic_slice_in_dim(new_key_values, request_index * NEW_TOKEN_COUNT, NEW_TOKEN_COUNT, 0).reshape(NEW_TOKEN_COUNT, KEY_VALUE_HEADS, 2, HEAD_SIZE)
        keys = jnp.concatenate([prefix_blocks[:, :, 0], fresh_tokens[:, :, 0]], 0).astype(jnp.float32)
        values = jnp.concatenate([prefix_blocks[:, :, 1], fresh_tokens[:, :, 1]], 0).astype(jnp.float32)
        query_rows = lax.dynamic_slice_in_dim(queries, request_index * NEW_TOKEN_COUNT, NEW_TOKEN_COUNT, 0).reshape(NEW_TOKEN_COUNT, KEY_VALUE_HEADS, query_group, HEAD_SIZE).astype(jnp.float32)
        scores = jnp.einsum("ihgd,jhd->hgij", query_rows, keys) * (HEAD_SIZE ** -0.5)
        valid = jnp.arange(token_span, dtype=jnp.int32) < prefix_len[request_index]
        causal = jnp.arange(NEW_TOKEN_COUNT, dtype=jnp.int32)[None, :] <= jnp.arange(NEW_TOKEN_COUNT, dtype=jnp.int32)[:, None]
        allowed = jnp.concatenate([jnp.broadcast_to(valid[None, :], (NEW_TOKEN_COUNT, token_span)), causal], 1)
        scores = jnp.where(allowed, scores, -jnp.inf)
        rowmax = jnp.max(scores, axis=-1, keepdims=True)
        expo = jnp.exp(scores - rowmax)
        denom = jnp.sum(expo, axis=-1)
        probs = expo.astype(jnp.bfloat16).astype(jnp.float32)
        mixed = jnp.einsum("hgij,jhd->ihgd", probs, values)
        mixed = mixed / jnp.transpose(denom, (2, 0, 1))[..., None]
        return mixed.reshape(NEW_TOKEN_COUNT, QUERY_HEADS * HEAD_SIZE).astype(jnp.bfloat16)

    attn = lax.map(one, jnp.arange(REQ, dtype=jnp.int32)).reshape(ALL_NEW_TOKENS, QUERY_HEADS * HEAD_SIZE)
    width = QUERY_HEADS * HEAD_SIZE // N_TP

    def add_group(g, total):
        left = lax.dynamic_slice_in_dim(attn, g * width, width, 1)
        right = lax.dynamic_slice_in_dim(o_weight, g * width, width, 0)
        part = jnp.dot(left, right, preferred_element_type=jnp.float32).astype(jnp.bfloat16)
        part = lax.optimization_barrier(part)
        return total + part.astype(jnp.float32)

    total = lax.fori_loop(0, N_TP, add_group, jnp.zeros((ALL_NEW_TOKENS, D), jnp.float32))
    return (total + residual.astype(jnp.float32)).astype(jnp.bfloat16)
```

```python
import functools
import math

import jax
import jax.numpy as jnp
from jax import lax
from jax.experimental import pallas as pl
from jax.experimental.pallas import tpu as pltpu
from jax.sharding import PartitionSpec as P

HEAD = 128
NEW = 128
BLOCK = 256
MAXB = 16
NY = 4
NZ = 4
SLOTS = 4
LOG2_SCALE = HEAD**-0.5 * math.log2(math.e)
FLOOR = -1e30
ROWS = 144
MESH = pl.DeviceIdType.MESH


def nt(a, b):
    return lax.dot_general(a, b, (((1,), (1,)), ((), ())), preferred_element_type=jnp.float32)


def stacked(q):
    return jnp.concatenate([q[:, :HEAD], q[:, HEAD:]], axis=0)


def put(ref, at, o, m, l):
    ref[at + (slice(0, HEAD), slice(None))] = o.astype(jnp.bfloat16)
    high = l.astype(jnp.bfloat16).astype(jnp.float32)
    row = lax.broadcasted_iota(jnp.int32, (16, 2 * NEW), 0)
    stats = jnp.where(row == 0, m, jnp.where(row == 1, high, jnp.where(row == 2, l - high, 0.0)))
    ref[at + (slice(HEAD, ROWS), slice(None))] = stats.astype(jnp.bfloat16)


def get(ref, at):
    o = ref[at + (slice(0, HEAD), slice(None))].astype(jnp.float32)
    stats = ref[at + (slice(HEAD, ROWS), slice(None))].astype(jnp.float32)
    return o, stats[0:1], stats[1:2] + stats[2:3]


def merge(parts):
    m = functools.reduce(jnp.maximum, [p[1] for p in parts])
    o, l = 0.0, 0.0
    for po, pm, ps in parts:
        w = jnp.exp2(pm - m)
        o, l = o + po * w, l + ps * w
    return o, m, l


def attention_kernel(
    tab, q_ref, nkv_ref, kv_ref, out_ref,
    qbuf, k_sib, vt_own, vt_sib, nkv, part, r2, r1, rz, att, land,
    kv_send, kv_recv, nk_local,
    qz_send, qz_recv, qy_send, qy_recv, qr_send, qr_recv,
    p2_send, p2_recv, p1_send, p1_recv, pz_send, pz_recv, at_send, at_recv,
):
    me = lax.axis_index("pool")
    core = lax.rem(me, 2)
    mz = lax.rem(lax.div(me, 2), NZ)
    my = lax.div(me, 2 * NZ)
    up, down = lax.rem(my + 1, NY), lax.rem(my + NY - 1, NY)
    across = lax.rem(my + 2, NY)
    sib = 1 - core

    def dev(y, z, c):
        return (y * NZ + z) * 2 + c

    def remote(src, dst, send, recv, to):
        return pltpu.make_async_remote_copy(
            src_ref=src, dst_ref=dst, send_sem=send, recv_sem=recv, device_id={"pool": to}, device_id_type=MESH
        )

    barrier = pltpu.get_barrier_semaphore()
    partners = [dev(my, lax.rem(mz + k, NZ), c) for k in range(1, NZ) for c in range(2)]
    partners += [dev(my, mz, sib), dev(up, mz, core), dev(down, mz, core)]
    for p in partners:
        pl.semaphore_signal(barrier, inc=1, device_id={"pool": p}, device_id_type=MESH)
    pl.semaphore_wait(barrier, len(partners))

    def half(c):
        return pl.ds(pl.multiple_of(c * 2 * HEAD, 2 * HEAD), 2 * HEAD)

    def q_z(i, k, c):
        z = lax.rem(mz + k, NZ)
        s = i * 2 + core
        return remote(
            q_ref.at[pl.ds(i * NEW, NEW), half(c)], qbuf.at[s, my, mz],
            qz_send.at[i, k, c], qz_recv.at[s, mz], dev(my, z, c),
        )

    def q_sib(i):
        s = i * 2 + core
        return remote(
            q_ref.at[pl.ds(i * NEW, NEW), half(sib)], qbuf.at[s, my, mz],
            qz_send.at[i, 0, 0], qz_recv.at[s, mz], dev(my, mz, sib),
        )

    def q_own(i):
        s = i * 2 + core
        return pltpu.make_async_copy(
            q_ref.at[pl.ds(i * NEW, NEW), half(core)], qbuf.at[s, my, mz], qz_recv.at[s, mz]
        )

    nk_copy = remote(nkv_ref, nkv.at[core], kv_send.at[0], kv_recv.at[0], dev(my, mz, sib))
    k_copy = remote(kv_ref.at[:, :, pl.ds(0, HEAD)], k_sib, kv_send.at[1], kv_recv.at[1], dev(my, mz, sib))
    v_copy = remote(vt_own, vt_sib, kv_send.at[2], kv_recv.at[2], dev(my, mz, sib))
    nk_own = pltpu.make_async_copy(nkv_ref, nkv.at[core], nk_local)

    for i in range(2):
        for k in range(1, NZ):
            for c in range(2):
                q_z(i, k, c).start()
        q_sib(i).start()
        q_own(i).start()
    k_copy.start()
    nk_copy.start()
    nk_own.start()

    @pl.loop(0, kv_ref.shape[0])
    def _(b):
        vt_own[b] = kv_ref[b, :, HEAD:].T

    v_copy.start()

    def q_y(s, d):
        to = (up, down)[d]
        return remote(
            qbuf.at[s, my], qbuf.at[s, my], qy_send.at[s, d], qy_recv.at[s, d], dev(to, mz, core)
        )

    def q_relay(s, d):
        to, of = ((up, down), (down, up))[d]
        piece = qbuf.at[s, of, pl.ds(2 * d, 2)]
        return remote(piece, piece, qr_send.at[s, d], qr_recv.at[s, d], dev(to, mz, core))

    def wait_into(ref, sem):
        pltpu.make_async_copy(ref, ref, sem).wait()

    def stage_a(s):
        for z in range(NZ):
            wait_into(qbuf.at[s, my, z], qz_recv.at[s, z])
        q_y(s, 0).start()
        q_y(s, 1).start()

    def stage_r(s):
        wait_into(qbuf.at[s, down], qy_recv.at[s, 0])
        q_relay(s, 0).start()
        wait_into(qbuf.at[s, up], qy_recv.at[s, 1])
        q_relay(s, 1).start()

    key = lax.broadcasted_iota(jnp.int32, (BLOCK, 2 * NEW), 0)

    def attend(s, y, z):
        r = dev(y, z, lax.rem(s, 2)) * 2 + lax.div(s, 2)
        q = stacked(qbuf[s, y, z])
        codes = [tab[0, r], tab[1, r]]
        blocks = [c % 32 for c in codes]
        counts = [c // 32 for c in codes]
        keys = [kv_ref[blocks[0], :, :HEAD], k_sib[blocks[1]]]
        values = [vt_own[blocks[0]], vt_sib[blocks[1]]]
        t = [jnp.where(key < n, nt(k, q) * LOG2_SCALE, -jnp.inf) for k, n in zip(keys, counts)]
        m = jnp.maximum(jnp.max(t[0], axis=0, keepdims=True), jnp.max(t[1], axis=0, keepdims=True))
        m = jnp.maximum(m, FLOOR).astype(jnp.bfloat16).astype(jnp.float32)
        e = [jnp.exp2(x - m) for x in t]
        l = jnp.sum(e[0], axis=0, keepdims=True) + jnp.sum(e[1], axis=0, keepdims=True)
        o = [
            jnp.dot(v, x.astype(jnp.bfloat16), preferred_element_type=jnp.float32)
            for v, x in zip(values, e)
        ]
        put(part, (s, y, z), o[0] + o[1], m, l)

    def attend_column(s, y):
        @pl.loop(0, NZ)
        def _(z):
            attend(s, y, z)

    def p_2(s, d):
        to = (up, down)[d]
        return remote(
            part.at[s, across, pl.ds(2 * d, 2)], r2.at[s, d], p2_send.at[s, d], p2_recv.at[s, d], dev(to, mz, core)
        )

    def p_1(s, d):
        to = (up, down)[d]
        return remote(part.at[s, to], r1.at[s, d], p1_send.at[s, d], p1_recv.at[s, d], dev(to, mz, core))

    def p_z(s, k):
        z = lax.rem(mz + k, NZ)
        return remote(
            part.at[s, my, z], rz.at[s, mz], pz_send.at[s, k], pz_recv.at[s, mz], dev(my, z, core)
        )

    def stage_c(s):
        wait_into(qbuf.at[s, across, pl.ds(0, 2)], qr_recv.at[s, 0])
        wait_into(qbuf.at[s, across, pl.ds(2, 2)], qr_recv.at[s, 1])
        attend_column(s, across)
        p_2(s, 0).start()
        p_2(s, 1).start()
        attend_column(s, up)
        attend_column(s, down)

    def stage_m(s):
        for d in range(2):
            wait_into(r2.at[s, d], p2_recv.at[s, d])
            to = (up, down)[d]

            @pl.loop(0, 2)
            def _(j):
                put(part, (s, to, 2 * d + j), *merge([get(part, (s, to, 2 * d + j)), get(r2, (s, d, j))]))

            p_1(s, d).start()
        attend_column(s, my)

    def stage_h(s):
        for d in range(2):
            wait_into(r1.at[s, d], p1_recv.at[s, d])

        @pl.loop(0, NZ)
        def _(z):
            put(part, (s, my, z), *merge([get(part, (s, my, z)), get(r1, (s, 0, z)), get(r1, (s, 1, z))]))

        for k in range(1, NZ):
            p_z(s, k).start()

    def fresh(s):
        q = stacked(qbuf[s, my, mz])
        rows = nkv[lax.rem(s, 2), pl.ds(pl.multiple_of(lax.div(s, 2) * NEW, NEW), NEW), :]
        j = lax.broadcasted_iota(jnp.int32, (NEW, 2 * NEW), 0)
        i = lax.broadcasted_iota(jnp.int32, (NEW, 2 * NEW), 1) % NEW
        t = jnp.where(j <= i, nt(rows[:, :HEAD], q) * LOG2_SCALE, -jnp.inf)
        m = jnp.max(t, axis=0, keepdims=True).astype(jnp.bfloat16).astype(jnp.float32)
        e = jnp.exp2(t - m)
        o = jnp.dot(rows[:, HEAD:].T, e.astype(jnp.bfloat16), preferred_element_type=jnp.float32)
        return o, m, jnp.sum(e, axis=0, keepdims=True)

    def a_copy(s):
        i = lax.div(s, 2)
        return remote(att.at[s], land.at[i], at_send.at[i], at_recv.at[i], dev(my, mz, sib))

    def stage_f(s):
        parts = [fresh(s), get(part, (s, my, mz))]
        for k in range(1, NZ):
            z = lax.rem(mz + k, NZ)
            wait_into(rz.at[s, z], pz_recv.at[s, z])
            parts.append(get(rz, (s, z)))
        o, _, l = merge(parts)
        o = o / l
        att[s] = jnp.concatenate([o[:, :NEW].T, o[:, NEW:].T], axis=1).astype(jnp.bfloat16)

        @pl.when(lax.rem(s, 2) == core)
        def _():
            i = lax.div(s, 2)
            out_ref[pl.ds(pl.multiple_of(i * NEW, NEW), NEW), half(core)] = att[s]

        @pl.when(lax.rem(s, 2) != core)
        def _():
            a_copy(s).start()

    stage_a(0)
    stage_a(1)
    stage_r(0)
    nk_own.wait()
    for copy in (k_copy, nk_copy, v_copy):
        copy.wait_send()
    wait_into(nkv.at[sib], kv_recv.at[0])
    wait_into(k_sib, kv_recv.at[1])
    wait_into(vt_sib, kv_recv.at[2])

    @pl.loop(0, SLOTS + 2)
    def _(t):
        @pl.when(t < SLOTS)
        def _():
            stage_c(t)

        @pl.when(t + 1 < SLOTS)
        def _():
            stage_r(t + 1)

        @pl.when(t + 2 < SLOTS)
        def _():
            stage_a(t + 2)

        @pl.when(jnp.logical_and(t >= 1, t <= SLOTS))
        def _():
            stage_h(t - 1)

        @pl.when(t < SLOTS)
        def _():
            stage_m(t)

        @pl.when(t >= 2)
        def _():
            stage_f(t - 2)

    for i in range(2):
        for k in range(1, NZ):
            for c in range(2):
                q_z(i, k, c).wait_send()
        q_sib(i).wait_send()

    @pl.loop(0, SLOTS)
    def _(s):
        for d in range(2):
            q_y(s, d).wait_send()
            q_relay(s, d).wait_send()
            p_2(s, d).wait_send()
            p_1(s, d).wait_send()
        for k in range(1, NZ):
            p_z(s, k).wait_send()

    for i in range(2):
        a_copy(2 * i + sib).wait_send()
        wait_into(land.at[i], at_recv.at[i])
        out_ref[pl.ds(i * NEW, NEW), half(sib)] = land[i]


def attention(tab, queries, nkv, store):
    bf = jnp.bfloat16
    blocks = store.shape[0]
    vmem = pl.BlockSpec(memory_space=pltpu.VMEM)
    dma = pltpu.SemaphoreType.DMA
    unit = (ROWS, 2 * NEW)
    return pl.pallas_call(
        attention_kernel,
        out_shape=jax.ShapeDtypeStruct(queries.shape, bf),
        in_specs=[pl.BlockSpec(memory_space=pltpu.SMEM), vmem, vmem, vmem],
        out_specs=vmem,
        scratch_shapes=[
            pltpu.VMEM((SLOTS, NY, NZ, NEW, 2 * HEAD), bf),
            pltpu.VMEM((blocks, BLOCK, HEAD), bf),
            pltpu.VMEM((blocks, HEAD, BLOCK), bf),
            pltpu.VMEM((blocks, HEAD, BLOCK), bf),
            pltpu.VMEM((2, 2 * NEW, 2 * HEAD), bf),
            pltpu.VMEM((SLOTS, NY, NZ) + unit, bf),
            pltpu.VMEM((SLOTS, 2, 2) + unit, bf),
            pltpu.VMEM((SLOTS, 2, NZ) + unit, bf),
            pltpu.VMEM((SLOTS, NZ) + unit, bf),
            pltpu.VMEM((SLOTS, NEW, 2 * HEAD), bf),
            pltpu.VMEM((2, NEW, 2 * HEAD), bf),
            dma((3,)), dma((3,)), dma(()),
            dma((2, NZ, 2)), dma((SLOTS, NZ)),
            dma((SLOTS, 2)), dma((SLOTS, 2)), dma((SLOTS, 2)), dma((SLOTS, 2)),
            dma((SLOTS, 2)), dma((SLOTS, 2)), dma((SLOTS, 2)), dma((SLOTS, 2)),
            dma((SLOTS, NZ)), dma((SLOTS, NZ)), dma((2,)), dma((2,)),
        ],
        compiler_params=pltpu.CompilerParams(
            collective_id=0, has_side_effects=True, vmem_limit_bytes=40 * 1024 * 1024
        ),
    )(tab, queries, nkv, store)


def hit_table(hit_dev, hit_blk, prefix_len):
    me = lax.axis_index("pool")
    start = jnp.arange(MAXB, dtype=jnp.int32) * BLOCK
    count = jnp.clip(prefix_len[:, None] - start[None, :], 0, BLOCK)
    code = hit_blk + 32 * count
    return jnp.stack([jnp.sum(jnp.where(hit_dev == d, code, 0), axis=1) for d in (me, me + 1 - 2 * (me % 2))])


def shards(queries, new_key_values, key_value_store, o_weight, residual, hit_dev, hit_blk, prefix_len):
    tab = hit_table(hit_dev, hit_blk, prefix_len)
    attn = attention(tab, queries, new_key_values, key_value_store)
    mine = lax.psum_scatter(
        jnp.dot(attn, o_weight, preferred_element_type=jnp.float32).astype(jnp.bfloat16),
        "tp",
        scatter_dimension=0,
        tiled=True,
    ).astype(jnp.float32)
    return (mine + residual.astype(jnp.float32)).astype(jnp.bfloat16)


def solution(mesh):
    placed = (
        P("pool", "tp"),
        P("pool", "tp"),
        P("pool", None, "tp"),
        P("tp", None),
        P(("pool", "tp"), None),
        P(),
        P(),
        P(),
    )
    return jax.shard_map(
        shards, mesh=mesh, in_specs=placed, out_specs=P(("pool", "tp"), None), check_vma=False
    )
```

```python
import functools
import math

import jax
import jax.numpy as jnp
from jax import lax
from jax.experimental import pallas as pl
from jax.experimental.pallas import tpu as pltpu
from jax.sharding import PartitionSpec as P

HEAD = 128
NEW = 128
BLOCK = 256
MAXB = 16
NY = 4
NZ = 4
NX = 4
SLOTS = 4
CHUNKS = 2
LOG2_SCALE = HEAD**-0.5 * math.log2(math.e)
FLOOR = -1e30
ROWS = 144
MESH = pl.DeviceIdType.MESH


def nt(a, b):
    return lax.dot_general(a, b, (((1,), (1,)), ((), ())), preferred_element_type=jnp.float32)


def stacked(q):
    return jnp.concatenate([q[:, :HEAD], q[:, HEAD:]], axis=0)


def put(ref, at, o, m, l):
    ref[at + (slice(0, HEAD), slice(None))] = o.astype(jnp.bfloat16)
    high = l.astype(jnp.bfloat16).astype(jnp.float32)
    row = lax.broadcasted_iota(jnp.int32, (16, 2 * NEW), 0)
    stats = jnp.where(row == 0, m, jnp.where(row == 1, high, jnp.where(row == 2, l - high, 0.0)))
    ref[at + (slice(HEAD, ROWS), slice(None))] = stats.astype(jnp.bfloat16)


def get(ref, at):
    o = ref[at + (slice(0, HEAD), slice(None))].astype(jnp.float32)
    stats = ref[at + (slice(HEAD, ROWS), slice(None))].astype(jnp.float32)
    return o, stats[0:1], stats[1:2] + stats[2:3]


def merge(parts):
    m = functools.reduce(jnp.maximum, [p[1] for p in parts])
    o, l = 0.0, 0.0
    for po, pm, ps in parts:
        w = jnp.exp2(pm - m)
        o, l = o + po * w, l + ps * w
    return o, m, l


def layer_kernel(
    tab, q_ref, nkv_ref, kv_ref, res_ref, w_ref, out_ref,
    qbuf, k_sib, vt_own, vt_sib, nkv, part, r2, r1, rz, att,
    w, res_sib, proj, x1, x2, zout, zin, done, fin,
    kv_send, kv_recv, local,
    qz_send, qz_recv, qy_send, qy_recv, qr_send, qr_recv,
    p2_send, p2_recv, p1_send, p1_recv, pz_send, pz_recv, at_send, at_recv,
    x1_send, x1_recv, x2_send, x2_recv, zh_send, zh_recv, fin_send, fin_recv,
):
    me, tp = lax.axis_index("pool"), lax.axis_index("tp")
    core = lax.rem(me, 2)
    mz = lax.rem(lax.div(me, 2), NZ)
    my = lax.div(me, 2 * NZ)
    zh = lax.rem(tp, 2)
    mx = lax.div(tp, 2)
    up, down = lax.rem(my + 1, NY), lax.rem(my + NY - 1, NY)
    across = lax.rem(my + 2, NY)
    sib = 1 - core
    others = (mz + 1 - 2 * lax.rem(mz, 2), lax.rem(mz + 2, NZ), NZ - 1 - mz)
    pair, facing = mx + 1 - 2 * lax.rem(mx, 2), NX - 1 - mx
    width = w.shape[1]
    chunk = width // CHUNKS

    def dev(y, z, c):
        return (y * NZ + z) * 2 + c

    def tp_of(x, h):
        return x * 2 + h

    def remote(src, dst, send, recv, **to):
        return pltpu.make_async_remote_copy(
            src_ref=src, dst_ref=dst, send_sem=send, recv_sem=recv, device_id=to, device_id_type=MESH
        )

    def wait_into(ref, sem):
        pltpu.make_async_copy(ref, ref, sem).wait()

    barrier = pltpu.get_barrier_semaphore()
    partners = [{"pool": dev(my, z, c)} for z in others for c in range(2)]
    partners += [{"pool": p} for p in (dev(my, mz, sib), dev(up, mz, core), dev(down, mz, core))]
    partners += [{"tp": p} for p in (tp_of(pair, zh), tp_of(facing, zh), tp_of(mx, 1 - zh))]
    for p in partners:
        pl.semaphore_signal(barrier, inc=1, device_id=p, device_id_type=MESH)
    pl.semaphore_wait(barrier, len(partners))

    def half(c):
        return pl.ds(pl.multiple_of(c * 2 * HEAD, 2 * HEAD), 2 * HEAD)

    def columns(c):
        return pl.ds(pl.multiple_of(c * width, width), width)

    def owner(s):
        return lax.rem(s + lax.div(s, 2), 2)

    firsts = ((core, core), (sib, 2 + sib))

    def tokens(i):
        return pl.ds(pl.multiple_of(i * NEW, NEW), NEW)

    def q_z(j, k, c):
        i, s = firsts[j]
        return remote(
            q_ref.at[tokens(i), half(c)], qbuf.at[s, my, mz],
            qz_send.at[j, k, c], qz_recv.at[s, mz], pool=dev(my, others[k], c),
        )

    def q_sib(j):
        i, s = firsts[j]
        return remote(
            q_ref.at[tokens(i), half(sib)], qbuf.at[s, my, mz],
            qz_send.at[j, 3, 0], qz_recv.at[s, mz], pool=dev(my, mz, sib),
        )

    def q_own(j):
        i, s = firsts[j]
        return pltpu.make_async_copy(q_ref.at[tokens(i), half(core)], qbuf.at[s, my, mz], qz_recv.at[s, mz])

    here = dev(my, mz, sib)
    nk_copy = remote(nkv_ref, nkv.at[core], kv_send.at[0], kv_recv.at[0], pool=here)
    k_copy = remote(kv_ref.at[:, :, pl.ds(0, HEAD)], k_sib, kv_send.at[1], kv_recv.at[1], pool=here)
    v_copy = remote(vt_own, vt_sib, kv_send.at[2], kv_recv.at[2], pool=here)
    res_copy = remote(res_ref.at[:, columns(sib)], res_sib, kv_send.at[3], kv_recv.at[3], pool=here)
    nk_own = pltpu.make_async_copy(nkv_ref, nkv.at[core], local.at[0])
    w_own = pltpu.make_async_copy(w_ref.at[:, columns(core)], w, local.at[1])

    def q_y(s, d, z):
        piece = qbuf.at[s, my, z]
        return remote(piece, piece, qy_send.at[s, d, z], qy_recv.at[s, d, z], pool=dev((up, down)[d], mz, core))

    def q_relay(s, d, j):
        to, of = ((up, down), (down, up))[d]
        piece = qbuf.at[s, of, 2 * d + j]
        return remote(piece, piece, qr_send.at[s, d, j], qr_recv.at[s, d, j], pool=dev(to, mz, core))

    def z_arrived(s, z):
        wait_into(qbuf.at[s, my, z], qz_recv.at[s, z])
        q_y(s, 0, z).start()
        q_y(s, 1, z).start()

    def y_arrived(s, d, z):
        wait_into(qbuf.at[s, (down, up)[d], z], qy_recv.at[s, d, z])

    def stage_r(s):
        for j in range(2):
            for d in range(2):
                y_arrived(s, d, 2 * d + j)
                q_relay(s, d, j).start()

    for j in range(2):
        q_own(j).start()
        q_sib(j).start()
    for k in range(NZ - 1):
        for c in range(2):
            q_z(0, k, c).start()
    for s in range(2):
        z_arrived(s, mz)
    nk_own.start()
    nk_copy.start()
    k_copy.start()

    @pl.loop(0, kv_ref.shape[0])
    def _(b):
        vt_own[b] = kv_ref[b, :, HEAD:].T

    v_copy.start()
    for z in others:
        for s in range(2):
            z_arrived(s, z)
    for k in range(NZ - 1):
        for c in range(2):
            q_z(1, k, c).start()
    for s in range(2):
        z_arrived(2 + s, mz)
    res_copy.start()
    w_own.start()
    stage_r(0)

    key = lax.broadcasted_iota(jnp.int32, (BLOCK, 2 * NEW), 0)

    def attend(s, y, z):
        r = dev(y, z, owner(s)) * 2 + lax.rem(s, 2)
        q = stacked(qbuf[s, y, z])
        codes = [tab[0, r], tab[1, r]]
        blocks = [c % 32 for c in codes]
        counts = [c // 32 for c in codes]
        keys = [kv_ref[blocks[0], :, :HEAD], k_sib[blocks[1]]]
        values = [vt_own[blocks[0]], vt_sib[blocks[1]]]
        t = [jnp.where(key < n, nt(k, q) * LOG2_SCALE, -jnp.inf) for k, n in zip(keys, counts)]
        m = jnp.maximum(jnp.max(t[0], axis=0, keepdims=True), jnp.max(t[1], axis=0, keepdims=True))
        m = jnp.maximum(m, FLOOR).astype(jnp.bfloat16).astype(jnp.float32)
        e = [jnp.exp2(x - m) for x in t]
        l = jnp.sum(e[0], axis=0, keepdims=True) + jnp.sum(e[1], axis=0, keepdims=True)
        o = [
            jnp.dot(v, x.astype(jnp.bfloat16), preferred_element_type=jnp.float32)
            for v, x in zip(values, e)
        ]
        put(part, (s, y, z), o[0] + o[1], m, l)

    def p_2(s, d, j):
        return remote(
            part.at[s, across, 2 * d + j], r2.at[s, d, j],
            p2_send.at[s, d, j], p2_recv.at[s, d, j], pool=dev((up, down)[d], mz, core),
        )

    def p_1(s, d, z):
        to = (up, down)[d]
        return remote(
            part.at[s, to, z], r1.at[s, d, z], p1_send.at[s, d, z], p1_recv.at[s, d, z], pool=dev(to, mz, core)
        )

    def p_z(s, z):
        return remote(
            part.at[s, my, z], rz.at[s, mz], pz_send.at[s, z], pz_recv.at[s, mz], pool=dev(my, z, core)
        )

    def stage_c(s):
        for j in range(2):
            for d in range(2):
                wait_into(qbuf.at[s, across, 2 * d + j], qr_recv.at[s, d, j])
                y_arrived(s, d, 2 - 2 * d + j)

        @pl.loop(0, 2)
        def _(j):
            attend(s, across, j)
            attend(s, across, 2 + j)
            p_2(s, 0, j).start()
            p_2(s, 1, j).start()

        @pl.loop(0, 2)
        def _(j):
            attend(s, up, 2 + j)
            attend(s, down, j)
            p_1(s, 0, 2 + j).start()
            p_1(s, 1, j).start()

        @pl.loop(0, 2)
        def _(j):
            attend(s, up, j)
            attend(s, down, 2 + j)

    def stage_m(s):
        @pl.loop(0, 2)
        def _(j):
            for d in range(2):
                z, to = 2 * d + j, (up, down)[d]
                wait_into(r2.at[s, d, j], p2_recv.at[s, d, j])
                put(part, (s, to, z), *merge([get(part, (s, to, z)), get(r2, (s, d, j))]))
                p_1(s, d, z).start()

        @pl.loop(0, 2)
        def _(j):
            attend(s, my, j)
            attend(s, my, 2 + j)

    def stage_h(s):
        @pl.loop(0, NZ)
        def _(k):
            z = lax.rem(mz + 1 + k, NZ)
            for d in range(2):
                wait_into(r1.at[s, d, z], p1_recv.at[s, d, z])
            put(part, (s, my, z), *merge([get(part, (s, my, z)), get(r1, (s, 0, z)), get(r1, (s, 1, z))]))

            @pl.when(k < NZ - 1)
            def _():
                p_z(s, z).start()

    def fresh(s):
        q = stacked(qbuf[s, my, mz])
        rows = nkv[owner(s), tokens(lax.rem(s, 2)), :]
        j = lax.broadcasted_iota(jnp.int32, (NEW, 2 * NEW), 0)
        i = lax.broadcasted_iota(jnp.int32, (NEW, 2 * NEW), 1) % NEW
        t = jnp.where(j <= i, nt(rows[:, :HEAD], q) * LOG2_SCALE, -jnp.inf)
        m = jnp.max(t, axis=0, keepdims=True).astype(jnp.bfloat16).astype(jnp.float32)
        e = jnp.exp2(t - m)
        o = jnp.dot(rows[:, HEAD:].T, e.astype(jnp.bfloat16), preferred_element_type=jnp.float32)
        return o, m, jnp.sum(e, axis=0, keepdims=True)

    def a_copy(s):
        mine = att.at[s, :, half(core)]
        return remote(mine, mine, at_send.at[s], at_recv.at[s], pool=here)

    def stage_f(s):
        parts = [fresh(s), get(part, (s, my, mz))]
        for z in others:
            wait_into(rz.at[s, z], pz_recv.at[s, z])
            parts.append(get(rz, (s, z)))
        o, _, l = merge(parts)
        o = o / l
        att[s, :, half(core)] = jnp.concatenate([o[:, :NEW].T, o[:, NEW:].T], axis=1).astype(jnp.bfloat16)
        a_copy(s).start()

    def is_dest(s):
        return lax.div(mx, 2) == lax.rem(s, 2)

    def sent_half(s):
        return jnp.where(is_dest(s), 1 - lax.rem(mx, 2), lax.rem(mx, 2))

    def rows64(h):
        return pl.ds(pl.multiple_of(h * 64, 64), 64)

    def rows32(h, g):
        return pl.ds(pl.multiple_of(h * 64 + g * 32, 32), 32)

    def cols(n):
        return pl.ds(pl.multiple_of(n * chunk, chunk), chunk)

    def x_1(s, n):
        return remote(
            proj.at[s, rows64(sent_half(s)), cols(n)], x1.at[s, :, cols(n)],
            x1_send.at[s, n], x1_recv.at[s, n], tp=tp_of(pair, zh),
        )

    def x_2(s, n):
        return remote(
            proj.at[s, rows64(1 - sent_half(s)), cols(n)], x2.at[s, :, cols(n)],
            x2_send.at[s, n], x2_recv.at[s, n], tp=tp_of(facing, zh),
        )

    def z_h(s, n):
        return remote(
            zout.at[s, :, cols(n)], zin.at[s, :, cols(n)], zh_send.at[s, n], zh_recv.at[s, n], tp=tp_of(mx, 1 - zh)
        )

    def stage_o(s):
        @pl.when(s == 0)
        def _():
            w_own.wait()

        theirs = att.at[s, :, half(sib)]
        wait_into(theirs, at_recv.at[s])

        @pl.loop(0, CHUNKS)
        def _(n):
            proj[s, :, cols(n)] = jnp.dot(
                att[s], w[:, cols(n)], preferred_element_type=jnp.float32
            ).astype(jnp.bfloat16)
            x_1(s, n).start()

    def f32(x):
        return x.astype(jnp.float32)

    def stage_x(s):
        @pl.when(jnp.logical_not(is_dest(s)))
        def _():
            keep = 1 - sent_half(s)

            @pl.loop(0, CHUNKS)
            def _(n):
                wait_into(x1.at[s, :, cols(n)], x1_recv.at[s, n])
                total = f32(proj[s, rows64(keep), cols(n)]) + f32(x1[s, :, cols(n)])
                proj[s, rows64(keep), cols(n)] = total.astype(jnp.bfloat16)
                x_2(s, n).start()

    def stage_d(s):
        @pl.when(is_dest(s))
        def _():
            keep = 1 - sent_half(s)

            @pl.loop(0, CHUNKS)
            def _(n):
                wait_into(x1.at[s, :, cols(n)], x1_recv.at[s, n])
                wait_into(x2.at[s, :, cols(n)], x2_recv.at[s, n])
                g = 1 - zh
                total = f32(proj[s, rows32(keep, g), cols(n)])
                total += f32(x1[s, rows32(0, g), cols(n)]) + f32(x2[s, rows32(0, g), cols(n)])
                zout[s, :, cols(n)] = total.astype(jnp.bfloat16)
                z_h(s, n).start()

    def fin_copy():
        return remote(done, fin, fin_send, fin_recv, pool=here)

    def stage_e(s):
        @pl.when(is_dest(s))
        def _():
            keep = 1 - sent_half(s)
            mine = owner(s) == core

            def total(n):
                wait_into(zin.at[s, :, cols(n)], zh_recv.at[s, n])
                t = f32(proj[s, rows32(keep, zh), cols(n)]) + f32(zin[s, :, cols(n)])
                return t + f32(x1[s, rows32(0, zh), cols(n)]) + f32(x2[s, rows32(0, zh), cols(n)])

            def at(n):
                return pl.ds(pl.multiple_of(core * width + n * chunk, chunk), chunk)

            @pl.when(mine)
            def _():
                @pl.loop(0, CHUNKS)
                def _(n):
                    out_ref[:, at(n)] = (total(n) + f32(res_ref[:, at(n)])).astype(jnp.bfloat16)

            @pl.when(jnp.logical_not(mine))
            def _():
                wait_into(res_sib, kv_recv.at[3])

                @pl.loop(0, CHUNKS)
                def _(n):
                    done[:, cols(n)] = (total(n) + f32(res_sib[:, cols(n)])).astype(jnp.bfloat16)

                fin_copy().start()

    nk_own.wait()
    for copy in (k_copy, nk_copy, v_copy, res_copy):
        copy.wait_send()
    wait_into(nkv.at[sib], kv_recv.at[0])
    wait_into(k_sib, kv_recv.at[1])
    wait_into(vt_sib, kv_recv.at[2])

    @pl.loop(0, SLOTS + 5)
    def _(t):
        def stage(f, s):
            @pl.when(jnp.logical_and(s >= 0, s < SLOTS))
            def _():
                f(s)

        stage(stage_c, t)
        stage(stage_h, t - 1)

        @pl.when(t + 1 < SLOTS)
        def _():
            @pl.when(t >= 1)
            def _():
                for z in others:
                    z_arrived(t + 1, z)

            stage_r(t + 1)

        stage(stage_m, t)
        stage(stage_x, t - 3)
        stage(stage_d, t - 4)
        stage(stage_e, t - 5)
        stage(stage_o, t - 2)
        stage(stage_f, t - 1)

    for j in range(2):
        for k in range(NZ - 1):
            for c in range(2):
                q_z(j, k, c).wait_send()
        q_sib(j).wait_send()

    @pl.loop(0, SLOTS)
    def _(s):
        for d in range(2):
            for z in range(NZ):
                q_y(s, d, z).wait_send()
                p_1(s, d, z).wait_send()
            for j in range(2):
                q_relay(s, d, j).wait_send()
                p_2(s, d, j).wait_send()
        for z in others:
            p_z(s, z).wait_send()
        a_copy(s).wait_send()
        for n in range(CHUNKS):
            x_1(s, n).wait_send()

            @pl.when(is_dest(s))
            def _():
                z_h(s, n).wait_send()

            @pl.when(jnp.logical_not(is_dest(s)))
            def _():
                x_2(s, n).wait_send()

    fin_copy().wait_send()
    wait_into(fin, fin_recv)
    out_ref[:, columns(sib)] = fin[...]


def layer(tab, queries, nkv, store, residual, weight):
    bf = jnp.bfloat16
    blocks = store.shape[0]
    depth, width = weight.shape[0], weight.shape[1] // 2
    rows = residual.shape[0]
    vmem = pl.BlockSpec(memory_space=pltpu.VMEM)
    dma = pltpu.SemaphoreType.DMA
    unit = (ROWS, 2 * NEW)
    each = [dma((SLOTS, CHUNKS))] * 2
    return pl.pallas_call(
        layer_kernel,
        out_shape=jax.ShapeDtypeStruct(residual.shape, bf),
        in_specs=[pl.BlockSpec(memory_space=pltpu.SMEM)] + [vmem] * 4 + [pl.BlockSpec(memory_space=pl.ANY)],
        out_specs=vmem,
        scratch_shapes=[
            pltpu.VMEM((SLOTS, NY, NZ, NEW, 2 * HEAD), bf),
            pltpu.VMEM((blocks, BLOCK, HEAD), bf),
            pltpu.VMEM((blocks, HEAD, BLOCK), bf),
            pltpu.VMEM((blocks, HEAD, BLOCK), bf),
            pltpu.VMEM((2, 2 * NEW, 2 * HEAD), bf),
            pltpu.VMEM((SLOTS, NY, NZ) + unit, bf),
            pltpu.VMEM((SLOTS, 2, 2) + unit, bf),
            pltpu.VMEM((SLOTS, 2, NZ) + unit, bf),
            pltpu.VMEM((SLOTS, NZ) + unit, bf),
            pltpu.VMEM((SLOTS, NEW, 4 * HEAD), bf),
            pltpu.VMEM((depth, width), bf),
            pltpu.VMEM((rows, width), bf),
            pltpu.VMEM((SLOTS, NEW, width), bf),
            pltpu.VMEM((SLOTS, NEW // 2, width), bf),
            pltpu.VMEM((SLOTS, NEW // 2, width), bf),
            pltpu.VMEM((SLOTS, NEW // 4, width), bf),
            pltpu.VMEM((SLOTS, NEW // 4, width), bf),
            pltpu.VMEM((rows, width), bf),
            pltpu.VMEM((rows, width), bf),
            dma((4,)), dma((4,)), dma((2,)),
            dma((2, NZ, 2)), dma((SLOTS, NZ)),
            dma((SLOTS, 2, NZ)), dma((SLOTS, 2, NZ)), dma((SLOTS, 2, 2)), dma((SLOTS, 2, 2)),
            dma((SLOTS, 2, 2)), dma((SLOTS, 2, 2)), dma((SLOTS, 2, NZ)), dma((SLOTS, 2, NZ)),
            dma((SLOTS, NZ)), dma((SLOTS, NZ)), dma((SLOTS,)), dma((SLOTS,)),
            *each, *each, *each, dma(()), dma(()),
        ],
        compiler_params=pltpu.CompilerParams(
            collective_id=0, has_side_effects=True, vmem_limit_bytes=56 * 1024 * 1024
        ),
    )(tab, queries, nkv, store, residual, weight)


def hit_table(hit_dev, hit_blk, prefix_len):
    me = lax.axis_index("pool")
    start = jnp.arange(MAXB, dtype=jnp.int32) * BLOCK
    count = jnp.clip(prefix_len[:, None] - start[None, :], 0, BLOCK)
    code = hit_blk + 32 * count
    return jnp.stack([jnp.sum(jnp.where(hit_dev == d, code, 0), axis=1) for d in (me, me + 1 - 2 * (me % 2))])


def shards(queries, new_key_values, key_value_store, o_weight, residual, hit_dev, hit_blk, prefix_len):
    tab = hit_table(hit_dev, hit_blk, prefix_len)
    return layer(tab, queries, new_key_values, key_value_store, residual, o_weight)


def solution(mesh):
    placed = (
        P("pool", "tp"),
        P("pool", "tp"),
        P("pool", None, "tp"),
        P("tp", None),
        P(("pool", "tp"), None),
        P(),
        P(),
        P(),
    )
    return jax.shard_map(
        shards, mesh=mesh, in_specs=placed, out_specs=P(("pool", "tp"), None), check_vma=False
    )
```

```python
import functools
import math

import jax
import jax.numpy as jnp
from jax import lax
from jax.experimental import pallas as pl
from jax.experimental.pallas import tpu as pltpu
from jax.sharding import PartitionSpec as P

HEAD = 128
NEW = 128
BLOCK = 256
MAXB = 16
NY = 4
NZ = 4
NX = 4
PART = 16
SLOTS = 8
CHUNKS = 4
LOG2_SCALE = HEAD**-0.5 * math.log2(math.e)
FLOOR = -1e30
ROWS = 144
MESH = pl.DeviceIdType.MESH


def nt(a, b):
    return lax.dot_general(a, b, (((1,), (1,)), ((), ())), preferred_element_type=jnp.float32)


def put(ref, at, o, m, l):
    ref[at + (slice(0, HEAD), slice(None))] = o.astype(jnp.bfloat16)
    high = l.astype(jnp.bfloat16).astype(jnp.float32)
    row = lax.broadcasted_iota(jnp.int32, (16, NEW), 0)
    stats = jnp.where(row == 0, m, jnp.where(row == 1, high, jnp.where(row == 2, l - high, 0.0)))
    ref[at + (slice(HEAD, ROWS), slice(None))] = stats.astype(jnp.bfloat16)


def get(ref, at):
    o = ref[at + (slice(0, HEAD), slice(None))].astype(jnp.float32)
    stats = ref[at + (slice(HEAD, ROWS), slice(None))].astype(jnp.float32)
    return o, stats[0:1], stats[1:2] + stats[2:3]


def merge(parts):
    m = functools.reduce(jnp.maximum, [p[1] for p in parts])
    o, l = 0.0, 0.0
    for po, pm, ps in parts:
        w = jnp.exp2(pm - m)
        o, l = o + po * w, l + ps * w
    return o, m, l


def layer_kernel(
    tab, q_ref, nkv_ref, res_ref, store_ref, w_ref, out_ref,
    kv_ref, qsrc, qbuf, k_sib, vt_own, vt_sib, nkv, part, r2, r1, rz, att,
    w, res_sib, proj, x1, x2, zout, zin, done, fin,
    kv_send, kv_recv, local,
    qz_send, qz_recv, qy_send, qy_recv, qr_send, qr_recv,
    p2_send, p2_recv, p1_send, p1_recv, pz_send, pz_recv, at_send, at_recv,
    x1_send, x1_recv, x2_send, x2_recv, zh_send, zh_recv, fin_send, fin_recv,
):
    kv_own = pltpu.make_async_copy(store_ref, kv_ref, local.at[2])
    kv_own.start()
    me, tp = lax.axis_index("pool"), lax.axis_index("tp")
    core = lax.rem(me, 2)
    mz = lax.rem(lax.div(me, 2), NZ)
    my = lax.div(me, 2 * NZ)
    zh = lax.rem(tp, 2)
    mx = lax.div(tp, 2)
    up, down = lax.rem(my + 1, NY), lax.rem(my + NY - 1, NY)
    across = lax.rem(my + 2, NY)
    sib = 1 - core
    others = (mz + 1 - 2 * lax.rem(mz, 2), lax.rem(mz + 2, NZ), NZ - 1 - mz)
    pair, facing = mx + 1 - 2 * lax.rem(mx, 2), NX - 1 - mx
    width = w.shape[1]
    chunk = width // CHUNKS

    def dev(y, z, c):
        return (y * NZ + z) * 2 + c

    def tp_of(x, h):
        return x * 2 + h

    def remote(src, dst, send, recv, **to):
        return pltpu.make_async_remote_copy(
            src_ref=src, dst_ref=dst, send_sem=send, recv_sem=recv, device_id=to, device_id_type=MESH
        )

    def wait_into(ref, sem):
        pltpu.make_async_copy(ref, ref, sem).wait()

    barrier = pltpu.get_barrier_semaphore()
    partners = [{"pool": dev(my, z, c)} for z in others for c in range(2)]
    partners += [{"pool": p} for p in (dev(my, mz, sib), dev(up, mz, core), dev(down, mz, core))]
    partners += [{"tp": p} for p in (tp_of(pair, zh), tp_of(facing, zh), tp_of(mx, 1 - zh))]
    for p in partners:
        pl.semaphore_signal(barrier, inc=1, device_id=p, device_id_type=MESH)

    for i in range(2):
        for g in range(2):
            for h in range(4):
                for b in range(4):
                    to, at = (h % 2 * 4 + b) * PART, i * NEW + (2 * b + g) * PART
                    qsrc[i, g, h // 2, to : to + PART, :] = q_ref[at : at + PART, h * HEAD : (h + 1) * HEAD]

    pl.semaphore_wait(barrier, len(partners))

    def half(c):
        return pl.ds(pl.multiple_of(c * 2 * HEAD, 2 * HEAD), 2 * HEAD)

    def columns(c):
        return pl.ds(pl.multiple_of(c * width, width), width)

    def owner(s):
        return lax.rem(s, 2)

    def which(s):
        return lax.rem(lax.div(s, 2) + lax.rem(s, 2), 2)

    def share(s):
        return lax.div(s, 4)

    def tokens(i):
        return pl.ds(pl.multiple_of(i * NEW, NEW), NEW)

    def q_z(j, k, c):
        s = 2 * j + core
        return remote(
            qsrc.at[which(s), lax.div(j, 2), c], qbuf.at[s, my, mz],
            qz_send.at[j, k, c], qz_recv.at[s, mz], pool=dev(my, others[k], c),
        )

    def q_sib(j):
        s = 2 * j + core
        return remote(
            qsrc.at[which(s), j // 2, sib], qbuf.at[s, my, mz],
            qz_send.at[j, 3, 0], qz_recv.at[s, mz], pool=dev(my, mz, sib),
        )

    def q_own(j):
        s = 2 * j + core
        return pltpu.make_async_copy(qsrc.at[which(s), j // 2, core], qbuf.at[s, my, mz], qz_recv.at[s, mz])

    here = dev(my, mz, sib)
    nk_copy = remote(nkv_ref, nkv.at[core], kv_send.at[0], kv_recv.at[0], pool=here)
    k_copy = remote(kv_ref.at[:, :, pl.ds(0, HEAD)], k_sib, kv_send.at[1], kv_recv.at[1], pool=here)
    v_copy = remote(vt_own, vt_sib, kv_send.at[2], kv_recv.at[2], pool=here)
    res_copy = remote(res_ref.at[:, columns(sib)], res_sib, kv_send.at[3], kv_recv.at[3], pool=here)
    nk_own = pltpu.make_async_copy(nkv_ref, nkv.at[core], local.at[0])
    w_own = pltpu.make_async_copy(w_ref.at[:, columns(core)], w, local.at[1])

    def q_y(s, d, z):
        piece = qbuf.at[s, my, z]
        return remote(piece, piece, qy_send.at[s, d, z], qy_recv.at[s, d, z], pool=dev((up, down)[d], mz, core))

    def q_relay(s, d, j):
        to, of = ((up, down), (down, up))[d]
        piece = qbuf.at[s, of, 2 * d + j]
        return remote(piece, piece, qr_send.at[s, d, j], qr_recv.at[s, d, j], pool=dev(to, mz, core))

    def z_arrived(s, z):
        wait_into(qbuf.at[s, my, z], qz_recv.at[s, z])
        q_y(s, 0, z).start()
        q_y(s, 1, z).start()

    def y_arrived(s, d, z):
        wait_into(qbuf.at[s, (down, up)[d], z], qy_recv.at[s, d, z])

    def relay_two(s, j):
        for d in range(2):
            y_arrived(s, d, 2 * d + j)
            q_relay(s, d, j).start()

    def stage_r(s):
        for j in range(2):
            relay_two(s, j)

    per_core = SLOTS // 2

    def send_z(j):
        for k in range(NZ - 1):
            for c in range(2):
                q_z(j, k, c).start()

    for j in range(per_core):
        q_own(j).start()
        q_sib(j).start()
        if j == 0:
            send_z(0)
    for s in range(4):
        z_arrived(s, mz)
    nk_own.start()
    nk_copy.start()
    kv_own.wait()
    k_copy.start()

    @pl.loop(0, kv_ref.shape[0])
    def _(b):
        vt_own[b] = kv_ref[b, :, HEAD:].T

    v_copy.start()
    for z in others:
        z_arrived(0, z)
        z_arrived(1, z)
    send_z(1)
    res_copy.start()
    w_own.start()
    stage_r(0)

    key = lax.broadcasted_iota(jnp.int32, (BLOCK, NEW), 0)

    def attend(s, y, z):
        r = dev(y, z, owner(s)) * 2 + which(s)
        q = qbuf[s, y, z]
        codes = [tab[0, r], tab[1, r]]
        blocks = [c % 32 for c in codes]
        counts = [c // 32 for c in codes]
        keys = [kv_ref[blocks[0], :, :HEAD], k_sib[blocks[1]]]
        values = [vt_own[blocks[0]], vt_sib[blocks[1]]]
        t = [jnp.where(key < n, nt(k, q) * LOG2_SCALE, -jnp.inf) for k, n in zip(keys, counts)]
        m = jnp.maximum(jnp.max(t[0], axis=0, keepdims=True), jnp.max(t[1], axis=0, keepdims=True))
        m = jnp.maximum(m, FLOOR).astype(jnp.bfloat16).astype(jnp.float32)
        e = [jnp.exp2(x - m) for x in t]
        l = jnp.sum(e[0], axis=0, keepdims=True) + jnp.sum(e[1], axis=0, keepdims=True)
        o = [
            jnp.dot(v, x.astype(jnp.bfloat16), preferred_element_type=jnp.float32)
            for v, x in zip(values, e)
        ]
        put(part, (s, y, z), o[0] + o[1], m, l)

    def p_2(s, d, j):
        return remote(
            part.at[s, across, 2 * d + j], r2.at[s, d, j],
            p2_send.at[s, d, j], p2_recv.at[s, d, j], pool=dev((up, down)[d], mz, core),
        )

    def p_1(s, d, z):
        to = (up, down)[d]
        return remote(
            part.at[s, to, z], r1.at[s, d, z], p1_send.at[s, d, z], p1_recv.at[s, d, z], pool=dev(to, mz, core)
        )

    def p_z(s, z):
        return remote(
            part.at[s, my, z], rz.at[s, mz], pz_send.at[s, z], pz_recv.at[s, mz], pool=dev(my, z, core)
        )

    def stage_c(s):
        for j in range(2):
            for d in range(2):
                wait_into(qbuf.at[s, across, 2 * d + j], qr_recv.at[s, d, j])
                y_arrived(s, d, 2 - 2 * d + j)

        for z in range(NZ):
            attend(s, across, z)
        for j in range(2):
            p_2(s, 0, j).start()
            p_2(s, 1, j).start()

        @pl.when(s == 0)
        def _():
            for z in others:
                z_arrived(2, z)

        for j in range(2):
            attend(s, up, 2 + j)
            attend(s, down, j)
        for j in range(2):
            p_1(s, 0, 2 + j).start()
            p_1(s, 1, j).start()

        @pl.when(s == 0)
        def _():
            stage_r(1)

        for j in range(2):
            attend(s, up, j)
            attend(s, down, 2 + j)
        for z in range(NZ):
            attend(s, my, z)

        @pl.when(s + 2 < SLOTS)
        def _():
            stage_r(s + 2)

    def stage_m(s):
        @pl.loop(0, 2)
        def _(j):
            for d in range(2):
                z, to = 2 * d + j, (up, down)[d]
                wait_into(r2.at[s, d, j], p2_recv.at[s, d, j])
                put(part, (s, to, z), *merge([get(part, (s, to, z)), get(r2, (s, d, j))]))
                p_1(s, d, z).start()

        @pl.when(s + 4 < SLOTS)
        def _():
            z_arrived(s + 4, mz)

        @pl.when(s + 3 < SLOTS)
        def _():
            for z in others:
                z_arrived(s + 3, z)

        @pl.when(jnp.logical_or(s == 0, s == 2))
        def _():
            send_z(lax.div(s, 2) + 2)

    def stage_h(s):
        @pl.loop(0, NZ)
        def _(k):
            z = lax.rem(mz + 1 + k, NZ)
            for d in range(2):
                wait_into(r1.at[s, d, z], p1_recv.at[s, d, z])
            put(part, (s, my, z), *merge([get(part, (s, my, z)), get(r1, (s, 0, z)), get(r1, (s, 1, z))]))

            @pl.when(k < NZ - 1)
            def _():
                p_z(s, z).start()

    def fresh(s):
        q = qbuf[s, my, mz]
        rows = nkv[owner(s), tokens(which(s)), :]
        j = lax.broadcasted_iota(jnp.int32, (NEW, NEW), 0)
        i = lax.broadcasted_iota(jnp.int32, (NEW, NEW), 1) % (4 * PART)
        i = i + i // PART * PART + share(s) * PART
        t = jnp.where(j <= i, nt(rows[:, :HEAD], q) * LOG2_SCALE, -jnp.inf)
        m = jnp.max(t, axis=0, keepdims=True).astype(jnp.bfloat16).astype(jnp.float32)
        e = jnp.exp2(t - m)
        o = jnp.dot(rows[:, HEAD:].T, e.astype(jnp.bfloat16), preferred_element_type=jnp.float32)
        return o, m, jnp.sum(e, axis=0, keepdims=True)

    def a_copy(s):
        mine = att.at[s, :, half(core)]
        return remote(mine, mine, at_send.at[s], at_recv.at[s], pool=here)

    def stage_f(s):
        parts = [fresh(s), get(part, (s, my, mz))]
        for z in others:
            wait_into(rz.at[s, z], pz_recv.at[s, z])
            parts.append(get(rz, (s, z)))
        o, _, l = merge(parts)
        o = o / l
        o = o.T
        att[s, :, half(core)] = jnp.concatenate([o[: 4 * PART], o[4 * PART :]], axis=1).astype(jnp.bfloat16)
        a_copy(s).start()

    def is_dest(s):
        return lax.div(mx, 2) == which(s)

    def sent_half(s):
        return jnp.where(is_dest(s), 1 - lax.rem(mx, 2), lax.rem(mx, 2))

    def rows(h):
        return pl.ds(pl.multiple_of(h * 2 * PART, 2 * PART), 2 * PART)

    def part_of(h, z):
        return pl.ds(pl.multiple_of((2 * h + z) * PART, PART), PART)

    def cols(n):
        return pl.ds(pl.multiple_of(n * chunk, chunk), chunk)

    def x_1(s, n):
        return remote(
            proj.at[s, rows(sent_half(s)), cols(n)], x1.at[s, :, cols(n)],
            x1_send.at[s, n], x1_recv.at[s, n], tp=tp_of(pair, zh),
        )

    def x_2(s, n):
        return remote(
            proj.at[s, rows(1 - sent_half(s)), cols(n)], x2.at[s, :, cols(n)],
            x2_send.at[s, n], x2_recv.at[s, n], tp=tp_of(facing, zh),
        )

    def z_h(s, n):
        return remote(
            zout.at[s, :, cols(n)], zin.at[s, :, cols(n)], zh_send.at[s, n], zh_recv.at[s, n], tp=tp_of(mx, 1 - zh)
        )

    def stage_o(s):
        @pl.when(s == 0)
        def _():
            w_own.wait()

        theirs = att.at[s, :, half(sib)]
        wait_into(theirs, at_recv.at[s])

        @pl.loop(0, CHUNKS)
        def _(n):
            proj[s, :, cols(n)] = jnp.dot(
                att[s], w[:, cols(n)], preferred_element_type=jnp.float32
            ).astype(jnp.bfloat16)
            x_1(s, n).start()

    def f32(x):
        return x.astype(jnp.float32)

    def stage_x(s):
        @pl.when(jnp.logical_not(is_dest(s)))
        def _():
            keep = 1 - sent_half(s)

            @pl.loop(0, CHUNKS)
            def _(n):
                wait_into(x1.at[s, :, cols(n)], x1_recv.at[s, n])
                total = f32(proj[s, rows(keep), cols(n)]) + f32(x1[s, :, cols(n)])
                proj[s, rows(keep), cols(n)] = total.astype(jnp.bfloat16)
                x_2(s, n).start()

    def stage_d(s):
        @pl.when(is_dest(s))
        def _():
            keep = 1 - sent_half(s)

            @pl.loop(0, CHUNKS)
            def _(n):
                wait_into(x1.at[s, :, cols(n)], x1_recv.at[s, n])
                wait_into(x2.at[s, :, cols(n)], x2_recv.at[s, n])
                z = 1 - zh
                total = f32(proj[s, part_of(keep, z), cols(n)])
                total += f32(x1[s, part_of(0, z), cols(n)]) + f32(x2[s, part_of(0, z), cols(n)])
                zout[s, :, cols(n)] = total.astype(jnp.bfloat16)
                z_h(s, n).start()

    def fin_copy(g):
        return remote(done.at[g], fin.at[g], fin_send.at[g], fin_recv.at[g], pool=here)

    def stage_e(s):
        @pl.when(is_dest(s))
        def _():
            keep = 1 - sent_half(s)
            mine = owner(s) == core
            g = share(s)
            out_rows = pl.ds(pl.multiple_of(g * PART, PART), PART)

            def total(n):
                wait_into(zin.at[s, :, cols(n)], zh_recv.at[s, n])
                t = f32(proj[s, part_of(keep, zh), cols(n)]) + f32(zin[s, :, cols(n)])
                return t + f32(x1[s, part_of(0, zh), cols(n)]) + f32(x2[s, part_of(0, zh), cols(n)])

            def at(n):
                return pl.ds(pl.multiple_of(core * width + n * chunk, chunk), chunk)

            @pl.when(mine)
            def _():
                @pl.loop(0, CHUNKS)
                def _(n):
                    out_ref[out_rows, at(n)] = (total(n) + f32(res_ref[out_rows, at(n)])).astype(jnp.bfloat16)

            @pl.when(jnp.logical_not(mine))
            def _():
                @pl.loop(0, CHUNKS)
                def _(n):
                    done[g, :, cols(n)] = (total(n) + f32(res_sib[out_rows, cols(n)])).astype(jnp.bfloat16)

                fin_copy(g).start()

    nk_own.wait()
    for copy in (k_copy, nk_copy, v_copy, res_copy):
        copy.wait_send()
    wait_into(nkv.at[sib], kv_recv.at[0])
    wait_into(k_sib, kv_recv.at[1])
    wait_into(vt_sib, kv_recv.at[2])
    wait_into(res_sib, kv_recv.at[3])

    @pl.loop(0, SLOTS + 2)
    def _(t):
        def stage(f, s):
            @pl.when(jnp.logical_and(s >= 0, s < SLOTS))
            def _():
                f(s)

        stage(stage_c, t)
        stage(stage_h, t - 1)
        stage(stage_f, t - 2)
        stage(stage_m, t)
        stage(stage_d, t - 5)
        stage(stage_o, t - 2)
        stage(stage_x, t - 3)

    stage_x(SLOTS - 1)
    for s in range(SLOTS - 3, SLOTS):
        stage_d(s)

    @pl.loop(0, SLOTS)
    def _(s):
        stage_e(s)

    for j in range(per_core):
        for k in range(NZ - 1):
            for c in range(2):
                q_z(j, k, c).wait_send()
        q_sib(j).wait_send()

    @pl.loop(0, SLOTS)
    def _(s):
        for d in range(2):
            for z in range(NZ):
                q_y(s, d, z).wait_send()
                p_1(s, d, z).wait_send()
            for j in range(2):
                q_relay(s, d, j).wait_send()
                p_2(s, d, j).wait_send()
        for z in others:
            p_z(s, z).wait_send()
        a_copy(s).wait_send()
        for n in range(CHUNKS):
            x_1(s, n).wait_send()

            @pl.when(is_dest(s))
            def _():
                z_h(s, n).wait_send()

            @pl.when(jnp.logical_not(is_dest(s)))
            def _():
                x_2(s, n).wait_send()

    for g in range(2):
        fin_copy(g).wait_send()
        wait_into(fin.at[g], fin_recv.at[g])
        out_ref[g * PART : (g + 1) * PART, columns(sib)] = fin[g]


def layer(tab, queries, nkv, store, residual, weight):
    bf = jnp.bfloat16
    blocks = store.shape[0]
    depth, width = weight.shape[0], weight.shape[1] // 2
    rows = residual.shape[0]
    vmem = pl.BlockSpec(memory_space=pltpu.VMEM)
    dma = pltpu.SemaphoreType.DMA
    unit = (ROWS, NEW)
    each = [dma((SLOTS, CHUNKS))] * 2
    return pl.pallas_call(
        layer_kernel,
        out_shape=jax.ShapeDtypeStruct(residual.shape, bf),
        in_specs=[pl.BlockSpec(memory_space=pltpu.SMEM)] + [vmem] * 3 + [pl.BlockSpec(memory_space=pl.ANY)] * 2,
        out_specs=vmem,
        scratch_shapes=[
            pltpu.VMEM(store.shape, bf),
            pltpu.VMEM((2, 2, 2, NEW, HEAD), bf),
            pltpu.VMEM((SLOTS, NY, NZ, NEW, HEAD), bf),
            pltpu.VMEM((blocks, BLOCK, HEAD), bf),
            pltpu.VMEM((blocks, HEAD, BLOCK), bf),
            pltpu.VMEM((blocks, HEAD, BLOCK), bf),
            pltpu.VMEM((2, 2 * NEW, 2 * HEAD), bf),
            pltpu.VMEM((SLOTS, NY, NZ) + unit, bf),
            pltpu.VMEM((SLOTS, 2, 2) + unit, bf),
            pltpu.VMEM((SLOTS, 2, NZ) + unit, bf),
            pltpu.VMEM((SLOTS, NZ) + unit, bf),
            pltpu.VMEM((SLOTS, 4 * PART, 4 * HEAD), bf),
            pltpu.VMEM((depth, width), bf),
            pltpu.VMEM((rows, width), bf),
            pltpu.VMEM((SLOTS, 4 * PART, width), bf),
            pltpu.VMEM((SLOTS, 2 * PART, width), bf),
            pltpu.VMEM((SLOTS, 2 * PART, width), bf),
            pltpu.VMEM((SLOTS, PART, width), bf),
            pltpu.VMEM((SLOTS, PART, width), bf),
            pltpu.VMEM((2, PART, width), bf),
            pltpu.VMEM((2, PART, width), bf),
            dma((4,)), dma((4,)), dma((3,)),
            dma((SLOTS // 2, NZ, 2)), dma((SLOTS, NZ)),
            dma((SLOTS, 2, NZ)), dma((SLOTS, 2, NZ)), dma((SLOTS, 2, 2)), dma((SLOTS, 2, 2)),
            dma((SLOTS, 2, 2)), dma((SLOTS, 2, 2)), dma((SLOTS, 2, NZ)), dma((SLOTS, 2, NZ)),
            dma((SLOTS, NZ)), dma((SLOTS, NZ)), dma((SLOTS,)), dma((SLOTS,)),
            *each, *each, *each, dma((2,)), dma((2,)),
        ],
        compiler_params=pltpu.CompilerParams(
            collective_id=0, has_side_effects=True, vmem_limit_bytes=56 * 1024 * 1024
        ),
    )(tab, queries, nkv, residual, store, weight)


def hit_table(hit_dev, hit_blk, prefix_len):
    me = lax.axis_index("pool")
    start = jnp.arange(MAXB, dtype=jnp.int32) * BLOCK
    count = jnp.clip(prefix_len[:, None] - start[None, :], 0, BLOCK)
    code = hit_blk + 32 * count
    return jnp.stack([jnp.sum(jnp.where(hit_dev == d, code, 0), axis=1) for d in (me, me + 1 - 2 * (me % 2))])


def shards(queries, new_key_values, key_value_store, o_weight, residual, hit_dev, hit_blk, prefix_len):
    tab = hit_table(hit_dev, hit_blk, prefix_len)
    return layer(tab, queries, new_key_values, key_value_store, residual, o_weight)


def solution(mesh):
    placed = (
        P("pool", "tp"),
        P("pool", "tp"),
        P("pool", None, "tp"),
        P("tp", None),
        P(("pool", "tp"), None),
        P(),
        P(),
        P(),
    )
    return jax.shard_map(
        shards, mesh=mesh, in_specs=placed, out_specs=P(("pool", "tp"), None), check_vma=False
    )
```

```python
import functools
import math

import jax
import jax.numpy as jnp
from jax import lax
from jax.experimental import pallas as pl
from jax.experimental.pallas import tpu as pltpu
from jax.sharding import PartitionSpec as P

HEAD = 128
NEW = 128
BLOCK = 256
MAXB = 16
NY = 4
NZ = 4
NX = 4
PART = 16
SLOTS = 8
CHUNKS = 4
LOG2_SCALE = HEAD**-0.5 * math.log2(math.e)
FLOOR = -1e30
ROWS = 144
MESH = pl.DeviceIdType.MESH


def nt(a, b):
    return lax.dot_general(a, b, (((1,), (1,)), ((), ())), preferred_element_type=jnp.float32)


def put(ref, at, o, m, l):
    ref[at + (slice(0, HEAD), slice(None))] = o.astype(jnp.bfloat16)
    high = l.astype(jnp.bfloat16).astype(jnp.float32)
    row = lax.broadcasted_iota(jnp.int32, (16, NEW), 0)
    stats = jnp.where(row == 0, m, jnp.where(row == 1, high, jnp.where(row == 2, l - high, 0.0)))
    ref[at + (slice(HEAD, ROWS), slice(None))] = stats.astype(jnp.bfloat16)


def get(ref, at):
    o = ref[at + (slice(0, HEAD), slice(None))].astype(jnp.float32)
    stats = ref[at + (slice(HEAD, ROWS), slice(None))].astype(jnp.float32)
    return o, stats[0:1], stats[1:2] + stats[2:3]


def merge(parts):
    m = functools.reduce(jnp.maximum, [p[1] for p in parts])
    o, l = 0.0, 0.0
    for po, pm, ps in parts:
        w = jnp.exp2(pm - m)
        o, l = o + po * w, l + ps * w
    return o, m, l


def layer_kernel(
    tab, q_ref, nkv_ref, res_ref, store_ref, w_ref, out_ref,
    kv_ref, qsrc, qbuf, k_sib, vt_own, vt_sib, nkv, part, r2, r1, rz, att,
    w, res_sib, proj, x1, x2, zout, zin, done, fin,
    kv_send, kv_recv, local,
    qs_send, qz_send, qz_recv, qy_send, qy_recv, qr_send, qr_recv,
    p2_send, p2_recv, p1_send, p1_recv, pz_send, pz_recv, at_send, at_recv,
    x1_send, x1_recv, x2_send, x2_recv, zh_send, zh_recv, fin_send, fin_recv,
):
    kv_own = pltpu.make_async_copy(store_ref, kv_ref, local.at[2])
    kv_own.start()
    me, tp = lax.axis_index("pool"), lax.axis_index("tp")
    core = lax.rem(me, 2)
    mz = lax.rem(lax.div(me, 2), NZ)
    my = lax.div(me, 2 * NZ)
    zh = lax.rem(tp, 2)
    mx = lax.div(tp, 2)
    up, down = lax.rem(my + 1, NY), lax.rem(my + NY - 1, NY)
    across = lax.rem(my + 2, NY)
    sib = 1 - core
    others = (mz + 1 - 2 * lax.rem(mz, 2), lax.rem(mz + 2, NZ), NZ - 1 - mz)
    pair, facing = mx + 1 - 2 * lax.rem(mx, 2), NX - 1 - mx
    width = w.shape[1]
    chunk = width // CHUNKS

    def dev(y, z, c):
        return (y * NZ + z) * 2 + c

    def tp_of(x, h):
        return x * 2 + h

    def remote(src, dst, send, recv, **to):
        return pltpu.make_async_remote_copy(
            src_ref=src, dst_ref=dst, send_sem=send, recv_sem=recv, device_id=to, device_id_type=MESH
        )

    def wait_into(ref, sem):
        pltpu.make_async_copy(ref, ref, sem).wait()

    barrier = pltpu.get_barrier_semaphore()
    partners = [{"pool": dev(my, z, c)} for z in others for c in range(2)]
    partners += [{"pool": p} for p in (dev(my, mz, sib), dev(up, mz, core), dev(down, mz, core))]
    partners += [{"tp": p} for p in (tp_of(pair, zh), tp_of(facing, zh), tp_of(mx, 1 - zh))]
    for p in partners:
        pl.semaphore_signal(barrier, inc=1, device_id=p, device_id_type=MESH)

    for i in range(2):
        for g in range(2):
            for h in range(4):
                for b in range(4):
                    to, at = (h % 2 * 4 + b) * PART, i * NEW + (2 * b + g) * PART
                    qsrc[i, g, h // 2, to : to + PART, :] = q_ref[at : at + PART, h * HEAD : (h + 1) * HEAD]

    pl.semaphore_wait(barrier, len(partners))

    def half(c):
        return pl.ds(pl.multiple_of(c * 2 * HEAD, 2 * HEAD), 2 * HEAD)

    def columns(c):
        return pl.ds(pl.multiple_of(c * width, width), width)

    def owner(s):
        return lax.rem(s, 2)

    def which(s):
        return lax.rem(lax.div(s, 2) + lax.rem(s, 2), 2)

    def share(s):
        return lax.div(s, 4)

    def tokens(i):
        return pl.ds(pl.multiple_of(i * NEW, NEW), NEW)

    def q_z(j, k, c):
        s = 2 * j + core
        return remote(
            qsrc.at[which(s), lax.div(j, 2), c], qbuf.at[s, my, mz],
            qz_send, qz_recv.at[s, mz], pool=dev(my, others[k], c),
        )

    def q_sib(j):
        s = 2 * j + core
        return remote(
            qsrc.at[which(s), j // 2, sib], qbuf.at[s, my, mz],
            qs_send, qz_recv.at[s, mz], pool=dev(my, mz, sib),
        )

    def q_own(j):
        s = 2 * j + core
        return pltpu.make_async_copy(qsrc.at[which(s), j // 2, core], qbuf.at[s, my, mz], qz_recv.at[s, mz])

    here = dev(my, mz, sib)
    nk_copy = remote(nkv_ref, nkv.at[core], kv_send.at[0], kv_recv.at[0], pool=here)
    k_copy = remote(kv_ref.at[:, :, pl.ds(0, HEAD)], k_sib, kv_send.at[1], kv_recv.at[1], pool=here)
    v_copy = remote(vt_own, vt_sib, kv_send.at[2], kv_recv.at[2], pool=here)
    res_copy = remote(res_ref.at[:, columns(sib)], res_sib, kv_send.at[3], kv_recv.at[3], pool=here)
    nk_own = pltpu.make_async_copy(nkv_ref, nkv.at[core], local.at[0])
    w_own = pltpu.make_async_copy(w_ref.at[:, columns(core)], w, local.at[1])

    def q_y(s, d, z):
        piece = qbuf.at[s, my, z]
        return remote(piece, piece, qy_send, qy_recv.at[s, d, z], pool=dev((up, down)[d], mz, core))

    def q_relay(s, d, j):
        to, of = ((up, down), (down, up))[d]
        piece = qbuf.at[s, of, 2 * d + j]
        return remote(piece, piece, qr_send, qr_recv.at[s, d, j], pool=dev(to, mz, core))

    def z_arrived(s, z):
        wait_into(qbuf.at[s, my, z], qz_recv.at[s, z])
        q_y(s, 0, z).start()
        q_y(s, 1, z).start()

    def y_arrived(s, d, z):
        wait_into(qbuf.at[s, (down, up)[d], z], qy_recv.at[s, d, z])

    def relay_two(s, j):
        for d in range(2):
            y_arrived(s, d, 2 * d + j)
            q_relay(s, d, j).start()

    def stage_r(s):
        for j in range(2):
            relay_two(s, j)

    per_core = SLOTS // 2

    def send_z(j):
        for k in range(NZ - 1):
            for c in range(2):
                q_z(j, k, c).start()

    for j in range(per_core):
        q_own(j).start()
        q_sib(j).start()
        if j == 0:
            send_z(0)
    for s in range(4):
        z_arrived(s, mz)
    nk_own.start()
    nk_copy.start()
    kv_own.wait()
    k_copy.start()

    @pl.loop(0, kv_ref.shape[0])
    def _(b):
        vt_own[b] = kv_ref[b, :, HEAD:].T

    v_copy.start()
    for z in others:
        z_arrived(0, z)
        z_arrived(1, z)
    send_z(1)
    res_copy.start()
    w_own.start()
    stage_r(0)

    key = lax.broadcasted_iota(jnp.int32, (BLOCK, NEW), 0)

    def attend(s, y, z):
        r = dev(y, z, owner(s)) * 2 + which(s)
        q = qbuf[s, y, z]
        codes = [tab[0, r], tab[1, r]]
        blocks = [c % 32 for c in codes]
        counts = [c // 32 for c in codes]
        keys = [kv_ref[blocks[0], :, :HEAD], k_sib[blocks[1]]]
        values = [vt_own[blocks[0]], vt_sib[blocks[1]]]
        t = [jnp.where(key < n, nt(k, q) * LOG2_SCALE, -jnp.inf) for k, n in zip(keys, counts)]
        m = jnp.maximum(jnp.max(t[0], axis=0, keepdims=True), jnp.max(t[1], axis=0, keepdims=True))
        m = jnp.maximum(m, FLOOR).astype(jnp.bfloat16).astype(jnp.float32)
        e = [jnp.exp2(x - m) for x in t]
        l = jnp.sum(e[0], axis=0, keepdims=True) + jnp.sum(e[1], axis=0, keepdims=True)
        o = [
            jnp.dot(v, x.astype(jnp.bfloat16), preferred_element_type=jnp.float32)
            for v, x in zip(values, e)
        ]
        put(part, (s, y, z), o[0] + o[1], m, l)

    def p_2(s, d, j):
        return remote(
            part.at[s, across, 2 * d + j], r2.at[s, d, j],
            p2_send, p2_recv.at[s, d, j], pool=dev((up, down)[d], mz, core),
        )

    def p_1(s, d, z):
        to = (up, down)[d]
        return remote(
            part.at[s, to, z], r1.at[s, d, z], p1_send, p1_recv.at[s, d, z], pool=dev(to, mz, core)
        )

    def p_z(s, z):
        return remote(
            part.at[s, my, z], rz.at[s, mz], pz_send, pz_recv.at[s, mz], pool=dev(my, z, core)
        )

    def stage_c(s):
        for j in range(2):
            for d in range(2):
                wait_into(qbuf.at[s, across, 2 * d + j], qr_recv.at[s, d, j])
                y_arrived(s, d, 2 - 2 * d + j)

        for z in range(NZ):
            attend(s, across, z)
        for j in range(2):
            p_2(s, 0, j).start()
            p_2(s, 1, j).start()

        @pl.when(s == 0)
        def _():
            for z in others:
                z_arrived(2, z)

        for j in range(2):
            attend(s, up, 2 + j)
            attend(s, down, j)
        for j in range(2):
            p_1(s, 0, 2 + j).start()
            p_1(s, 1, j).start()

        @pl.when(s + 1 < SLOTS)
        def _():
            stage_r(s + 1)

        for j in range(2):
            attend(s, up, j)
            attend(s, down, 2 + j)
        for z in range(NZ):
            attend(s, my, z)

    def stage_m(s):
        @pl.loop(0, 2)
        def _(j):
            for d in range(2):
                z, to = 2 * d + j, (up, down)[d]
                wait_into(r2.at[s, d, j], p2_recv.at[s, d, j])
                put(part, (s, to, z), *merge([get(part, (s, to, z)), get(r2, (s, d, j))]))
                p_1(s, d, z).start()

        @pl.when(s + 4 < SLOTS)
        def _():
            z_arrived(s + 4, mz)

        @pl.when(s + 3 < SLOTS)
        def _():
            for z in others:
                z_arrived(s + 3, z)

        @pl.when(jnp.logical_or(s == 0, s == 2))
        def _():
            send_z(lax.div(s, 2) + 2)

    def stage_h(s):
        @pl.loop(0, NZ)
        def _(k):
            z = lax.rem(mz + 1 + k, NZ)
            for d in range(2):
                wait_into(r1.at[s, d, z], p1_recv.at[s, d, z])
            put(part, (s, my, z), *merge([get(part, (s, my, z)), get(r1, (s, 0, z)), get(r1, (s, 1, z))]))

            @pl.when(k < NZ - 1)
            def _():
                p_z(s, z).start()

    def fresh(s):
        q = qbuf[s, my, mz]
        rows = nkv[owner(s), tokens(which(s)), :]
        j = lax.broadcasted_iota(jnp.int32, (NEW, NEW), 0)
        i = lax.broadcasted_iota(jnp.int32, (NEW, NEW), 1) % (4 * PART)
        i = i + i // PART * PART + share(s) * PART
        t = jnp.where(j <= i, nt(rows[:, :HEAD], q) * LOG2_SCALE, -jnp.inf)
        m = jnp.max(t, axis=0, keepdims=True).astype(jnp.bfloat16).astype(jnp.float32)
        e = jnp.exp2(t - m)
        o = jnp.dot(rows[:, HEAD:].T, e.astype(jnp.bfloat16), preferred_element_type=jnp.float32)
        return o, m, jnp.sum(e, axis=0, keepdims=True)

    def a_copy(s):
        mine = att.at[s, :, half(core)]
        return remote(mine, mine, at_send, at_recv.at[s], pool=here)

    def stage_f(s):
        parts = [fresh(s), get(part, (s, my, mz))]
        for z in others:
            wait_into(rz.at[s, z], pz_recv.at[s, z])
            parts.append(get(rz, (s, z)))
        o, _, l = merge(parts)
        o = o / l
        o = o.T
        att[s, :, half(core)] = jnp.concatenate([o[: 4 * PART], o[4 * PART :]], axis=1).astype(jnp.bfloat16)
        a_copy(s).start()

    def is_dest(s):
        return lax.div(mx, 2) == which(s)

    def sent_half(s):
        return jnp.where(is_dest(s), 1 - lax.rem(mx, 2), lax.rem(mx, 2))

    def rows(h):
        return pl.ds(pl.multiple_of(h * 2 * PART, 2 * PART), 2 * PART)

    def part_of(h, z):
        return pl.ds(pl.multiple_of((2 * h + z) * PART, PART), PART)

    def cols(n):
        return pl.ds(pl.multiple_of(n * chunk, chunk), chunk)

    def x_1(s, n):
        return remote(
            proj.at[s, rows(sent_half(s)), cols(n)], x1.at[s, :, cols(n)],
            x1_send, x1_recv.at[s, n], tp=tp_of(pair, zh),
        )

    def x_2(s, n):
        return remote(
            proj.at[s, rows(1 - sent_half(s)), cols(n)], x2.at[s, :, cols(n)],
            x2_send, x2_recv.at[s, n], tp=tp_of(facing, zh),
        )

    def z_h(s, n):
        return remote(
            zout.at[s, :, cols(n)], zin.at[s, :, cols(n)], zh_send, zh_recv.at[s, n], tp=tp_of(mx, 1 - zh)
        )

    def stage_o(s):
        @pl.when(s == 0)
        def _():
            w_own.wait()

        theirs = att.at[s, :, half(sib)]
        wait_into(theirs, at_recv.at[s])

        @pl.loop(0, CHUNKS)
        def _(n):
            proj[s, :, cols(n)] = jnp.dot(
                att[s], w[:, cols(n)], preferred_element_type=jnp.float32
            ).astype(jnp.bfloat16)
            x_1(s, n).start()

    def f32(x):
        return x.astype(jnp.float32)

    def stage_x(s):
        @pl.when(jnp.logical_not(is_dest(s)))
        def _():
            keep = 1 - sent_half(s)

            @pl.loop(0, CHUNKS)
            def _(n):
                wait_into(x1.at[s, :, cols(n)], x1_recv.at[s, n])
                total = f32(proj[s, rows(keep), cols(n)]) + f32(x1[s, :, cols(n)])
                proj[s, rows(keep), cols(n)] = total.astype(jnp.bfloat16)
                x_2(s, n).start()

    def stage_d(s):
        @pl.when(is_dest(s))
        def _():
            keep = 1 - sent_half(s)

            @pl.loop(0, CHUNKS)
            def _(n):
                wait_into(x1.at[s, :, cols(n)], x1_recv.at[s, n])
                wait_into(x2.at[s, :, cols(n)], x2_recv.at[s, n])
                z = 1 - zh
                total = f32(proj[s, part_of(keep, z), cols(n)])
                total += f32(x1[s, part_of(0, z), cols(n)]) + f32(x2[s, part_of(0, z), cols(n)])
                zout[s, :, cols(n)] = total.astype(jnp.bfloat16)
                z_h(s, n).start()

    def fin_copy(g):
        return remote(done.at[g], fin.at[g], fin_send, fin_recv.at[g], pool=here)

    def stage_e(s):
        @pl.when(is_dest(s))
        def _():
            keep = 1 - sent_half(s)
            mine = owner(s) == core
            g = share(s)
            out_rows = pl.ds(pl.multiple_of(g * PART, PART), PART)

            def total(n):
                wait_into(zin.at[s, :, cols(n)], zh_recv.at[s, n])
                t = f32(proj[s, part_of(keep, zh), cols(n)]) + f32(zin[s, :, cols(n)])
                return t + f32(x1[s, part_of(0, zh), cols(n)]) + f32(x2[s, part_of(0, zh), cols(n)])

            def at(n):
                return pl.ds(pl.multiple_of(core * width + n * chunk, chunk), chunk)

            @pl.when(mine)
            def _():
                @pl.loop(0, CHUNKS)
                def _(n):
                    out_ref[out_rows, at(n)] = (total(n) + f32(res_ref[out_rows, at(n)])).astype(jnp.bfloat16)

            @pl.when(jnp.logical_not(mine))
            def _():
                @pl.loop(0, CHUNKS)
                def _(n):
                    done[g, :, cols(n)] = (total(n) + f32(res_sib[out_rows, cols(n)])).astype(jnp.bfloat16)

                fin_copy(g).start()

    nk_own.wait()
    for copy in (k_copy, nk_copy, v_copy, res_copy):
        copy.wait_send()
    wait_into(nkv.at[sib], kv_recv.at[0])
    wait_into(k_sib, kv_recv.at[1])
    wait_into(vt_sib, kv_recv.at[2])
    wait_into(res_sib, kv_recv.at[3])

    @pl.loop(0, SLOTS + 2)
    def _(t):
        def stage(f, s):
            @pl.when(jnp.logical_and(s >= 0, s < SLOTS))
            def _():
                f(s)

        stage(stage_c, t)
        stage(stage_h, t - 1)
        stage(stage_m, t)
        stage(stage_f, t - 2)
        stage(stage_d, t - 5)
        stage(stage_o, t - 2)
        stage(stage_x, t - 3)
        stage(stage_e, t - 7)

    stage_x(SLOTS - 1)
    for s in range(SLOTS - 3, SLOTS):
        stage_d(s)

    @pl.loop(SLOTS - 5, SLOTS)
    def _(s):
        stage_e(s)

    for ref, sem in (
        (qbuf.at[pl.ds(0, 6), 0], qz_send),
        (qbuf.at[0, 0], qs_send),
        (qbuf.at[pl.ds(0, 4)], qy_send),
        (qbuf.at[pl.ds(0, 2)], qr_send),
        (part.at[pl.ds(0, 2)], p2_send),
        (part.at[pl.ds(0, 4)], p1_send),
        (part.at[pl.ds(0, 6), 0], pz_send),
        (att.at[:, :, pl.ds(0, 2 * HEAD)], at_send),
        (x1, x1_send),
        (x2.at[pl.ds(0, SLOTS // 2)], x2_send),
        (zout.at[pl.ds(0, SLOTS // 2)], zh_send),
        (fin, fin_send),
    ):
        wait_into(ref, sem)
    for g in range(2):
        wait_into(fin.at[g], fin_recv.at[g])
        out_ref[g * PART : (g + 1) * PART, columns(sib)] = fin[g]


def layer(tab, queries, nkv, store, residual, weight):
    bf = jnp.bfloat16
    blocks = store.shape[0]
    depth, width = weight.shape[0], weight.shape[1] // 2
    rows = residual.shape[0]
    vmem = pl.BlockSpec(memory_space=pltpu.VMEM)
    dma = pltpu.SemaphoreType.DMA
    unit = (ROWS, NEW)
    one, each = dma(()), dma((SLOTS, CHUNKS))
    return pl.pallas_call(
        layer_kernel,
        out_shape=jax.ShapeDtypeStruct(residual.shape, bf),
        in_specs=[pl.BlockSpec(memory_space=pltpu.SMEM)] + [vmem] * 3 + [pl.BlockSpec(memory_space=pl.ANY)] * 2,
        out_specs=vmem,
        scratch_shapes=[
            pltpu.VMEM(store.shape, bf),
            pltpu.VMEM((2, 2, 2, NEW, HEAD), bf),
            pltpu.VMEM((SLOTS, NY, NZ, NEW, HEAD), bf),
            pltpu.VMEM((blocks, BLOCK, HEAD), bf),
            pltpu.VMEM((blocks, HEAD, BLOCK), bf),
            pltpu.VMEM((blocks, HEAD, BLOCK), bf),
            pltpu.VMEM((2, 2 * NEW, 2 * HEAD), bf),
            pltpu.VMEM((SLOTS, NY, NZ) + unit, bf),
            pltpu.VMEM((SLOTS, 2, 2) + unit, bf),
            pltpu.VMEM((SLOTS, 2, NZ) + unit, bf),
            pltpu.VMEM((SLOTS, NZ) + unit, bf),
            pltpu.VMEM((SLOTS, 4 * PART, 4 * HEAD), bf),
            pltpu.VMEM((depth, width), bf),
            pltpu.VMEM((rows, width), bf),
            pltpu.VMEM((SLOTS, 4 * PART, width), bf),
            pltpu.VMEM((SLOTS, 2 * PART, width), bf),
            pltpu.VMEM((SLOTS, 2 * PART, width), bf),
            pltpu.VMEM((SLOTS, PART, width), bf),
            pltpu.VMEM((SLOTS, PART, width), bf),
            pltpu.VMEM((2, PART, width), bf),
            pltpu.VMEM((2, PART, width), bf),
            dma((4,)), dma((4,)), dma((3,)),
            one, one, dma((SLOTS, NZ)),
            one, dma((SLOTS, 2, NZ)), one, dma((SLOTS, 2, 2)),
            one, dma((SLOTS, 2, 2)), one, dma((SLOTS, 2, NZ)),
            one, dma((SLOTS, NZ)), one, dma((SLOTS,)),
            one, each, one, each, one, each, one, dma((2,)),
        ],
        compiler_params=pltpu.CompilerParams(
            collective_id=0, has_side_effects=True, vmem_limit_bytes=56 * 1024 * 1024
        ),
    )(tab, queries, nkv, residual, store, weight)


def hit_table(hit_dev, hit_blk, prefix_len):
    me = lax.axis_index("pool")
    there = jnp.stack([me, me + 1 - 2 * (me % 2)])[:, None, None]
    start = jnp.arange(MAXB, dtype=jnp.int32) * BLOCK
    count = jnp.clip(prefix_len[:, None] - start[None, :], 0, BLOCK)
    return jnp.sum(jnp.where(hit_dev[None] == there, (hit_blk + 32 * count)[None], 0), axis=2)


def shards(queries, new_key_values, key_value_store, o_weight, residual, hit_dev, hit_blk, prefix_len):
    tab = hit_table(hit_dev, hit_blk, prefix_len)
    return layer(tab, queries, new_key_values, key_value_store, residual, o_weight)


def solution(mesh):
    placed = (
        P("pool", "tp"),
        P("pool", "tp"),
        P("pool", None, "tp"),
        P("tp", None),
        P(("pool", "tp"), None),
        P(),
        P(),
        P(),
    )
    return jax.shard_map(
        shards, mesh=mesh, in_specs=placed, out_specs=P(("pool", "tp"), None), check_vma=False
    )
```

```python
import functools
import math

import jax
import jax.numpy as jnp
from jax import lax
from jax.experimental import pallas as pl
from jax.experimental.pallas import tpu as pltpu
from jax.sharding import PartitionSpec as P

HEAD = 128
NEW = 128
BLOCK = 256
MAXB = 16
NY = 4
NZ = 4
NX = 4
PART = 16
SLOTS = 8
CHUNKS = 4
LOG2_SCALE = HEAD**-0.5 * math.log2(math.e)
FLOOR = -1e30
ROWS = 144
MESH = pl.DeviceIdType.MESH


def nt(a, b):
    return lax.dot_general(a, b, (((1,), (1,)), ((), ())), preferred_element_type=jnp.float32)


def put(ref, at, o, m, l):
    ref[at + (slice(0, HEAD), slice(None))] = o.astype(jnp.bfloat16)
    high = l.astype(jnp.bfloat16).astype(jnp.float32)
    row = lax.broadcasted_iota(jnp.int32, (16, NEW), 0)
    stats = jnp.where(row == 0, m, jnp.where(row == 1, high, jnp.where(row == 2, l - high, 0.0)))
    ref[at + (slice(HEAD, ROWS), slice(None))] = stats.astype(jnp.bfloat16)


def get(ref, at):
    o = ref[at + (slice(0, HEAD), slice(None))].astype(jnp.float32)
    stats = ref[at + (slice(HEAD, ROWS), slice(None))].astype(jnp.float32)
    return o, stats[0:1], stats[1:2] + stats[2:3]


def merge(parts):
    m = functools.reduce(jnp.maximum, [p[1] for p in parts])
    o, l = 0.0, 0.0
    for po, pm, ps in parts:
        w = jnp.exp2(pm - m)
        o, l = o + po * w, l + ps * w
    return o, m, l


def layer_kernel(
    tab, q_ref, nkv_ref, res_ref, store_ref, w_ref, out_ref,
    kv_ref, qsrc, qbuf, k_sib, vt_own, vt_sib, nkv, part, r2, r1, rz, att,
    w, res_sib, proj, x1, x2, zout, zin, done, fin,
    kv_send, kv_recv, local,
    qs_send, qz_send, qz_recv, qy_send, qy_recv, qr_send, qr_recv,
    p2_send, p2_recv, p1_send, p1_recv, pz_send, pz_recv, at_send, at_recv,
    x1_send, x1_recv, x2_send, x2_recv, zh_send, zh_recv, fin_send, fin_recv,
):
    kv_own = pltpu.make_async_copy(store_ref, kv_ref, local.at[2])
    kv_own.start()
    me, tp = lax.axis_index("pool"), lax.axis_index("tp")
    core = lax.rem(me, 2)
    mz = lax.rem(lax.div(me, 2), NZ)
    my = lax.div(me, 2 * NZ)
    zh = lax.rem(tp, 2)
    mx = lax.div(tp, 2)
    up, down = lax.rem(my + 1, NY), lax.rem(my + NY - 1, NY)
    across = lax.rem(my + 2, NY)
    sib = 1 - core
    others = (mz + 1 - 2 * lax.rem(mz, 2), lax.rem(mz + 2, NZ), NZ - 1 - mz)
    pair, facing = mx + 1 - 2 * lax.rem(mx, 2), NX - 1 - mx
    width = w.shape[1]
    chunk = width // CHUNKS

    def dev(y, z, c):
        return (y * NZ + z) * 2 + c

    def tp_of(x, h):
        return x * 2 + h

    def remote(src, dst, send, recv, **to):
        return pltpu.make_async_remote_copy(
            src_ref=src, dst_ref=dst, send_sem=send, recv_sem=recv, device_id=to, device_id_type=MESH
        )

    def wait_into(ref, sem):
        pltpu.make_async_copy(ref, ref, sem).wait()

    barrier = pltpu.get_barrier_semaphore()
    partners = [{"pool": dev(my, z, c)} for z in others for c in range(2)]
    partners += [{"pool": p} for p in (dev(my, mz, sib), dev(up, mz, core), dev(down, mz, core))]
    partners += [{"tp": p} for p in (tp_of(pair, zh), tp_of(facing, zh), tp_of(mx, 1 - zh))]
    for p in partners:
        pl.semaphore_signal(barrier, inc=1, device_id=p, device_id_type=MESH)

    for i in range(2):
        for g in range(2):
            for h in range(4):
                for b in range(4):
                    to, at = (h % 2 * 4 + b) * PART, i * NEW + (2 * b + g) * PART
                    qsrc[i, g, h // 2, to : to + PART, :] = q_ref[at : at + PART, h * HEAD : (h + 1) * HEAD]

    pl.semaphore_wait(barrier, len(partners))

    def half(c):
        return pl.ds(pl.multiple_of(c * 2 * HEAD, 2 * HEAD), 2 * HEAD)

    def columns(c):
        return pl.ds(pl.multiple_of(c * width, width), width)

    def owner(s):
        return lax.rem(s, 2)

    def which(s):
        return lax.rem(lax.div(s, 2) + lax.rem(s, 2), 2)

    def share(s):
        return lax.div(s, 4)

    def tokens(i):
        return pl.ds(pl.multiple_of(i * NEW, NEW), NEW)

    def q_z(j, k, c):
        s = 2 * j + core
        return remote(
            qsrc.at[which(s), lax.div(j, 2), c], qbuf.at[s, my, mz],
            qz_send, qz_recv.at[s, mz], pool=dev(my, others[k], c),
        )

    def q_sib(j):
        s = 2 * j + core
        return remote(
            qsrc.at[which(s), j // 2, sib], qbuf.at[s, my, mz],
            qs_send, qz_recv.at[s, mz], pool=dev(my, mz, sib),
        )

    def q_own(j):
        s = 2 * j + core
        return pltpu.make_async_copy(qsrc.at[which(s), j // 2, core], qbuf.at[s, my, mz], qz_recv.at[s, mz])

    here = dev(my, mz, sib)
    nk_copy = remote(nkv_ref, nkv.at[core], kv_send.at[0], kv_recv.at[0], pool=here)
    k_copy = remote(kv_ref.at[:, :, pl.ds(0, HEAD)], k_sib, kv_send.at[1], kv_recv.at[1], pool=here)
    v_copy = remote(vt_own, vt_sib, kv_send.at[2], kv_recv.at[2], pool=here)
    res_copy = remote(res_ref.at[:, columns(sib)], res_sib, kv_send.at[3], kv_recv.at[3], pool=here)
    nk_own = pltpu.make_async_copy(nkv_ref, nkv.at[core], local.at[0])
    w_own = pltpu.make_async_copy(w_ref.at[:, columns(core)], w, local.at[1])

    def q_y(s, d, z):
        piece = qbuf.at[s, my, z]
        return remote(piece, piece, qy_send, qy_recv.at[s, d, z], pool=dev((up, down)[d], mz, core))

    def q_relay(s, d, j):
        to, of = ((up, down), (down, up))[d]
        piece = qbuf.at[s, of, 2 * d + j]
        return remote(piece, piece, qr_send, qr_recv.at[s, d, j], pool=dev(to, mz, core))

    def z_arrived(s, z):
        wait_into(qbuf.at[s, my, z], qz_recv.at[s, z])
        q_y(s, 0, z).start()
        q_y(s, 1, z).start()

    def y_arrived(s, d, z):
        wait_into(qbuf.at[s, (down, up)[d], z], qy_recv.at[s, d, z])

    def relay_two(s, j):
        for d in range(2):
            y_arrived(s, d, 2 * d + j)
            q_relay(s, d, j).start()

    def stage_r(s):
        for j in range(2):
            relay_two(s, j)

    per_core = SLOTS // 2

    def send_z(j):
        for k in range(NZ - 1):
            for c in range(2):
                q_z(j, k, c).start()

    for j in range(per_core):
        q_own(j).start()
        q_sib(j).start()
        if j == 0:
            send_z(0)
    for s in range(4):
        z_arrived(s, mz)
    nk_own.start()
    nk_copy.start()
    kv_own.wait()
    k_copy.start()

    @pl.loop(0, kv_ref.shape[0])
    def _(b):
        vt_own[b] = kv_ref[b, :, HEAD:].T

    v_copy.start()
    for z in others:
        z_arrived(0, z)
        z_arrived(1, z)
    send_z(1)
    res_copy.start()
    w_own.start()
    stage_r(0)
    stage_r(1)

    key = lax.broadcasted_iota(jnp.int32, (BLOCK, NEW), 0)

    def attend(s, y, z):
        r = dev(y, z, owner(s)) * 2 + which(s)
        q = qbuf[s, y, z]
        codes = [tab[0, r], tab[1, r]]
        blocks = [c % 32 for c in codes]
        counts = [c // 32 for c in codes]
        keys = [kv_ref[blocks[0], :, :HEAD], k_sib[blocks[1]]]
        values = [vt_own[blocks[0]], vt_sib[blocks[1]]]
        t = [jnp.where(key < n, nt(k, q) * LOG2_SCALE, -jnp.inf) for k, n in zip(keys, counts)]
        m = jnp.maximum(jnp.max(t[0], axis=0, keepdims=True), jnp.max(t[1], axis=0, keepdims=True))
        m = jnp.maximum(m, FLOOR).astype(jnp.bfloat16).astype(jnp.float32)
        e = [jnp.exp2(x - m) for x in t]
        l = jnp.sum(e[0], axis=0, keepdims=True) + jnp.sum(e[1], axis=0, keepdims=True)
        o = [
            jnp.dot(v, x.astype(jnp.bfloat16), preferred_element_type=jnp.float32)
            for v, x in zip(values, e)
        ]
        put(part, (s, y, z), o[0] + o[1], m, l)

    def p_2(s, d, j):
        return remote(
            part.at[s, across, 2 * d + j], r2.at[s, d, j],
            p2_send, p2_recv.at[s, d, j], pool=dev((up, down)[d], mz, core),
        )

    def p_1(s, d, z):
        to = (up, down)[d]
        return remote(
            part.at[s, to, z], r1.at[s, d, z], p1_send, p1_recv.at[s, d, z], pool=dev(to, mz, core)
        )

    def p_z(s, z):
        return remote(
            part.at[s, my, z], rz.at[s, mz], pz_send, pz_recv.at[s, mz], pool=dev(my, z, core)
        )

    def stage_c(s):
        for j in range(2):
            for d in range(2):
                wait_into(qbuf.at[s, across, 2 * d + j], qr_recv.at[s, d, j])
                y_arrived(s, d, 2 - 2 * d + j)

        for z in range(NZ):
            attend(s, across, z)
        for j in range(2):
            p_2(s, 0, j).start()
            p_2(s, 1, j).start()

        @pl.when(jnp.logical_and(s >= 1, s + 1 < SLOTS))
        def _():
            stage_r(s + 1)

        @pl.when(s == 0)
        def _():
            for z in others:
                z_arrived(2, z)

        for j in range(2):
            attend(s, up, 2 + j)
            attend(s, down, j)
        for j in range(2):
            p_1(s, 0, 2 + j).start()
            p_1(s, 1, j).start()

        for j in range(2):
            attend(s, up, j)
            attend(s, down, 2 + j)
        for z in range(NZ):
            attend(s, my, z)

    def stage_m(s):
        @pl.loop(0, 2)
        def _(j):
            for d in range(2):
                z, to = 2 * d + j, (up, down)[d]
                wait_into(r2.at[s, d, j], p2_recv.at[s, d, j])
                put(part, (s, to, z), *merge([get(part, (s, to, z)), get(r2, (s, d, j))]))
                p_1(s, d, z).start()

        @pl.when(s + 4 < SLOTS)
        def _():
            z_arrived(s + 4, mz)

        @pl.when(s + 3 < SLOTS)
        def _():
            for z in others:
                z_arrived(s + 3, z)

        @pl.when(jnp.logical_or(s == 0, s == 2))
        def _():
            send_z(lax.div(s, 2) + 2)

    def stage_h(s):
        @pl.loop(0, NZ)
        def _(k):
            z = lax.rem(mz + 1 + k, NZ)
            for d in range(2):
                wait_into(r1.at[s, d, z], p1_recv.at[s, d, z])
            put(part, (s, my, z), *merge([get(part, (s, my, z)), get(r1, (s, 0, z)), get(r1, (s, 1, z))]))

            @pl.when(k < NZ - 1)
            def _():
                p_z(s, z).start()

    def fresh(s):
        q = qbuf[s, my, mz]
        rows = nkv[owner(s), tokens(which(s)), :]
        j = lax.broadcasted_iota(jnp.int32, (NEW, NEW), 0)
        i = lax.broadcasted_iota(jnp.int32, (NEW, NEW), 1) % (4 * PART)
        i = i + i // PART * PART + share(s) * PART
        t = jnp.where(j <= i, nt(rows[:, :HEAD], q) * LOG2_SCALE, -jnp.inf)
        m = jnp.max(t, axis=0, keepdims=True).astype(jnp.bfloat16).astype(jnp.float32)
        e = jnp.exp2(t - m)
        o = jnp.dot(rows[:, HEAD:].T, e.astype(jnp.bfloat16), preferred_element_type=jnp.float32)
        return o, m, jnp.sum(e, axis=0, keepdims=True)

    def a_copy(s):
        mine = att.at[s, :, half(core)]
        return remote(mine, mine, at_send, at_recv.at[s], pool=here)

    def stage_f(s):
        parts = [fresh(s), get(part, (s, my, mz))]
        for z in others:
            wait_into(rz.at[s, z], pz_recv.at[s, z])
            parts.append(get(rz, (s, z)))
        o, _, l = merge(parts)
        o = o / l
        o = o.T
        att[s, :, half(core)] = jnp.concatenate([o[: 4 * PART], o[4 * PART :]], axis=1).astype(jnp.bfloat16)
        a_copy(s).start()

    def is_dest(s):
        return lax.div(mx, 2) == which(s)

    def sent_half(s):
        return jnp.where(is_dest(s), 1 - lax.rem(mx, 2), lax.rem(mx, 2))

    def rows(h):
        return pl.ds(pl.multiple_of(h * 2 * PART, 2 * PART), 2 * PART)

    def part_of(h, z):
        return pl.ds(pl.multiple_of((2 * h + z) * PART, PART), PART)

    def cols(n):
        return pl.ds(pl.multiple_of(n * chunk, chunk), chunk)

    def x_1(s, n):
        return remote(
            proj.at[s, rows(sent_half(s)), cols(n)], x1.at[s, :, cols(n)],
            x1_send, x1_recv.at[s, n], tp=tp_of(pair, zh),
        )

    def x_2(s, n):
        return remote(
            proj.at[s, rows(1 - sent_half(s)), cols(n)], x2.at[s, :, cols(n)],
            x2_send, x2_recv.at[s, n], tp=tp_of(facing, zh),
        )

    def z_h(s, n):
        return remote(
            zout.at[s, :, cols(n)], zin.at[s, :, cols(n)], zh_send, zh_recv.at[s, n], tp=tp_of(mx, 1 - zh)
        )

    def stage_o(s):
        @pl.when(s == 0)
        def _():
            w_own.wait()

        theirs = att.at[s, :, half(sib)]
        wait_into(theirs, at_recv.at[s])

        @pl.loop(0, CHUNKS)
        def _(n):
            proj[s, :, cols(n)] = jnp.dot(
                att[s], w[:, cols(n)], preferred_element_type=jnp.float32
            ).astype(jnp.bfloat16)
            x_1(s, n).start()

    def f32(x):
        return x.astype(jnp.float32)

    def stage_x(s):
        @pl.when(jnp.logical_not(is_dest(s)))
        def _():
            keep = 1 - sent_half(s)

            @pl.loop(0, CHUNKS)
            def _(n):
                wait_into(x1.at[s, :, cols(n)], x1_recv.at[s, n])
                total = f32(proj[s, rows(keep), cols(n)]) + f32(x1[s, :, cols(n)])
                proj[s, rows(keep), cols(n)] = total.astype(jnp.bfloat16)
                x_2(s, n).start()

    def stage_d(s):
        @pl.when(is_dest(s))
        def _():
            keep = 1 - sent_half(s)

            @pl.loop(0, CHUNKS)
            def _(n):
                wait_into(x1.at[s, :, cols(n)], x1_recv.at[s, n])
                wait_into(x2.at[s, :, cols(n)], x2_recv.at[s, n])
                z = 1 - zh
                total = f32(proj[s, part_of(keep, z), cols(n)])
                total += f32(x1[s, part_of(0, z), cols(n)]) + f32(x2[s, part_of(0, z), cols(n)])
                zout[s, :, cols(n)] = total.astype(jnp.bfloat16)
                z_h(s, n).start()

    def fin_copy(g):
        return remote(done.at[g], fin.at[g], fin_send, fin_recv.at[g], pool=here)

    def stage_e(s):
        @pl.when(is_dest(s))
        def _():
            keep = 1 - sent_half(s)
            mine = owner(s) == core
            g = share(s)
            out_rows = pl.ds(pl.multiple_of(g * PART, PART), PART)

            def total(n):
                wait_into(zin.at[s, :, cols(n)], zh_recv.at[s, n])
                t = f32(proj[s, part_of(keep, zh), cols(n)]) + f32(zin[s, :, cols(n)])
                return t + f32(x1[s, part_of(0, zh), cols(n)]) + f32(x2[s, part_of(0, zh), cols(n)])

            def at(n):
                return pl.ds(pl.multiple_of(core * width + n * chunk, chunk), chunk)

            @pl.when(mine)
            def _():
                @pl.loop(0, CHUNKS)
                def _(n):
                    out_ref[out_rows, at(n)] = (total(n) + f32(res_ref[out_rows, at(n)])).astype(jnp.bfloat16)

            @pl.when(jnp.logical_not(mine))
            def _():
                @pl.loop(0, CHUNKS)
                def _(n):
                    done[g, :, cols(n)] = (total(n) + f32(res_sib[out_rows, cols(n)])).astype(jnp.bfloat16)

                fin_copy(g).start()

    nk_own.wait()
    for copy in (k_copy, nk_copy, v_copy, res_copy):
        copy.wait_send()
    wait_into(nkv.at[sib], kv_recv.at[0])
    wait_into(k_sib, kv_recv.at[1])
    wait_into(vt_sib, kv_recv.at[2])
    wait_into(res_sib, kv_recv.at[3])

    @pl.loop(0, SLOTS + 2)
    def _(t):
        def stage(f, s):
            @pl.when(jnp.logical_and(s >= 0, s < SLOTS))
            def _():
                f(s)

        stage(stage_c, t)
        stage(stage_h, t - 1)
        stage(stage_f, jnp.where(t < SLOTS - 1, t - 2, -1))
        stage(stage_m, t)
        stage(stage_f, jnp.where(t < SLOTS - 1, -1, t - 2))
        stage(stage_o, t - 2)
        stage(stage_d, jnp.where(t < SLOTS, t - 4, jnp.where(t > SLOTS, SLOTS - 4, -1)))
        stage(stage_x, t - 3)
        stage(stage_e, t - 7)

    stage_x(SLOTS - 1)
    for s in range(SLOTS - 3, SLOTS):
        stage_d(s)

    @pl.loop(SLOTS - 5, SLOTS)
    def _(s):
        stage_e(s)

    for ref, sem in (
        (qbuf.at[pl.ds(0, 6), 0], qz_send),
        (qbuf.at[0, 0], qs_send),
        (qbuf.at[pl.ds(0, 4)], qy_send),
        (qbuf.at[pl.ds(0, 2)], qr_send),
        (part.at[pl.ds(0, 2)], p2_send),
        (part.at[pl.ds(0, 4)], p1_send),
        (part.at[pl.ds(0, 6), 0], pz_send),
        (att.at[:, :, pl.ds(0, 2 * HEAD)], at_send),
        (x1, x1_send),
        (x2.at[pl.ds(0, SLOTS // 2)], x2_send),
        (zout.at[pl.ds(0, SLOTS // 2)], zh_send),
        (fin, fin_send),
    ):
        wait_into(ref, sem)
    for g in range(2):
        wait_into(fin.at[g], fin_recv.at[g])
        out_ref[g * PART : (g + 1) * PART, columns(sib)] = fin[g]


def layer(tab, queries, nkv, store, residual, weight):
    bf = jnp.bfloat16
    blocks = store.shape[0]
    depth, width = weight.shape[0], weight.shape[1] // 2
    rows = residual.shape[0]
    vmem = pl.BlockSpec(memory_space=pltpu.VMEM)
    dma = pltpu.SemaphoreType.DMA
    unit = (ROWS, NEW)
    one, each = dma(()), dma((SLOTS, CHUNKS))
    return pl.pallas_call(
        layer_kernel,
        out_shape=jax.ShapeDtypeStruct(residual.shape, bf),
        in_specs=[pl.BlockSpec(memory_space=pltpu.SMEM)] + [vmem] * 3 + [pl.BlockSpec(memory_space=pl.ANY)] * 2,
        out_specs=vmem,
        scratch_shapes=[
            pltpu.VMEM(store.shape, bf),
            pltpu.VMEM((2, 2, 2, NEW, HEAD), bf),
            pltpu.VMEM((SLOTS, NY, NZ, NEW, HEAD), bf),
            pltpu.VMEM((blocks, BLOCK, HEAD), bf),
            pltpu.VMEM((blocks, HEAD, BLOCK), bf),
            pltpu.VMEM((blocks, HEAD, BLOCK), bf),
            pltpu.VMEM((2, 2 * NEW, 2 * HEAD), bf),
            pltpu.VMEM((SLOTS, NY, NZ) + unit, bf),
            pltpu.VMEM((SLOTS, 2, 2) + unit, bf),
            pltpu.VMEM((SLOTS, 2, NZ) + unit, bf),
            pltpu.VMEM((SLOTS, NZ) + unit, bf),
            pltpu.VMEM((SLOTS, 4 * PART, 4 * HEAD), bf),
            pltpu.VMEM((depth, width), bf),
            pltpu.VMEM((rows, width), bf),
            pltpu.VMEM((SLOTS, 4 * PART, width), bf),
            pltpu.VMEM((SLOTS, 2 * PART, width), bf),
            pltpu.VMEM((SLOTS, 2 * PART, width), bf),
            pltpu.VMEM((SLOTS, PART, width), bf),
            pltpu.VMEM((SLOTS, PART, width), bf),
            pltpu.VMEM((2, PART, width), bf),
            pltpu.VMEM((2, PART, width), bf),
            dma((4,)), dma((4,)), dma((3,)),
            one, one, dma((SLOTS, NZ)),
            one, dma((SLOTS, 2, NZ)), one, dma((SLOTS, 2, 2)),
            one, dma((SLOTS, 2, 2)), one, dma((SLOTS, 2, NZ)),
            one, dma((SLOTS, NZ)), one, dma((SLOTS,)),
            one, each, one, each, one, each, one, dma((2,)),
        ],
        compiler_params=pltpu.CompilerParams(
            collective_id=0, has_side_effects=True, vmem_limit_bytes=56 * 1024 * 1024
        ),
    )(tab, queries, nkv, residual, store, weight)


def hit_table(hit_dev, hit_blk, prefix_len):
    me = lax.axis_index("pool")
    there = jnp.stack([me, me + 1 - 2 * (me % 2)])[:, None, None]
    start = jnp.arange(MAXB, dtype=jnp.int32) * BLOCK
    count = jnp.clip(prefix_len[:, None] - start[None, :], 0, BLOCK)
    return jnp.sum(jnp.where(hit_dev[None] == there, (hit_blk + 32 * count)[None], 0), axis=2)


def shards(queries, new_key_values, key_value_store, o_weight, residual, hit_dev, hit_blk, prefix_len):
    tab = hit_table(hit_dev, hit_blk, prefix_len)
    return layer(tab, queries, new_key_values, key_value_store, residual, o_weight)


def solution(mesh):
    placed = (
        P("pool", "tp"),
        P("pool", "tp"),
        P("pool", None, "tp"),
        P("tp", None),
        P(("pool", "tp"), None),
        P(),
        P(),
        P(),
    )
    return jax.shard_map(
        shards, mesh=mesh, in_specs=placed, out_specs=P(("pool", "tp"), None), check_vma=False
    )
```

```python
import functools
import math

import jax
import jax.numpy as jnp
from jax import lax
from jax.experimental import pallas as pl
from jax.experimental.pallas import tpu as pltpu
from jax.sharding import PartitionSpec as P

HEAD = 128
NEW = 128
BLOCK = 256
MAXB = 16
NY = 4
NZ = 4
NX = 4
PART = 16
SLOTS = 8
CHUNKS = 4
LOG2_SCALE = HEAD**-0.5 * math.log2(math.e)
FLOOR = -1e30
ROWS = 144
MESH = pl.DeviceIdType.MESH


def nt(a, b):
    return lax.dot_general(a, b, (((1,), (1,)), ((), ())), preferred_element_type=jnp.float32)


def put(ref, at, o, m, l):
    ref[at + (slice(0, HEAD), slice(None))] = o.astype(jnp.bfloat16)
    high = l.astype(jnp.bfloat16).astype(jnp.float32)
    row = lax.broadcasted_iota(jnp.int32, (16, NEW), 0)
    stats = jnp.where(row == 0, m, jnp.where(row == 1, high, jnp.where(row == 2, l - high, 0.0)))
    ref[at + (slice(HEAD, ROWS), slice(None))] = stats.astype(jnp.bfloat16)


def get(ref, at):
    o = ref[at + (slice(0, HEAD), slice(None))].astype(jnp.float32)
    stats = ref[at + (slice(HEAD, ROWS), slice(None))].astype(jnp.float32)
    return o, stats[0:1], stats[1:2] + stats[2:3]


def merge(parts):
    m = functools.reduce(jnp.maximum, [p[1] for p in parts])
    o, l = 0.0, 0.0
    for po, pm, ps in parts:
        w = jnp.exp2(pm - m)
        o, l = o + po * w, l + ps * w
    return o, m, l


def layer_kernel(
    tab, q_ref, nkv_ref, res_ref, store_ref, w_ref, out_ref,
    kv_ref, qsrc, qbuf, k_sib, vt_own, vt_sib, nkv, part, r2, r1, rz, att,
    w, proj, x1, x2, zout, zin, sout, sin,
    kv_send, kv_recv, local,
    qs_send, qz_send, qz_recv, qy_send, qy_recv, qr_send, qr_recv,
    p2_send, p2_recv, p1_send, p1_recv, pz_send, pz_recv, at_send, at_recv,
    x1_send, x1_recv, x2_send, x2_recv, zh_send, zh_recv, si_send, si_recv,
):
    kv_own = pltpu.make_async_copy(store_ref, kv_ref, local.at[2])
    kv_own.start()
    me, tp = lax.axis_index("pool"), lax.axis_index("tp")
    core = lax.rem(me, 2)
    mz = lax.rem(lax.div(me, 2), NZ)
    my = lax.div(me, 2 * NZ)
    zh = lax.rem(tp, 2)
    mx = lax.div(tp, 2)
    up, down = lax.rem(my + 1, NY), lax.rem(my + NY - 1, NY)
    across = lax.rem(my + 2, NY)
    sib = 1 - core
    others = (mz + 1 - 2 * lax.rem(mz, 2), lax.rem(mz + 2, NZ), NZ - 1 - mz)
    pair, facing = mx + 1 - 2 * lax.rem(mx, 2), NX - 1 - mx
    width = w.shape[1]
    chunk = width // CHUNKS

    def dev(y, z, c):
        return (y * NZ + z) * 2 + c

    def tp_of(x, h):
        return x * 2 + h

    def remote(src, dst, send, recv, **to):
        return pltpu.make_async_remote_copy(
            src_ref=src, dst_ref=dst, send_sem=send, recv_sem=recv, device_id=to, device_id_type=MESH
        )

    def wait_into(ref, sem):
        pltpu.make_async_copy(ref, ref, sem).wait()

    barrier = pltpu.get_barrier_semaphore()
    partners = [{"pool": dev(my, z, c)} for z in others for c in range(2)]
    partners += [{"pool": p} for p in (dev(my, mz, sib), dev(up, mz, core), dev(down, mz, core))]
    partners += [{"tp": p} for p in (tp_of(pair, zh), tp_of(facing, zh))]
    partners += [{"pool": dev(my, mz, c), "tp": tp_of(mx, 1 - zh)} for c in range(2)]
    for p in partners:
        pl.semaphore_signal(barrier, inc=1, device_id=p, device_id_type=MESH)

    for i in range(2):
        for g in range(2):
            for h in range(4):
                for b in range(4):
                    to, at = (h % 2 * 4 + b) * PART, i * NEW + (2 * b + g) * PART
                    qsrc[i, g, h // 2, to : to + PART, :] = q_ref[at : at + PART, h * HEAD : (h + 1) * HEAD]

    pl.semaphore_wait(barrier, len(partners))

    def half(c):
        return pl.ds(pl.multiple_of(c * 2 * HEAD, 2 * HEAD), 2 * HEAD)

    def columns(c):
        return pl.ds(pl.multiple_of(c * width, width), width)

    def owner(s):
        return lax.rem(s, 2)

    def which(s):
        return lax.rem(lax.div(s, 2) + lax.rem(s, 2), 2)

    def share(s):
        return lax.div(s, 4)

    def tokens(i):
        return pl.ds(pl.multiple_of(i * NEW, NEW), NEW)

    def q_z(j, k, c):
        s = 2 * j + core
        return remote(
            qsrc.at[which(s), lax.div(j, 2), c], qbuf.at[s, my, mz],
            qz_send, qz_recv.at[s, mz], pool=dev(my, others[k], c),
        )

    def q_sib(j):
        s = 2 * j + core
        return remote(
            qsrc.at[which(s), j // 2, sib], qbuf.at[s, my, mz],
            qs_send, qz_recv.at[s, mz], pool=dev(my, mz, sib),
        )

    def q_own(j):
        s = 2 * j + core
        return pltpu.make_async_copy(qsrc.at[which(s), j // 2, core], qbuf.at[s, my, mz], qz_recv.at[s, mz])

    here = dev(my, mz, sib)
    nk_copy = remote(nkv_ref, nkv.at[core], kv_send.at[0], kv_recv.at[0], pool=here)
    k_copy = remote(kv_ref.at[:, :, pl.ds(0, HEAD)], k_sib, kv_send.at[1], kv_recv.at[1], pool=here)
    v_copy = remote(vt_own, vt_sib, kv_send.at[2], kv_recv.at[2], pool=here)
    nk_own = pltpu.make_async_copy(nkv_ref, nkv.at[core], local.at[0])
    w_own = pltpu.make_async_copy(w_ref.at[:, columns(core)], w, local.at[1])

    def q_y(s, d, z):
        piece = qbuf.at[s, my, z]
        passed = lax.div(z, 2) if d == 0 else 1 - lax.div(z, 2)
        return remote(piece, piece, qy_send, qy_recv.at[s, d, passed], pool=dev((up, down)[d], mz, core))

    def q_relay(s, d, j):
        to, of = ((up, down), (down, up))[d]
        piece = qbuf.at[s, of, 2 * d + j]
        return remote(piece, piece, qr_send, qr_recv.at[s], pool=dev(to, mz, core))

    def z_arrived(s, z):
        wait_into(qbuf.at[s, my, z], qz_recv.at[s, z])
        q_y(s, 0, z).start()
        q_y(s, 1, z).start()

    def y_arrived(s, d, passed):
        first = 2 * d if passed == 0 else 2 - 2 * d
        wait_into(qbuf.at[s, (down, up)[d], pl.ds(first, 2)], qy_recv.at[s, d, passed])

    def stage_r(s):
        for d in range(2):
            y_arrived(s, d, 0)
            for j in range(2):
                q_relay(s, d, j).start()

    per_core = SLOTS // 2

    def send_z(j):
        for k in range(NZ - 1):
            for c in range(2):
                q_z(j, k, c).start()

    for j in range(per_core):
        q_own(j).start()
        q_sib(j).start()
        if j == 0:
            send_z(0)
    for s in range(4):
        z_arrived(s, mz)
    nk_own.start()
    nk_copy.start()
    kv_own.wait()
    k_copy.start()

    @pl.loop(0, kv_ref.shape[0])
    def _(b):
        vt_own[b] = kv_ref[b, :, HEAD:].T

    v_copy.start()
    for z in others:
        z_arrived(0, z)
        z_arrived(1, z)
    send_z(1)
    w_own.start()
    stage_r(0)
    stage_r(1)

    key = lax.broadcasted_iota(jnp.int32, (BLOCK, NEW), 0)

    def attend(s, y, z):
        r = dev(y, z, owner(s)) * 2 + which(s)
        q = qbuf[s, y, z]
        codes = [tab[0, r], tab[1, r]]
        blocks = [c % 32 for c in codes]
        counts = [c // 32 for c in codes]
        keys = [kv_ref[blocks[0], :, :HEAD], k_sib[blocks[1]]]
        values = [vt_own[blocks[0]], vt_sib[blocks[1]]]
        t = [jnp.where(key < n, nt(k, q) * LOG2_SCALE, -jnp.inf) for k, n in zip(keys, counts)]
        m = jnp.maximum(jnp.max(t[0], axis=0, keepdims=True), jnp.max(t[1], axis=0, keepdims=True))
        m = jnp.maximum(m, FLOOR).astype(jnp.bfloat16).astype(jnp.float32)
        e = [jnp.exp2(x - m) for x in t]
        l = jnp.sum(e[0], axis=0, keepdims=True) + jnp.sum(e[1], axis=0, keepdims=True)
        o = [
            jnp.dot(v, x.astype(jnp.bfloat16), preferred_element_type=jnp.float32)
            for v, x in zip(values, e)
        ]
        put(part, (s, y, z), o[0] + o[1], m, l)

    def p_2(s, d, j):
        return remote(
            part.at[s, across, 2 * d + j], r2.at[s, d, j],
            p2_send, p2_recv.at[s, d], pool=dev((up, down)[d], mz, core),
        )

    def p_1(s, d, z):
        to = (up, down)[d]
        return remote(
            part.at[s, to, z], r1.at[s, d, z], p1_send, p1_recv.at[s, d], pool=dev(to, mz, core)
        )

    def p_z(s, k):
        z = others[k]
        return remote(part.at[s, my, z], rz.at[s, k], pz_send, pz_recv.at[s], pool=dev(my, z, core))

    def stage_c(s):
        @pl.when(s == 0)
        def _():
            for z in range(NZ):
                attend(s, my, z)

        for d in range(2):
            y_arrived(s, d, 1)
        wait_into(qbuf.at[s, across], qr_recv.at[s])

        for z in range(NZ):
            attend(s, across, z)
        for j in range(2):
            p_2(s, 0, j).start()
            p_2(s, 1, j).start()

        @pl.when(jnp.logical_and(s >= 1, s + 1 < SLOTS))
        def _():
            stage_r(s + 1)

        @pl.when(s == 0)
        def _():
            for z in others:
                z_arrived(2, z)

        for j in range(2):
            attend(s, up, 2 + j)
            attend(s, down, j)
        for j in range(2):
            p_1(s, 0, 2 + j).start()
            p_1(s, 1, j).start()

        for j in range(2):
            attend(s, up, j)
            attend(s, down, 2 + j)
        @pl.when(s > 0)
        def _():
            for z in range(NZ):
                attend(s, my, z)

    def stage_m(s):
        for d in range(2):
            wait_into(r2.at[s, d], p2_recv.at[s, d])
            for j in range(2):
                z, to = 2 * d + j, (up, down)[d]
                put(part, (s, to, z), *merge([get(part, (s, to, z)), get(r2, (s, d, j))]))
                p_1(s, d, z).start()

        @pl.when(s + 4 < SLOTS)
        def _():
            z_arrived(s + 4, mz)

        @pl.when(s + 3 < SLOTS)
        def _():
            for z in others:
                z_arrived(s + 3, z)

        @pl.when(jnp.logical_or(s == 0, s == 2))
        def _():
            send_z(lax.div(s, 2) + 2)

    def stage_h(s):
        for d in range(2):
            wait_into(r1.at[s, d], p1_recv.at[s, d])
        for k, z in enumerate((*others, mz)):
            put(part, (s, my, z), *merge([get(part, (s, my, z)), get(r1, (s, 0, z)), get(r1, (s, 1, z))]))
            if k < NZ - 1:
                p_z(s, k).start()

    def fresh(s):
        q = qbuf[s, my, mz]
        rows = nkv[owner(s), tokens(which(s)), :]
        j = lax.broadcasted_iota(jnp.int32, (NEW, NEW), 0)
        i = lax.broadcasted_iota(jnp.int32, (NEW, NEW), 1) % (4 * PART)
        i = i + i // PART * PART + share(s) * PART
        t = jnp.where(j <= i, nt(rows[:, :HEAD], q) * LOG2_SCALE, -jnp.inf)
        m = jnp.max(t, axis=0, keepdims=True).astype(jnp.bfloat16).astype(jnp.float32)
        e = jnp.exp2(t - m)
        o = jnp.dot(rows[:, HEAD:].T, e.astype(jnp.bfloat16), preferred_element_type=jnp.float32)
        return o, m, jnp.sum(e, axis=0, keepdims=True)

    def a_copy(s):
        mine = att.at[s, :, half(core)]
        return remote(mine, mine, at_send, at_recv.at[s], pool=here)

    def stage_f(s):
        parts = [fresh(s), get(part, (s, my, mz))]
        wait_into(rz.at[s], pz_recv.at[s])
        parts += [get(rz, (s, k)) for k in range(NZ - 1)]
        o, _, l = merge(parts)
        o = o / l
        o = o.T
        att[s, :, half(core)] = jnp.concatenate([o[: 4 * PART], o[4 * PART :]], axis=1).astype(jnp.bfloat16)
        a_copy(s).start()

    def is_dest(s):
        return lax.div(mx, 2) == which(s)

    def sent_half(s):
        return jnp.where(is_dest(s), 1 - lax.rem(mx, 2), lax.rem(mx, 2))

    def rows(h):
        return pl.ds(pl.multiple_of(h * 2 * PART, 2 * PART), 2 * PART)

    def part_of(h, z):
        return pl.ds(pl.multiple_of((2 * h + z) * PART, PART), PART)

    def cols(n):
        return pl.ds(pl.multiple_of(n * chunk, chunk), chunk)

    def x_1(s, n):
        return remote(
            proj.at[s, rows(sent_half(s)), cols(n)], x1.at[s, :, cols(n)],
            x1_send, x1_recv.at[s, n], tp=tp_of(pair, zh),
        )

    def x_2(s, n):
        return remote(
            proj.at[s, rows(1 - sent_half(s)), cols(n)], x2.at[s, :, cols(n)],
            x2_send, x2_recv.at[lax.div(s, 2), n], tp=tp_of(facing, zh),
        )

    def z_h(s, n):
        return remote(
            zout.at[s, :, cols(n)], zin.at[s, core, :, cols(n)], zh_send, zh_recv.at[share(s), core, n],
            pool=dev(my, mz, owner(s)), tp=tp_of(mx, 1 - zh),
        )

    def s_in(s, n):
        return remote(sout.at[s, :, cols(n)], sin.at[s, :, cols(n)], si_send, si_recv.at[share(s), n], pool=here)

    def stage_o(s):
        @pl.when(s == 0)
        def _():
            w_own.wait()

        theirs = att.at[s, :, half(sib)]
        wait_into(theirs, at_recv.at[s])

        @pl.loop(0, CHUNKS)
        def _(n):
            proj[s, :, cols(n)] = jnp.dot(
                att[s], w[:, cols(n)], preferred_element_type=jnp.float32
            ).astype(jnp.bfloat16)
            x_1(s, n).start()

    def f32(x):
        return x.astype(jnp.float32)

    def stage_x(s):
        @pl.when(jnp.logical_not(is_dest(s)))
        def _():
            keep = 1 - sent_half(s)

            @pl.loop(0, CHUNKS)
            def _(n):
                wait_into(x1.at[s, :, cols(n)], x1_recv.at[s, n])
                total = f32(proj[s, rows(keep), cols(n)]) + f32(x1[s, :, cols(n)])
                proj[s, rows(keep), cols(n)] = total.astype(jnp.bfloat16)
                x_2(s, n).start()

    def stage_d(s):
        @pl.when(is_dest(s))
        def _():
            keep = 1 - sent_half(s)

            def total(n, z):
                t = f32(proj[s, part_of(keep, z), cols(n)])
                return t + f32(x1[s, part_of(0, z), cols(n)]) + f32(x2[s, part_of(0, z), cols(n)])

            @pl.loop(0, CHUNKS)
            def _(n):
                wait_into(x1.at[s, :, cols(n)], x1_recv.at[s, n])
                wait_into(x2.at[s, :, cols(n)], x2_recv.at[lax.div(s, 2), n])
                zout[s, :, cols(n)] = total(n, 1 - zh).astype(jnp.bfloat16)
                z_h(s, n).start()

                @pl.when(owner(s) != core)
                def _():
                    sout[s, :, cols(n)] = total(n, zh).astype(jnp.bfloat16)
                    s_in(s, n).start()

    def stage_e(s):
        @pl.when(jnp.logical_and(is_dest(s), owner(s) == core))
        def _():
            keep = 1 - sent_half(s)
            out_rows = pl.ds(pl.multiple_of(share(s) * PART, PART), PART)

            @pl.loop(0, CHUNKS)
            def _(n):
                own = f32(proj[s, part_of(keep, zh), cols(n)])
                own += f32(x1[s, part_of(0, zh), cols(n)]) + f32(x2[s, part_of(0, zh), cols(n)])
                wait_into(sin.at[s, :, cols(n)], si_recv.at[share(s), n])
                for c, t in ((core, own), (sib, f32(sin[s, :, cols(n)]))):
                    wait_into(zin.at[s, c, :, cols(n)], zh_recv.at[share(s), c, n])
                    at = pl.ds(pl.multiple_of(c * width + n * chunk, chunk), chunk)
                    t += f32(zin[s, c, :, cols(n)]) + f32(res_ref[out_rows, at])
                    out_ref[out_rows, at] = t.astype(jnp.bfloat16)

    nk_own.wait()
    for copy in (k_copy, nk_copy, v_copy):
        copy.wait_send()
    wait_into(nkv.at[sib], kv_recv.at[0])
    wait_into(k_sib, kv_recv.at[1])
    wait_into(vt_sib, kv_recv.at[2])

    @pl.loop(0, SLOTS + 2)
    def _(t):
        def stage(f, s):
            @pl.when(jnp.logical_and(s >= 0, s < SLOTS))
            def _():
                f(s)

        stage(stage_c, t)
        stage(stage_h, t - 1)
        stage(stage_f, jnp.where(t < SLOTS - 1, t - 2, -1))
        stage(stage_m, t)
        stage(stage_f, jnp.where(t < SLOTS - 1, -1, t - 2))
        stage(stage_o, t - 2)
        stage(stage_d, jnp.where(t < SLOTS, t - 4, jnp.where(t > SLOTS, SLOTS - 4, -1)))
        stage(stage_x, t - 3)
        stage(stage_e, t - 7)

    stage_x(SLOTS - 1)
    for s in range(SLOTS - 3, SLOTS):
        stage_d(s)

    @pl.loop(SLOTS - 5, SLOTS)
    def _(s):
        stage_e(s)

    for ref, sem in (
        (qbuf.at[pl.ds(0, 6), 0], qz_send),
        (qbuf.at[0, 0], qs_send),
        (qbuf.at[pl.ds(0, 4)], qy_send),
        (qbuf.at[pl.ds(0, 2)], qr_send),
        (part.at[pl.ds(0, 2)], p2_send),
        (part.at[pl.ds(0, 4)], p1_send),
        (part.at[pl.ds(0, 6), 0], pz_send),
        (att.at[:, :, pl.ds(0, 2 * HEAD)], at_send),
        (x1, x1_send),
        (x2.at[pl.ds(0, SLOTS // 2)], x2_send),
        (zout.at[pl.ds(0, SLOTS // 2)], zh_send),
        (sout.at[pl.ds(0, SLOTS // 4)], si_send),
    ):
        wait_into(ref, sem)

def layer(tab, queries, nkv, store, residual, weight):
    bf = jnp.bfloat16
    blocks = store.shape[0]
    depth, width = weight.shape[0], weight.shape[1] // 2
    vmem = pl.BlockSpec(memory_space=pltpu.VMEM)
    dma = pltpu.SemaphoreType.DMA
    unit = (ROWS, NEW)
    one = dma(())
    return pl.pallas_call(
        layer_kernel,
        out_shape=jax.ShapeDtypeStruct(residual.shape, bf),
        in_specs=[pl.BlockSpec(memory_space=pltpu.SMEM)] + [vmem] * 3 + [pl.BlockSpec(memory_space=pl.ANY)] * 2,
        out_specs=vmem,
        scratch_shapes=[
            pltpu.VMEM(store.shape, bf),
            pltpu.VMEM((2, 2, 2, NEW, HEAD), bf),
            pltpu.VMEM((SLOTS, NY, NZ, NEW, HEAD), bf),
            pltpu.VMEM((blocks, BLOCK, HEAD), bf),
            pltpu.VMEM((blocks, HEAD, BLOCK), bf),
            pltpu.VMEM((blocks, HEAD, BLOCK), bf),
            pltpu.VMEM((2, 2 * NEW, 2 * HEAD), bf),
            pltpu.VMEM((SLOTS, NY, NZ) + unit, bf),
            pltpu.VMEM((SLOTS, 2, 2) + unit, bf),
            pltpu.VMEM((SLOTS, 2, NZ) + unit, bf),
            pltpu.VMEM((SLOTS, NZ - 1) + unit, bf),
            pltpu.VMEM((SLOTS, 4 * PART, 4 * HEAD), bf),
            pltpu.VMEM((depth, width), bf),
            pltpu.VMEM((SLOTS, 4 * PART, width), bf),
            pltpu.VMEM((SLOTS, 2 * PART, width), bf),
            pltpu.VMEM((SLOTS, 2 * PART, width), bf),
            pltpu.VMEM((SLOTS, PART, width), bf),
            pltpu.VMEM((SLOTS, 2, PART, width), bf),
            pltpu.VMEM((SLOTS, PART, width), bf),
            pltpu.VMEM((SLOTS, PART, width), bf),
            dma((3,)), dma((3,)), dma((3,)),
            one, one, dma((SLOTS, NZ)),
            one, dma((SLOTS, 2, 2)), one, dma((SLOTS,)),
            one, dma((SLOTS, 2)), one, dma((SLOTS, 2)),
            one, dma((SLOTS,)), one, dma((SLOTS,)),
            one, dma((SLOTS, CHUNKS)), one, dma((SLOTS // 2, CHUNKS)),
            one, dma((2, 2, CHUNKS)), one, dma((2, CHUNKS)),
        ],
        compiler_params=pltpu.CompilerParams(
            collective_id=0, has_side_effects=True, vmem_limit_bytes=56 * 1024 * 1024
        ),
    )(tab, queries, nkv, residual, store, weight)


def hit_table(hit_dev, hit_blk, prefix_len):
    me = lax.axis_index("pool")
    there = jnp.stack([me, me + 1 - 2 * (me % 2)])[:, None, None]
    start = jnp.arange(MAXB, dtype=jnp.int32) * BLOCK
    count = jnp.clip(prefix_len[:, None] - start[None, :], 0, BLOCK)
    return jnp.sum(jnp.where(hit_dev[None] == there, (hit_blk + 32 * count)[None], 0), axis=2)


def shards(queries, new_key_values, key_value_store, o_weight, residual, hit_dev, hit_blk, prefix_len):
    tab = hit_table(hit_dev, hit_blk, prefix_len)
    return layer(tab, queries, new_key_values, key_value_store, residual, o_weight)


def solution(mesh):
    placed = (
        P("pool", "tp"),
        P("pool", "tp"),
        P("pool", None, "tp"),
        P("tp", None),
        P(("pool", "tp"), None),
        P(),
        P(),
        P(),
    )
    return jax.shard_map(
        shards, mesh=mesh, in_specs=placed, out_specs=P(("pool", "tp"), None), check_vma=False
    )
```

```python
import functools
import math

import jax
import jax.numpy as jnp
from jax import lax
from jax.experimental import pallas as pl
from jax.experimental.pallas import tpu as pltpu
from jax.sharding import PartitionSpec as P

HEAD = 128
NEW = 128
BLOCK = 256
MAXB = 16
NY = 4
NZ = 4
NX = 4
PART = 16
SLOTS = 8
CHUNKS = 4
LOG2_SCALE = HEAD**-0.5 * math.log2(math.e)
FLOOR = -1e30
ROWS = 144
MESH = pl.DeviceIdType.MESH


def nt(a, b):
    return lax.dot_general(a, b, (((1,), (1,)), ((), ())), preferred_element_type=jnp.float32)


def put(ref, at, o, m, l):
    ref[at + (slice(0, HEAD), slice(None))] = o.astype(jnp.bfloat16)
    high = l.astype(jnp.bfloat16).astype(jnp.float32)
    row = lax.broadcasted_iota(jnp.int32, (16, NEW), 0)
    stats = jnp.where(row == 0, m, jnp.where(row == 1, high, jnp.where(row == 2, l - high, 0.0)))
    ref[at + (slice(HEAD, ROWS), slice(None))] = stats.astype(jnp.bfloat16)


def get(ref, at):
    o = ref[at + (slice(0, HEAD), slice(None))].astype(jnp.float32)
    stats = ref[at + (slice(HEAD, ROWS), slice(None))].astype(jnp.float32)
    return o, stats[0:1], stats[1:2] + stats[2:3]


def merge(parts):
    m = functools.reduce(jnp.maximum, [p[1] for p in parts])
    o, l = 0.0, 0.0
    for po, pm, ps in parts:
        w = jnp.exp2(pm - m)
        o, l = o + po * w, l + ps * w
    return o, m, l


def layer_kernel(
    tab, q_ref, nkv_ref, res_ref, store_ref, w_ref, out_ref,
    kv_ref, qsrc, qbuf, k_sib, vt_own, vt_sib, nkv, part, r2, r1, rz, att,
    w, proj, x1, x2, zout, zin, sout, sin,
    kv_send, kv_recv, local,
    qs_send, qz_send, qz_recv, qy_send, qy_recv, qr_send, qr_recv,
    p2_send, p2_recv, p1_send, p1_recv, pz_send, pz_recv, at_send, at_recv,
    x1_send, x1_recv, x2_send, x2_recv, zh_send, zh_recv, si_send, si_recv,
):
    kv_own = pltpu.make_async_copy(store_ref, kv_ref, local.at[2])
    kv_own.start()
    me, tp = lax.axis_index("pool"), lax.axis_index("tp")
    core = lax.rem(me, 2)
    mz = lax.rem(lax.div(me, 2), NZ)
    my = lax.div(me, 2 * NZ)
    zh = lax.rem(tp, 2)
    mx = lax.div(tp, 2)
    up, down = lax.rem(my + 1, NY), lax.rem(my + NY - 1, NY)
    across = lax.rem(my + 2, NY)
    sib = 1 - core
    others = (mz + 1 - 2 * lax.rem(mz, 2), lax.rem(mz + 2, NZ), NZ - 1 - mz)
    pair, facing = mx + 1 - 2 * lax.rem(mx, 2), NX - 1 - mx
    width = w.shape[1]
    chunk = width // CHUNKS

    def dev(y, z, c):
        return (y * NZ + z) * 2 + c

    def tp_of(x, h):
        return x * 2 + h

    def remote(src, dst, send, recv, **to):
        return pltpu.make_async_remote_copy(
            src_ref=src, dst_ref=dst, send_sem=send, recv_sem=recv, device_id=to, device_id_type=MESH
        )

    def wait_into(ref, sem):
        pltpu.make_async_copy(ref, ref, sem).wait()

    barrier = pltpu.get_barrier_semaphore()
    partners = [{"pool": dev(my, z, c)} for z in others for c in range(2)]
    partners += [{"pool": p} for p in (dev(my, mz, sib), dev(up, mz, core), dev(down, mz, core))]
    partners += [{"tp": p} for p in (tp_of(pair, zh), tp_of(facing, zh))]
    partners += [{"pool": dev(my, mz, c), "tp": tp_of(mx, 1 - zh)} for c in range(2)]
    for p in partners:
        pl.semaphore_signal(barrier, inc=1, device_id=p, device_id_type=MESH)

    for i in range(2):
        for g in range(2):
            for h in range(4):
                for b in range(4):
                    to, at = (h % 2 * 4 + b) * PART, i * NEW + (2 * b + g) * PART
                    qsrc[i, g, h // 2, to : to + PART, :] = q_ref[at : at + PART, h * HEAD : (h + 1) * HEAD]

    pl.semaphore_wait(barrier, len(partners))

    def half(c):
        return pl.ds(pl.multiple_of(c * 2 * HEAD, 2 * HEAD), 2 * HEAD)

    def columns(c):
        return pl.ds(pl.multiple_of(c * width, width), width)

    def owner(s):
        return lax.rem(s, 2)

    def which(s):
        return lax.rem(lax.rem(s, 2) + lax.div(s, 4), 2)

    def share(s):
        return lax.rem(lax.div(s, 2), 2)

    def tokens(i):
        return pl.ds(pl.multiple_of(i * NEW, NEW), NEW)

    def q_z(j, k, c):
        s = 2 * j + core
        return remote(
            qsrc.at[which(s), share(s), c], qbuf.at[s, my, mz],
            qz_send, qz_recv.at[s, mz], pool=dev(my, others[k], c),
        )

    def q_sib(j):
        s = 2 * j + core
        return remote(
            qsrc.at[which(s), share(s), sib], qbuf.at[s, my, mz],
            qs_send, qz_recv.at[s, mz], pool=dev(my, mz, sib),
        )

    def q_own(j):
        s = 2 * j + core
        return pltpu.make_async_copy(qsrc.at[which(s), share(s), core], qbuf.at[s, my, mz], qz_recv.at[s, mz])

    here = dev(my, mz, sib)
    nk_copy = remote(nkv_ref, nkv.at[core], kv_send.at[0], kv_recv.at[0], pool=here)
    k_copy = remote(kv_ref.at[:, :, pl.ds(0, HEAD)], k_sib, kv_send.at[1], kv_recv.at[1], pool=here)
    v_copy = remote(vt_own, vt_sib, kv_send.at[2], kv_recv.at[2], pool=here)
    nk_own = pltpu.make_async_copy(nkv_ref, nkv.at[core], local.at[0])
    w_own = pltpu.make_async_copy(w_ref.at[:, columns(core)], w, local.at[1])

    def q_y(s, d, z):
        piece = qbuf.at[s, my, z]
        passed = lax.div(z, 2) if d == 0 else 1 - lax.div(z, 2)
        return remote(piece, piece, qy_send, qy_recv.at[s, d, passed], pool=dev((up, down)[d], mz, core))

    def q_relay(s, d, j):
        to, of = ((up, down), (down, up))[d]
        piece = qbuf.at[s, of, 2 * d + j]
        return remote(piece, piece, qr_send, qr_recv.at[s], pool=dev(to, mz, core))

    def z_arrived(s, z):
        wait_into(qbuf.at[s, my, z], qz_recv.at[s, z])
        q_y(s, 0, z).start()
        q_y(s, 1, z).start()

    def y_arrived(s, d, passed):
        first = 2 * d if passed == 0 else 2 - 2 * d
        wait_into(qbuf.at[s, (down, up)[d], pl.ds(first, 2)], qy_recv.at[s, d, passed])

    def stage_r(s):
        for d in range(2):
            y_arrived(s, d, 0)
            for j in range(2):
                q_relay(s, d, j).start()

    per_core = SLOTS // 2

    def send_z(j):
        for k in range(NZ - 1):
            for c in range(2):
                q_z(j, k, c).start()

    for j in range(per_core):
        q_own(j).start()
        q_sib(j).start()
        if j == 0:
            send_z(0)
    for s in range(4):
        z_arrived(s, mz)
    nk_own.start()
    nk_copy.start()
    kv_own.wait()
    k_copy.start()

    @pl.loop(0, kv_ref.shape[0])
    def _(b):
        vt_own[b] = kv_ref[b, :, HEAD:].T

    v_copy.start()
    for z in others:
        z_arrived(0, z)
        z_arrived(1, z)
    send_z(1)
    w_own.start()
    stage_r(0)
    stage_r(1)

    key = lax.broadcasted_iota(jnp.int32, (BLOCK, NEW), 0)

    def attend(s, y, z):
        r = dev(y, z, owner(s)) * 2 + which(s)
        q = qbuf[s, y, z]
        codes = [tab[0, r], tab[1, r]]
        blocks = [c % 32 for c in codes]
        counts = [c // 32 for c in codes]
        keys = [kv_ref[blocks[0], :, :HEAD], k_sib[blocks[1]]]
        values = [vt_own[blocks[0]], vt_sib[blocks[1]]]
        t = [jnp.where(key < n, nt(k, q) * LOG2_SCALE, -jnp.inf) for k, n in zip(keys, counts)]
        m = jnp.maximum(jnp.max(t[0], axis=0, keepdims=True), jnp.max(t[1], axis=0, keepdims=True))
        m = jnp.maximum(m, FLOOR).astype(jnp.bfloat16).astype(jnp.float32)
        e = [jnp.exp2(x - m) for x in t]
        l = jnp.sum(e[0], axis=0, keepdims=True) + jnp.sum(e[1], axis=0, keepdims=True)
        o = [
            jnp.dot(v, x.astype(jnp.bfloat16), preferred_element_type=jnp.float32)
            for v, x in zip(values, e)
        ]
        put(part, (s, y, z), o[0] + o[1], m, l)

    def p_2(s, d, j):
        return remote(
            part.at[s, across, 2 * d + j], r2.at[s, d, j],
            p2_send, p2_recv.at[s, d], pool=dev((up, down)[d], mz, core),
        )

    def p_1(s, d, z):
        to = (up, down)[d]
        return remote(
            part.at[s, to, z], r1.at[s, d, z], p1_send, p1_recv.at[s, d], pool=dev(to, mz, core)
        )

    def p_z(s, k):
        z = others[k]
        return remote(part.at[s, my, z], rz.at[s, k], pz_send, pz_recv.at[s], pool=dev(my, z, core))

    def stage_c(s):
        @pl.when(s == 0)
        def _():
            for z in range(NZ):
                attend(s, my, z)

        for d in range(2):
            y_arrived(s, d, 1)
        wait_into(qbuf.at[s, across], qr_recv.at[s])

        for z in range(NZ):
            attend(s, across, z)
        for j in range(2):
            p_2(s, 0, j).start()
            p_2(s, 1, j).start()

        @pl.when(jnp.logical_and(s >= 1, s + 1 < SLOTS))
        def _():
            stage_r(s + 1)

        @pl.when(s == 0)
        def _():
            for z in others:
                z_arrived(2, z)

        for j in range(2):
            attend(s, up, 2 + j)
            attend(s, down, j)
        for j in range(2):
            p_1(s, 0, 2 + j).start()
            p_1(s, 1, j).start()

        for j in range(2):
            attend(s, up, j)
            attend(s, down, 2 + j)
        @pl.when(s > 0)
        def _():
            for z in range(NZ):
                attend(s, my, z)

    def stage_m(s):
        for d in range(2):
            wait_into(r2.at[s, d], p2_recv.at[s, d])
            for j in range(2):
                z, to = 2 * d + j, (up, down)[d]
                put(part, (s, to, z), *merge([get(part, (s, to, z)), get(r2, (s, d, j))]))
                p_1(s, d, z).start()

        @pl.when(s + 4 < SLOTS)
        def _():
            z_arrived(s + 4, mz)

        @pl.when(s + 3 < SLOTS)
        def _():
            for z in others:
                z_arrived(s + 3, z)

        @pl.when(jnp.logical_or(s == 0, s == 2))
        def _():
            send_z(lax.div(s, 2) + 2)

    def stage_h(s):
        for d in range(2):
            wait_into(r1.at[s, d], p1_recv.at[s, d])
        for k, z in enumerate((*others, mz)):
            put(part, (s, my, z), *merge([get(part, (s, my, z)), get(r1, (s, 0, z)), get(r1, (s, 1, z))]))
            if k < NZ - 1:
                p_z(s, k).start()

    def fresh(s):
        q = qbuf[s, my, mz]
        rows = nkv[owner(s), tokens(which(s)), :]
        j = lax.broadcasted_iota(jnp.int32, (NEW, NEW), 0)
        i = lax.broadcasted_iota(jnp.int32, (NEW, NEW), 1) % (4 * PART)
        i = i + i // PART * PART + share(s) * PART
        t = jnp.where(j <= i, nt(rows[:, :HEAD], q) * LOG2_SCALE, -jnp.inf)
        m = jnp.max(t, axis=0, keepdims=True).astype(jnp.bfloat16).astype(jnp.float32)
        e = jnp.exp2(t - m)
        o = jnp.dot(rows[:, HEAD:].T, e.astype(jnp.bfloat16), preferred_element_type=jnp.float32)
        return o, m, jnp.sum(e, axis=0, keepdims=True)

    def a_copy(s):
        mine = att.at[s, :, half(core)]
        return remote(mine, mine, at_send, at_recv.at[s], pool=here)

    def stage_f(s):
        parts = [fresh(s), get(part, (s, my, mz))]
        wait_into(rz.at[s], pz_recv.at[s])
        parts += [get(rz, (s, k)) for k in range(NZ - 1)]
        o, _, l = merge(parts)
        o = o / l
        o = o.T
        att[s, :, half(core)] = jnp.concatenate([o[: 4 * PART], o[4 * PART :]], axis=1).astype(jnp.bfloat16)
        a_copy(s).start()

    def is_dest(s):
        return lax.div(mx, 2) == which(s)

    def sent_half(s):
        return jnp.where(is_dest(s), 1 - lax.rem(mx, 2), lax.rem(mx, 2))

    def rows(h):
        return pl.ds(pl.multiple_of(h * 2 * PART, 2 * PART), 2 * PART)

    def part_of(h, z):
        return pl.ds(pl.multiple_of((2 * h + z) * PART, PART), PART)

    def cols(n):
        return pl.ds(pl.multiple_of(n * chunk, chunk), chunk)

    def x_1(s, n):
        return remote(
            proj.at[s, rows(sent_half(s)), cols(n)], x1.at[s, :, cols(n)],
            x1_send, x1_recv.at[s, n], tp=tp_of(pair, zh),
        )

    def x_2(s, n):
        return remote(
            proj.at[s, rows(1 - sent_half(s)), cols(n)], x2.at[s, :, cols(n)],
            x2_send, x2_recv.at[lax.div(s, 2), n], tp=tp_of(facing, zh),
        )

    def z_h(s, n):
        return remote(
            zout.at[s, :, cols(n)], zin.at[s, core, :, cols(n)], zh_send, zh_recv.at[share(s), core, n],
            pool=dev(my, mz, owner(s)), tp=tp_of(mx, 1 - zh),
        )

    def s_in(s, n):
        return remote(sout.at[s, :, cols(n)], sin.at[s, :, cols(n)], si_send, si_recv.at[share(s), n], pool=here)

    def stage_o(s):
        @pl.when(s == 0)
        def _():
            w_own.wait()

        theirs = att.at[s, :, half(sib)]
        wait_into(theirs, at_recv.at[s])

        @pl.loop(0, CHUNKS)
        def _(n):
            proj[s, :, cols(n)] = jnp.dot(
                att[s], w[:, cols(n)], preferred_element_type=jnp.float32
            ).astype(jnp.bfloat16)
            x_1(s, n).start()

    def f32(x):
        return x.astype(jnp.float32)

    def stage_x(s):
        @pl.when(jnp.logical_not(is_dest(s)))
        def _():
            keep = 1 - sent_half(s)

            @pl.loop(0, CHUNKS)
            def _(n):
                wait_into(x1.at[s, :, cols(n)], x1_recv.at[s, n])
                total = f32(proj[s, rows(keep), cols(n)]) + f32(x1[s, :, cols(n)])
                proj[s, rows(keep), cols(n)] = total.astype(jnp.bfloat16)
                x_2(s, n).start()

    def stage_d(s):
        @pl.when(is_dest(s))
        def _():
            keep = 1 - sent_half(s)

            def total(n, z):
                t = f32(proj[s, part_of(keep, z), cols(n)])
                return t + f32(x1[s, part_of(0, z), cols(n)]) + f32(x2[s, part_of(0, z), cols(n)])

            @pl.loop(0, CHUNKS)
            def _(n):
                wait_into(x1.at[s, :, cols(n)], x1_recv.at[s, n])
                wait_into(x2.at[s, :, cols(n)], x2_recv.at[lax.div(s, 2), n])
                zout[s, :, cols(n)] = total(n, 1 - zh).astype(jnp.bfloat16)
                z_h(s, n).start()

                @pl.when(owner(s) != core)
                def _():
                    sout[s, :, cols(n)] = total(n, zh).astype(jnp.bfloat16)
                    s_in(s, n).start()

    def stage_e(s):
        @pl.when(jnp.logical_and(is_dest(s), owner(s) == core))
        def _():
            keep = 1 - sent_half(s)
            out_rows = pl.ds(pl.multiple_of(share(s) * PART, PART), PART)

            @pl.loop(0, CHUNKS)
            def _(n):
                own = f32(proj[s, part_of(keep, zh), cols(n)])
                own += f32(x1[s, part_of(0, zh), cols(n)]) + f32(x2[s, part_of(0, zh), cols(n)])
                wait_into(sin.at[s, :, cols(n)], si_recv.at[share(s), n])
                for c, t in ((core, own), (sib, f32(sin[s, :, cols(n)]))):
                    wait_into(zin.at[s, c, :, cols(n)], zh_recv.at[share(s), c, n])
                    at = pl.ds(pl.multiple_of(c * width + n * chunk, chunk), chunk)
                    t += f32(zin[s, c, :, cols(n)]) + f32(res_ref[out_rows, at])
                    out_ref[out_rows, at] = t.astype(jnp.bfloat16)

    nk_own.wait()
    for copy in (k_copy, nk_copy, v_copy):
        copy.wait_send()
    wait_into(nkv.at[sib], kv_recv.at[0])
    wait_into(k_sib, kv_recv.at[1])
    wait_into(vt_sib, kv_recv.at[2])

    @pl.loop(0, SLOTS + 2)
    def _(t):
        def stage(f, s):
            @pl.when(jnp.logical_and(s >= 0, s < SLOTS))
            def _():
                f(s)

        stage(stage_c, t)
        stage(stage_h, t - 1)
        stage(stage_f, jnp.where(t < SLOTS - 1, t - 2, -1))
        stage(stage_m, t)
        stage(stage_f, jnp.where(t < SLOTS - 1, -1, t - 2))
        stage(stage_o, t - 2)
        stage(stage_d, jnp.where(t < SLOTS, t - 4, jnp.where(t > SLOTS, SLOTS - 4, -1)))
        stage(stage_x, t - 3)
        stage(stage_e, t - 7)

    stage_d(SLOTS - 3)
    stage_x(SLOTS - 1)
    for s in range(SLOTS - 2, SLOTS):
        stage_d(s)

    @pl.loop(SLOTS - 5, SLOTS)
    def _(s):
        stage_e(s)

    for ref, sem in (
        (qbuf.at[pl.ds(0, 6), 0], qz_send),
        (qbuf.at[0, 0], qs_send),
        (qbuf.at[pl.ds(0, 4)], qy_send),
        (qbuf.at[pl.ds(0, 2)], qr_send),
        (part.at[pl.ds(0, 2)], p2_send),
        (part.at[pl.ds(0, 4)], p1_send),
        (part.at[pl.ds(0, 6), 0], pz_send),
        (att.at[:, :, pl.ds(0, 2 * HEAD)], at_send),
        (x1, x1_send),
        (x2.at[pl.ds(0, SLOTS // 2)], x2_send),
        (zout.at[pl.ds(0, SLOTS // 2)], zh_send),
        (sout.at[pl.ds(0, SLOTS // 4)], si_send),
    ):
        wait_into(ref, sem)

def layer(tab, queries, nkv, store, residual, weight):
    bf = jnp.bfloat16
    blocks = store.shape[0]
    depth, width = weight.shape[0], weight.shape[1] // 2
    vmem = pl.BlockSpec(memory_space=pltpu.VMEM)
    dma = pltpu.SemaphoreType.DMA
    unit = (ROWS, NEW)
    one = dma(())
    return pl.pallas_call(
        layer_kernel,
        out_shape=jax.ShapeDtypeStruct(residual.shape, bf),
        in_specs=[pl.BlockSpec(memory_space=pltpu.SMEM)] + [vmem] * 3 + [pl.BlockSpec(memory_space=pl.ANY)] * 2,
        out_specs=vmem,
        scratch_shapes=[
            pltpu.VMEM(store.shape, bf),
            pltpu.VMEM((2, 2, 2, NEW, HEAD), bf),
            pltpu.VMEM((SLOTS, NY, NZ, NEW, HEAD), bf),
            pltpu.VMEM((blocks, BLOCK, HEAD), bf),
            pltpu.VMEM((blocks, HEAD, BLOCK), bf),
            pltpu.VMEM((blocks, HEAD, BLOCK), bf),
            pltpu.VMEM((2, 2 * NEW, 2 * HEAD), bf),
            pltpu.VMEM((SLOTS, NY, NZ) + unit, bf),
            pltpu.VMEM((SLOTS, 2, 2) + unit, bf),
            pltpu.VMEM((SLOTS, 2, NZ) + unit, bf),
            pltpu.VMEM((SLOTS, NZ - 1) + unit, bf),
            pltpu.VMEM((SLOTS, 4 * PART, 4 * HEAD), bf),
            pltpu.VMEM((depth, width), bf),
            pltpu.VMEM((SLOTS, 4 * PART, width), bf),
            pltpu.VMEM((SLOTS, 2 * PART, width), bf),
            pltpu.VMEM((SLOTS, 2 * PART, width), bf),
            pltpu.VMEM((SLOTS, PART, width), bf),
            pltpu.VMEM((SLOTS, 2, PART, width), bf),
            pltpu.VMEM((SLOTS, PART, width), bf),
            pltpu.VMEM((SLOTS, PART, width), bf),
            dma((3,)), dma((3,)), dma((3,)),
            one, one, dma((SLOTS, NZ)),
            one, dma((SLOTS, 2, 2)), one, dma((SLOTS,)),
            one, dma((SLOTS, 2)), one, dma((SLOTS, 2)),
            one, dma((SLOTS,)), one, dma((SLOTS,)),
            one, dma((SLOTS, CHUNKS)), one, dma((SLOTS // 2, CHUNKS)),
            one, dma((2, 2, CHUNKS)), one, dma((2, CHUNKS)),
        ],
        compiler_params=pltpu.CompilerParams(
            collective_id=0, has_side_effects=True, vmem_limit_bytes=56 * 1024 * 1024
        ),
    )(tab, queries, nkv, residual, store, weight)


def hit_table(hit_dev, hit_blk, prefix_len):
    me = lax.axis_index("pool")
    there = jnp.stack([me, me + 1 - 2 * (me % 2)])[:, None, None]
    start = jnp.arange(MAXB, dtype=jnp.int32) * BLOCK
    count = jnp.clip(prefix_len[:, None] - start[None, :], 0, BLOCK)
    return jnp.sum(jnp.where(hit_dev[None] == there, (hit_blk + 32 * count)[None], 0), axis=2)


def shards(queries, new_key_values, key_value_store, o_weight, residual, hit_dev, hit_blk, prefix_len):
    tab = hit_table(hit_dev, hit_blk, prefix_len)
    return layer(tab, queries, new_key_values, key_value_store, residual, o_weight)


def solution(mesh):
    placed = (
        P("pool", "tp"),
        P("pool", "tp"),
        P("pool", None, "tp"),
        P("tp", None),
        P(("pool", "tp"), None),
        P(),
        P(),
        P(),
    )
    return jax.shard_map(
        shards, mesh=mesh, in_specs=placed, out_specs=P(("pool", "tp"), None), check_vma=False
    )
```

```python
import functools
import math

import jax
import jax.numpy as jnp
from jax import lax
from jax.experimental import pallas as pl
from jax.experimental.pallas import tpu as pltpu
from jax.sharding import PartitionSpec as P

HEAD = 128
NEW = 128
BLOCK = 256
MAXB = 16
NY = 4
NZ = 4
NX = 4
PART = 16
SLOTS = 8
CHUNKS = 4
LOG2_SCALE = HEAD**-0.5 * math.log2(math.e)
FLOOR = -1e30
ROWS = 144
MESH = pl.DeviceIdType.MESH


def nt(a, b):
    return lax.dot_general(a, b, (((1,), (1,)), ((), ())), preferred_element_type=jnp.float32)


def put(ref, at, o, m, l):
    ref[at + (slice(0, HEAD), slice(None))] = o.astype(jnp.bfloat16)
    high = l.astype(jnp.bfloat16).astype(jnp.float32)
    row = lax.broadcasted_iota(jnp.int32, (16, NEW), 0)
    stats = jnp.where(row == 0, m, jnp.where(row == 1, high, jnp.where(row == 2, l - high, 0.0)))
    ref[at + (slice(HEAD, ROWS), slice(None))] = stats.astype(jnp.bfloat16)


def get(ref, at):
    o = ref[at + (slice(0, HEAD), slice(None))].astype(jnp.float32)
    stats = ref[at + (slice(HEAD, ROWS), slice(None))].astype(jnp.float32)
    return o, stats[0:1], stats[1:2] + stats[2:3]


def merge(parts):
    m = functools.reduce(jnp.maximum, [p[1] for p in parts])
    o, l = 0.0, 0.0
    for po, pm, ps in parts:
        w = jnp.exp2(pm - m)
        o, l = o + po * w, l + ps * w
    return o, m, l


def layer_kernel(
    tab, q_ref, nkv_ref, res_ref, store_ref, w_ref, out_ref,
    kv_ref, qsrc, qbuf, k_sib, vt_own, vt_sib, nkv, part, r2, r1, rz, att,
    w, proj, x1, x2, zout, zin, sout, sin,
    kv_send, kv_recv, local,
    qs_send, qz_send, qz_recv, qy_send, qy_recv, qr_send, qr_recv,
    p2_send, p2_recv, p1_send, p1_recv, pz_send, pz_recv, at_send, at_recv,
    x1_send, x1_recv, x2_send, x2_recv, zh_send, zh_recv, si_send, si_recv,
):
    kv_own = pltpu.make_async_copy(store_ref, kv_ref, local.at[2])
    kv_own.start()
    me, tp = lax.axis_index("pool"), lax.axis_index("tp")
    core = lax.rem(me, 2)
    mz = lax.rem(lax.div(me, 2), NZ)
    my = lax.div(me, 2 * NZ)
    zh = lax.rem(tp, 2)
    mx = lax.div(tp, 2)
    up, down = lax.rem(my + 1, NY), lax.rem(my + NY - 1, NY)
    across = lax.rem(my + 2, NY)
    sib = 1 - core
    others = (mz + 1 - 2 * lax.rem(mz, 2), lax.rem(mz + 2, NZ), NZ - 1 - mz)
    pair, facing = mx + 1 - 2 * lax.rem(mx, 2), NX - 1 - mx
    width = w.shape[1]
    chunk = width // CHUNKS

    def dev(y, z, c):
        return (y * NZ + z) * 2 + c

    def tp_of(x, h):
        return x * 2 + h

    def remote(src, dst, send, recv, **to):
        return pltpu.make_async_remote_copy(
            src_ref=src, dst_ref=dst, send_sem=send, recv_sem=recv, device_id=to, device_id_type=MESH
        )

    def wait_into(ref, sem):
        pltpu.make_async_copy(ref, ref, sem).wait()

    barrier = pltpu.get_barrier_semaphore()
    partners = [{"pool": dev(my, z, c)} for z in others for c in range(2)]
    partners += [{"pool": p} for p in (dev(my, mz, sib), dev(up, mz, core), dev(down, mz, core))]
    partners += [{"tp": p} for p in (tp_of(pair, zh), tp_of(facing, zh))]
    partners += [{"pool": dev(my, mz, c), "tp": tp_of(mx, 1 - zh)} for c in range(2)]
    for p in partners:
        pl.semaphore_signal(barrier, inc=1, device_id=p, device_id_type=MESH)

    for i in range(2):
        for g in range(2):
            for h in range(4):
                for b in range(4):
                    to, at = (h % 2 * 4 + b) * PART, i * NEW + (2 * b + g) * PART
                    qsrc[i, g, h // 2, to : to + PART, :] = q_ref[at : at + PART, h * HEAD : (h + 1) * HEAD]

    pl.semaphore_wait(barrier, len(partners))

    def half(c):
        return pl.ds(pl.multiple_of(c * 2 * HEAD, 2 * HEAD), 2 * HEAD)

    def columns(c):
        return pl.ds(pl.multiple_of(c * width, width), width)

    def owner(s):
        return lax.rem(s, 2)

    def which(s):
        return lax.rem(lax.rem(s, 2) + lax.div(s, 4), 2)

    def share(s):
        return lax.rem(lax.div(s, 2), 2)

    def tokens(i):
        return pl.ds(pl.multiple_of(i * NEW, NEW), NEW)

    def q_z(j, k, c):
        s = 2 * j + core
        return remote(
            qsrc.at[which(s), share(s), c], qbuf.at[s, my, mz],
            qz_send, qz_recv.at[s, mz], pool=dev(my, others[k], c),
        )

    def q_sib(j):
        s = 2 * j + core
        return remote(
            qsrc.at[which(s), share(s), sib], qbuf.at[s, my, mz],
            qs_send, qz_recv.at[s, mz], pool=dev(my, mz, sib),
        )

    def q_own(j):
        s = 2 * j + core
        return pltpu.make_async_copy(qsrc.at[which(s), share(s), core], qbuf.at[s, my, mz], qz_recv.at[s, mz])

    here = dev(my, mz, sib)
    nk_copy = remote(nkv_ref, nkv.at[core], kv_send.at[0], kv_recv.at[0], pool=here)
    k_copy = remote(kv_ref.at[:, :, pl.ds(0, HEAD)], k_sib, kv_send.at[1], kv_recv.at[1], pool=here)
    v_copy = remote(vt_own, vt_sib, kv_send.at[2], kv_recv.at[2], pool=here)
    nk_own = pltpu.make_async_copy(nkv_ref, nkv.at[core], local.at[0])
    w_own = pltpu.make_async_copy(w_ref.at[:, columns(core)], w, local.at[1])

    def q_y(s, d, z):
        piece = qbuf.at[s, my, z]
        passed = lax.div(z, 2) if d == 0 else 1 - lax.div(z, 2)
        return remote(piece, piece, qy_send, qy_recv.at[s, d, passed], pool=dev((up, down)[d], mz, core))

    def q_relay(s, d, j):
        to, of = ((up, down), (down, up))[d]
        piece = qbuf.at[s, of, 2 * d + j]
        return remote(piece, piece, qr_send, qr_recv.at[s], pool=dev(to, mz, core))

    def z_arrived(s, z):
        wait_into(qbuf.at[s, my, z], qz_recv.at[s, z])
        q_y(s, 0, z).start()
        q_y(s, 1, z).start()

    def y_arrived(s, d, passed):
        first = 2 * d if passed == 0 else 2 - 2 * d
        wait_into(qbuf.at[s, (down, up)[d], pl.ds(first, 2)], qy_recv.at[s, d, passed])

    def stage_r(s):
        for d in range(2):
            y_arrived(s, d, 0)
            for j in range(2):
                q_relay(s, d, j).start()

    per_core = SLOTS // 2

    def send_z(j):
        for k in range(NZ - 1):
            for c in range(2):
                q_z(j, k, c).start()

    for j in range(per_core):
        q_own(j).start()
        q_sib(j).start()
        if j == 0:
            send_z(0)
    for s in range(SLOTS):
        z_arrived(s, mz)
    nk_own.start()
    nk_copy.start()
    kv_own.wait()
    k_copy.start()

    @pl.loop(0, kv_ref.shape[0])
    def _(b):
        vt_own[b] = kv_ref[b, :, HEAD:].T

    v_copy.start()
    for z in others:
        z_arrived(0, z)
        z_arrived(1, z)
    send_z(1)
    w_own.start()
    stage_r(0)
    stage_r(1)

    key = lax.broadcasted_iota(jnp.int32, (BLOCK, NEW), 0)

    def attend(s, y, z):
        r = dev(y, z, owner(s)) * 2 + which(s)
        q = qbuf[s, y, z]
        codes = [tab[0, r], tab[1, r]]
        blocks = [c % 32 for c in codes]
        counts = [c // 32 for c in codes]
        keys = [kv_ref[blocks[0], :, :HEAD], k_sib[blocks[1]]]
        values = [vt_own[blocks[0]], vt_sib[blocks[1]]]
        t = [jnp.where(key < n, nt(k, q) * LOG2_SCALE, -jnp.inf) for k, n in zip(keys, counts)]
        m = jnp.maximum(jnp.max(t[0], axis=0, keepdims=True), jnp.max(t[1], axis=0, keepdims=True))
        m = jnp.maximum(m, FLOOR).astype(jnp.bfloat16).astype(jnp.float32)
        e = [jnp.exp2(x - m) for x in t]
        l = jnp.sum(e[0], axis=0, keepdims=True) + jnp.sum(e[1], axis=0, keepdims=True)
        o = [
            jnp.dot(v, x.astype(jnp.bfloat16), preferred_element_type=jnp.float32)
            for v, x in zip(values, e)
        ]
        put(part, (s, y, z), o[0] + o[1], m, l)

    def p_2(s, d, j):
        return remote(
            part.at[s, across, 2 * d + j], r2.at[s, d, j],
            p2_send, p2_recv.at[s, d], pool=dev((up, down)[d], mz, core),
        )

    def p_1(s, d, z):
        to = (up, down)[d]
        return remote(
            part.at[s, to, z], r1.at[s, d, z], p1_send, p1_recv.at[s, d], pool=dev(to, mz, core)
        )

    def p_z(s, k):
        z = others[k]
        return remote(part.at[s, my, z], rz.at[s, k], pz_send, pz_recv.at[s], pool=dev(my, z, core))

    def stage_c(s):
        @pl.when(s == 0)
        def _():
            for z in range(NZ):
                attend(s, my, z)

        for d in range(2):
            y_arrived(s, d, 1)
        wait_into(qbuf.at[s, across], qr_recv.at[s])

        for z in range(NZ):
            attend(s, across, z)
        for j in range(2):
            p_2(s, 0, j).start()
            p_2(s, 1, j).start()

        @pl.when(jnp.logical_and(s >= 1, s + 1 < SLOTS))
        def _():
            stage_r(s + 1)

        @pl.when(s == 0)
        def _():
            for z in others:
                z_arrived(2, z)

        for j in range(2):
            attend(s, up, 2 + j)
            attend(s, down, j)
        for j in range(2):
            p_1(s, 0, 2 + j).start()
            p_1(s, 1, j).start()

        for j in range(2):
            attend(s, up, j)
            attend(s, down, 2 + j)
        @pl.when(s > 0)
        def _():
            for z in range(NZ):
                attend(s, my, z)

    def stage_m(s):
        for d in range(2):
            wait_into(r2.at[s, d], p2_recv.at[s, d])
            for j in range(2):
                z, to = 2 * d + j, (up, down)[d]
                put(part, (s, to, z), *merge([get(part, (s, to, z)), get(r2, (s, d, j))]))
                p_1(s, d, z).start()

        @pl.when(s + 3 < SLOTS)
        def _():
            for z in others:
                z_arrived(s + 3, z)

        @pl.when(jnp.logical_or(s == 0, s == 2))
        def _():
            send_z(lax.div(s, 2) + 2)

    def stage_h(s):
        for d in range(2):
            wait_into(r1.at[s, d], p1_recv.at[s, d])
        for k, z in enumerate((*others, mz)):
            put(part, (s, my, z), *merge([get(part, (s, my, z)), get(r1, (s, 0, z)), get(r1, (s, 1, z))]))
            if k < NZ - 1:
                p_z(s, k).start()

    def fresh(s):
        q = qbuf[s, my, mz]
        rows = nkv[owner(s), tokens(which(s)), :]
        j = lax.broadcasted_iota(jnp.int32, (NEW, NEW), 0)
        i = lax.broadcasted_iota(jnp.int32, (NEW, NEW), 1) % (4 * PART)
        i = i + i // PART * PART + share(s) * PART
        t = jnp.where(j <= i, nt(rows[:, :HEAD], q) * LOG2_SCALE, -jnp.inf)
        m = jnp.max(t, axis=0, keepdims=True).astype(jnp.bfloat16).astype(jnp.float32)
        e = jnp.exp2(t - m)
        o = jnp.dot(rows[:, HEAD:].T, e.astype(jnp.bfloat16), preferred_element_type=jnp.float32)
        return o, m, jnp.sum(e, axis=0, keepdims=True)

    def a_copy(s):
        mine = att.at[s, :, half(core)]
        return remote(mine, mine, at_send, at_recv.at[s], pool=here)

    def stage_f(s):
        parts = [fresh(s), get(part, (s, my, mz))]
        wait_into(rz.at[s], pz_recv.at[s])
        parts += [get(rz, (s, k)) for k in range(NZ - 1)]
        o, _, l = merge(parts)
        o = o / l
        o = o.T
        att[s, :, half(core)] = jnp.concatenate([o[: 4 * PART], o[4 * PART :]], axis=1).astype(jnp.bfloat16)
        a_copy(s).start()

    def is_dest(s):
        return lax.div(mx, 2) == which(s)

    def sent_half(s):
        return jnp.where(is_dest(s), 1 - lax.rem(mx, 2), lax.rem(mx, 2))

    def rows(h):
        return pl.ds(pl.multiple_of(h * 2 * PART, 2 * PART), 2 * PART)

    def part_of(h, z):
        return pl.ds(pl.multiple_of((2 * h + z) * PART, PART), PART)

    def cols(n):
        return pl.ds(pl.multiple_of(n * chunk, chunk), chunk)

    def x_1(s, n):
        return remote(
            proj.at[s, rows(sent_half(s)), cols(n)], x1.at[s, :, cols(n)],
            x1_send, x1_recv.at[s, n], tp=tp_of(pair, zh),
        )

    def x_2(s, n):
        return remote(
            proj.at[s, rows(1 - sent_half(s)), cols(n)], x2.at[s, :, cols(n)],
            x2_send, x2_recv.at[lax.div(s, 2), n], tp=tp_of(facing, zh),
        )

    def z_h(s, n):
        return remote(
            zout.at[s, :, cols(n)], zin.at[s, core, :, cols(n)], zh_send, zh_recv.at[share(s), core, n],
            pool=dev(my, mz, owner(s)), tp=tp_of(mx, 1 - zh),
        )

    def s_in(s, n):
        return remote(sout.at[s, :, cols(n)], sin.at[s, :, cols(n)], si_send, si_recv.at[share(s), n], pool=here)

    def stage_o(s):
        @pl.when(s == 0)
        def _():
            w_own.wait()

        theirs = att.at[s, :, half(sib)]
        wait_into(theirs, at_recv.at[s])

        @pl.loop(0, CHUNKS)
        def _(n):
            proj[s, :, cols(n)] = jnp.dot(
                att[s], w[:, cols(n)], preferred_element_type=jnp.float32
            ).astype(jnp.bfloat16)
            x_1(s, n).start()

    def f32(x):
        return x.astype(jnp.float32)

    def stage_x(s):
        @pl.when(jnp.logical_not(is_dest(s)))
        def _():
            keep = 1 - sent_half(s)

            @pl.loop(0, CHUNKS)
            def _(n):
                wait_into(x1.at[s, :, cols(n)], x1_recv.at[s, n])
                total = f32(proj[s, rows(keep), cols(n)]) + f32(x1[s, :, cols(n)])
                proj[s, rows(keep), cols(n)] = total.astype(jnp.bfloat16)
                x_2(s, n).start()

    def stage_d(s):
        @pl.when(is_dest(s))
        def _():
            keep = 1 - sent_half(s)

            def total(n, z):
                t = f32(proj[s, part_of(keep, z), cols(n)])
                return t + f32(x1[s, part_of(0, z), cols(n)]) + f32(x2[s, part_of(0, z), cols(n)])

            @pl.loop(0, CHUNKS)
            def _(n):
                wait_into(x1.at[s, :, cols(n)], x1_recv.at[s, n])
                wait_into(x2.at[s, :, cols(n)], x2_recv.at[lax.div(s, 2), n])
                zout[s, :, cols(n)] = total(n, 1 - zh).astype(jnp.bfloat16)
                z_h(s, n).start()

                @pl.when(owner(s) != core)
                def _():
                    sout[s, :, cols(n)] = total(n, zh).astype(jnp.bfloat16)
                    s_in(s, n).start()

    def stage_e(s):
        @pl.when(jnp.logical_and(is_dest(s), owner(s) == core))
        def _():
            keep = 1 - sent_half(s)
            out_rows = pl.ds(pl.multiple_of(share(s) * PART, PART), PART)

            @pl.loop(0, CHUNKS)
            def _(n):
                own = f32(proj[s, part_of(keep, zh), cols(n)])
                own += f32(x1[s, part_of(0, zh), cols(n)]) + f32(x2[s, part_of(0, zh), cols(n)])
                wait_into(sin.at[s, :, cols(n)], si_recv.at[share(s), n])
                for c, t in ((core, own), (sib, f32(sin[s, :, cols(n)]))):
                    wait_into(zin.at[s, c, :, cols(n)], zh_recv.at[share(s), c, n])
                    at = pl.ds(pl.multiple_of(c * width + n * chunk, chunk), chunk)
                    t += f32(zin[s, c, :, cols(n)]) + f32(res_ref[out_rows, at])
                    out_ref[out_rows, at] = t.astype(jnp.bfloat16)

    nk_own.wait()
    for copy in (k_copy, nk_copy, v_copy):
        copy.wait_send()
    wait_into(nkv.at[sib], kv_recv.at[0])
    wait_into(k_sib, kv_recv.at[1])
    wait_into(vt_sib, kv_recv.at[2])

    @pl.loop(0, SLOTS + 2)
    def _(t):
        def stage(f, s):
            @pl.when(jnp.logical_and(s >= 0, s < SLOTS))
            def _():
                f(s)

        stage(stage_c, t)
        stage(stage_h, t - 1)
        stage(stage_f, jnp.where(t < SLOTS - 1, t - 2, -1))
        stage(stage_m, t)
        stage(stage_f, jnp.where(t < SLOTS - 1, -1, t - 2))
        stage(stage_o, t - 2)
        stage(stage_d, jnp.where(t < SLOTS, t - 4, jnp.where(t > SLOTS, SLOTS - 4, -1)))
        stage(stage_x, t - 3)
        stage(stage_e, t - 7)

    stage_d(SLOTS - 3)
    stage_x(SLOTS - 1)
    for s in range(SLOTS - 2, SLOTS):
        stage_d(s)

    @pl.loop(SLOTS - 5, SLOTS)
    def _(s):
        stage_e(s)

    for ref, sem in (
        (qbuf.at[pl.ds(0, 6), 0], qz_send),
        (qbuf.at[0, 0], qs_send),
        (qbuf.at[pl.ds(0, 4)], qy_send),
        (qbuf.at[pl.ds(0, 2)], qr_send),
        (part.at[pl.ds(0, 2)], p2_send),
        (part.at[pl.ds(0, 4)], p1_send),
        (part.at[pl.ds(0, 6), 0], pz_send),
        (att.at[:, :, pl.ds(0, 2 * HEAD)], at_send),
        (x1, x1_send),
        (x2.at[pl.ds(0, SLOTS // 2)], x2_send),
        (zout.at[pl.ds(0, SLOTS // 2)], zh_send),
        (sout.at[pl.ds(0, SLOTS // 4)], si_send),
    ):
        wait_into(ref, sem)

def layer(tab, queries, nkv, store, residual, weight):
    bf = jnp.bfloat16
    blocks = store.shape[0]
    depth, width = weight.shape[0], weight.shape[1] // 2
    vmem = pl.BlockSpec(memory_space=pltpu.VMEM)
    dma = pltpu.SemaphoreType.DMA
    unit = (ROWS, NEW)
    one = dma(())
    return pl.pallas_call(
        layer_kernel,
        out_shape=jax.ShapeDtypeStruct(residual.shape, bf),
        in_specs=[pl.BlockSpec(memory_space=pltpu.SMEM)] + [vmem] * 3 + [pl.BlockSpec(memory_space=pl.ANY)] * 2,
        out_specs=vmem,
        scratch_shapes=[
            pltpu.VMEM(store.shape, bf),
            pltpu.VMEM((2, 2, 2, NEW, HEAD), bf),
            pltpu.VMEM((SLOTS, NY, NZ, NEW, HEAD), bf),
            pltpu.VMEM((blocks, BLOCK, HEAD), bf),
            pltpu.VMEM((blocks, HEAD, BLOCK), bf),
            pltpu.VMEM((blocks, HEAD, BLOCK), bf),
            pltpu.VMEM((2, 2 * NEW, 2 * HEAD), bf),
            pltpu.VMEM((SLOTS, NY, NZ) + unit, bf),
            pltpu.VMEM((SLOTS, 2, 2) + unit, bf),
            pltpu.VMEM((SLOTS, 2, NZ) + unit, bf),
            pltpu.VMEM((SLOTS, NZ - 1) + unit, bf),
            pltpu.VMEM((SLOTS, 4 * PART, 4 * HEAD), bf),
            pltpu.VMEM((depth, width), bf),
            pltpu.VMEM((SLOTS, 4 * PART, width), bf),
            pltpu.VMEM((SLOTS, 2 * PART, width), bf),
            pltpu.VMEM((SLOTS, 2 * PART, width), bf),
            pltpu.VMEM((SLOTS, PART, width), bf),
            pltpu.VMEM((SLOTS, 2, PART, width), bf),
            pltpu.VMEM((SLOTS, PART, width), bf),
            pltpu.VMEM((SLOTS, PART, width), bf),
            dma((3,)), dma((3,)), dma((3,)),
            one, one, dma((SLOTS, NZ)),
            one, dma((SLOTS, 2, 2)), one, dma((SLOTS,)),
            one, dma((SLOTS, 2)), one, dma((SLOTS, 2)),
            one, dma((SLOTS,)), one, dma((SLOTS,)),
            one, dma((SLOTS, CHUNKS)), one, dma((SLOTS // 2, CHUNKS)),
            one, dma((2, 2, CHUNKS)), one, dma((2, CHUNKS)),
        ],
        compiler_params=pltpu.CompilerParams(
            collective_id=0, has_side_effects=True, vmem_limit_bytes=56 * 1024 * 1024
        ),
    )(tab, queries, nkv, residual, store, weight)


def hit_table(hit_dev, hit_blk, prefix_len):
    me = lax.axis_index("pool")
    there = jnp.stack([me, me + 1 - 2 * (me % 2)])[:, None, None]
    start = jnp.arange(MAXB, dtype=jnp.int32) * BLOCK
    count = jnp.clip(prefix_len[:, None] - start[None, :], 0, BLOCK)
    return jnp.sum(jnp.where(hit_dev[None] == there, (hit_blk + 32 * count)[None], 0), axis=2)


def shards(queries, new_key_values, key_value_store, o_weight, residual, hit_dev, hit_blk, prefix_len):
    tab = hit_table(hit_dev, hit_blk, prefix_len)
    return layer(tab, queries, new_key_values, key_value_store, residual, o_weight)


def solution(mesh):
    placed = (
        P("pool", "tp"),
        P("pool", "tp"),
        P("pool", None, "tp"),
        P("tp", None),
        P(("pool", "tp"), None),
        P(),
        P(),
        P(),
    )
    return jax.shard_map(
        shards, mesh=mesh, in_specs=placed, out_specs=P(("pool", "tp"), None), check_vma=False
    )
```

```python
import functools
import math

import jax
import jax.numpy as jnp
from jax import lax
from jax.experimental import pallas as pl
from jax.experimental.pallas import tpu as pltpu
from jax.sharding import PartitionSpec as P

HEAD = 128
NEW = 128
BLOCK = 256
MAXB = 16
NY = 4
NZ = 4
NX = 4
PART = 16
SLOTS = 8
CHUNKS = 4
LOG2_SCALE = HEAD**-0.5 * math.log2(math.e)
FLOOR = -1e30
ROWS = 144
MESH = pl.DeviceIdType.MESH


def nt(a, b):
    return lax.dot_general(a, b, (((1,), (1,)), ((), ())), preferred_element_type=jnp.float32)


def put(ref, at, o, m, l):
    ref[at + (slice(0, HEAD), slice(None))] = o.astype(jnp.bfloat16)
    high = l.astype(jnp.bfloat16).astype(jnp.float32)
    row = lax.broadcasted_iota(jnp.int32, (16, NEW), 0)
    stats = jnp.where(row == 0, m, jnp.where(row == 1, high, jnp.where(row == 2, l - high, 0.0)))
    ref[at + (slice(HEAD, ROWS), slice(None))] = stats.astype(jnp.bfloat16)


def get(ref, at):
    o = ref[at + (slice(0, HEAD), slice(None))].astype(jnp.float32)
    stats = ref[at + (slice(HEAD, ROWS), slice(None))].astype(jnp.float32)
    return o, stats[0:1], stats[1:2] + stats[2:3]


def merge(parts):
    m = functools.reduce(jnp.maximum, [p[1] for p in parts])
    o, l = 0.0, 0.0
    for po, pm, ps in parts:
        w = jnp.exp2(pm - m)
        o, l = o + po * w, l + ps * w
    return o, m, l


def layer_kernel(
    tab, q_ref, nkv_ref, res_ref, store_ref, w_ref, out_ref,
    kv_ref, qsrc, qbuf, k_sib, vt_own, vt_sib, nkv, part, r2, r1, rz, att,
    w, proj, x1, x2, zout, zin, sout, sin,
    kv_send, kv_recv, local,
    qs_send, qz_send, qz_recv, qy_send, qy_recv, qr_send, qr_recv,
    p2_send, p2_recv, p1_send, p1_recv, pz_send, pz_recv, at_send, at_recv,
    x1_send, x1_recv, x2_send, x2_recv, zh_send, zh_recv, si_send, si_recv,
):
    kv_own = pltpu.make_async_copy(store_ref, kv_ref, local.at[2])
    kv_own.start()
    me, tp = lax.axis_index("pool"), lax.axis_index("tp")
    core = lax.rem(me, 2)
    mz = lax.rem(lax.div(me, 2), NZ)
    my = lax.div(me, 2 * NZ)
    zh = lax.rem(tp, 2)
    mx = lax.div(tp, 2)
    up, down = lax.rem(my + 1, NY), lax.rem(my + NY - 1, NY)
    across = lax.rem(my + 2, NY)
    sib = 1 - core
    others = (mz + 1 - 2 * lax.rem(mz, 2), lax.rem(mz + 2, NZ), NZ - 1 - mz)
    pair, facing = mx + 1 - 2 * lax.rem(mx, 2), NX - 1 - mx
    width = w.shape[1]
    chunk = width // CHUNKS

    def dev(y, z, c):
        return (y * NZ + z) * 2 + c

    def tp_of(x, h):
        return x * 2 + h

    def remote(src, dst, send, recv, **to):
        return pltpu.make_async_remote_copy(
            src_ref=src, dst_ref=dst, send_sem=send, recv_sem=recv, device_id=to, device_id_type=MESH
        )

    def wait_into(ref, sem):
        pltpu.make_async_copy(ref, ref, sem).wait()

    barrier = pltpu.get_barrier_semaphore()
    partners = [{"pool": dev(my, z, c)} for z in others for c in range(2)]
    partners += [{"pool": p} for p in (dev(my, mz, sib), dev(up, mz, core), dev(down, mz, core))]
    partners += [{"tp": p} for p in (tp_of(pair, zh), tp_of(facing, zh))]
    partners += [{"pool": dev(my, mz, c), "tp": tp_of(mx, 1 - zh)} for c in range(2)]
    for p in partners:
        pl.semaphore_signal(barrier, inc=1, device_id=p, device_id_type=MESH)

    for i in range(2):
        for g in range(2):
            for h in range(4):
                for b in range(4):
                    to, at = (h % 2 * 4 + b) * PART, i * NEW + (2 * b + g) * PART
                    qsrc[i, g, h // 2, to : to + PART, :] = q_ref[at : at + PART, h * HEAD : (h + 1) * HEAD]

    pl.semaphore_wait(barrier, len(partners))

    def half(c):
        return pl.ds(pl.multiple_of(c * 2 * HEAD, 2 * HEAD), 2 * HEAD)

    def columns(c):
        return pl.ds(pl.multiple_of(c * width, width), width)

    def owner(s):
        return lax.rem(s, 2)

    def which(s):
        return lax.rem(lax.rem(s, 2) + lax.div(s, 4), 2)

    def share(s):
        return lax.rem(lax.div(s, 2), 2)

    def tokens(i):
        return pl.ds(pl.multiple_of(i * NEW, NEW), NEW)

    def q_z(j, k, c):
        s = 2 * j + core
        return remote(
            qsrc.at[which(s), share(s), c], qbuf.at[s, my, mz],
            qz_send, qz_recv.at[s, mz], pool=dev(my, others[k], c),
        )

    def q_sib(j):
        s = 2 * j + core
        return remote(
            qsrc.at[which(s), share(s), sib], qbuf.at[s, my, mz],
            qs_send, qz_recv.at[s, mz], pool=dev(my, mz, sib),
        )

    def q_own(j):
        s = 2 * j + core
        return pltpu.make_async_copy(qsrc.at[which(s), share(s), core], qbuf.at[s, my, mz], qz_recv.at[s, mz])

    here = dev(my, mz, sib)
    nk_copy = remote(nkv_ref, nkv.at[core], kv_send.at[0], kv_recv.at[0], pool=here)
    k_copy = remote(kv_ref.at[:, :, pl.ds(0, HEAD)], k_sib, kv_send.at[1], kv_recv.at[1], pool=here)
    v_copy = remote(vt_own, vt_sib, kv_send.at[2], kv_recv.at[2], pool=here)
    nk_own = pltpu.make_async_copy(nkv_ref, nkv.at[core], local.at[0])
    w_own = pltpu.make_async_copy(w_ref.at[:, columns(core)], w, local.at[1])

    def q_y(s, d, z):
        piece = qbuf.at[s, my, z]
        passed = lax.div(z, 2) if d == 0 else 1 - lax.div(z, 2)
        return remote(piece, piece, qy_send, qy_recv.at[s, d, passed], pool=dev((up, down)[d], mz, core))

    def q_relay(s, d, j):
        to, of = ((up, down), (down, up))[d]
        piece = qbuf.at[s, of, 2 * d + j]
        return remote(piece, piece, qr_send, qr_recv.at[s], pool=dev(to, mz, core))

    def z_arrived(s, z):
        wait_into(qbuf.at[s, my, z], qz_recv.at[s, z])
        q_y(s, 0, z).start()
        q_y(s, 1, z).start()

    def y_arrived(s, d, passed):
        first = 2 * d if passed == 0 else 2 - 2 * d
        wait_into(qbuf.at[s, (down, up)[d], pl.ds(first, 2)], qy_recv.at[s, d, passed])

    def stage_r(s):
        for d in range(2):
            y_arrived(s, d, 0)
            for j in range(2):
                q_relay(s, d, j).start()

    per_core = SLOTS // 2

    def send_z(j):
        for k in range(NZ - 1):
            for c in range(2):
                q_z(j, k, c).start()

    for j in range(per_core):
        q_own(j).start()
        q_sib(j).start()
        if j == 0:
            send_z(0)
    for s in range(SLOTS):
        z_arrived(s, mz)
    nk_own.start()
    nk_copy.start()
    kv_own.wait()
    k_copy.start()

    @pl.loop(0, kv_ref.shape[0])
    def _(b):
        vt_own[b] = kv_ref[b, :, HEAD:].T

    v_copy.start()
    for z in others:
        z_arrived(0, z)
        z_arrived(1, z)
    send_z(1)
    w_own.start()
    stage_r(0)
    stage_r(1)

    key = lax.broadcasted_iota(jnp.int32, (BLOCK, NEW), 0)

    def attend(s, y, z):
        r = dev(y, z, owner(s)) * 2 + which(s)
        q = qbuf[s, y, z]
        codes = [tab[0, r], tab[1, r]]
        blocks = [c % 32 for c in codes]
        counts = [c // 32 for c in codes]
        keys = [kv_ref[blocks[0], :, :HEAD], k_sib[blocks[1]]]
        values = [vt_own[blocks[0]], vt_sib[blocks[1]]]
        t = [jnp.where(key < n, nt(k, q) * LOG2_SCALE, -jnp.inf) for k, n in zip(keys, counts)]
        m = jnp.maximum(jnp.max(t[0], axis=0, keepdims=True), jnp.max(t[1], axis=0, keepdims=True))
        m = jnp.maximum(m, FLOOR).astype(jnp.bfloat16).astype(jnp.float32)
        e = [jnp.exp2(x - m) for x in t]
        l = jnp.sum(e[0], axis=0, keepdims=True) + jnp.sum(e[1], axis=0, keepdims=True)
        o = [
            jnp.dot(v, x.astype(jnp.bfloat16), preferred_element_type=jnp.float32)
            for v, x in zip(values, e)
        ]
        put(part, (s, y, z), o[0] + o[1], m, l)

    def p_2(s, d, j):
        return remote(
            part.at[s, across, 2 * d + j], r2.at[s, d, j],
            p2_send, p2_recv.at[s, d], pool=dev((up, down)[d], mz, core),
        )

    def p_1(s, d, z):
        to = (up, down)[d]
        return remote(
            part.at[s, to, z], r1.at[s, d, z], p1_send, p1_recv.at[s, d], pool=dev(to, mz, core)
        )

    def p_z(s, k):
        z = others[k]
        return remote(part.at[s, my, z], rz.at[s, k], pz_send, pz_recv.at[s], pool=dev(my, z, core))

    def stage_c(s):
        @pl.when(s == 0)
        def _():
            for z in range(NZ):
                attend(s, my, z)

        for d in range(2):
            y_arrived(s, d, 1)
        wait_into(qbuf.at[s, across], qr_recv.at[s])

        for z in range(NZ):
            attend(s, across, z)
        for j in range(2):
            p_2(s, 0, j).start()
            p_2(s, 1, j).start()

        @pl.when(jnp.logical_and(s >= 1, s + 1 < SLOTS))
        def _():
            stage_r(s + 1)

        @pl.when(s == 0)
        def _():
            for z in others:
                z_arrived(2, z)

        for j in range(2):
            attend(s, up, 2 + j)
            attend(s, down, j)
        for j in range(2):
            p_1(s, 0, 2 + j).start()
            p_1(s, 1, j).start()

        for j in range(2):
            attend(s, up, j)
            attend(s, down, 2 + j)
        @pl.when(s > 0)
        def _():
            for z in range(NZ):
                attend(s, my, z)

    def stage_m(s):
        for d in range(2):
            wait_into(r2.at[s, d], p2_recv.at[s, d])
            for j in range(2):
                z, to = 2 * d + j, (up, down)[d]
                put(part, (s, to, z), *merge([get(part, (s, to, z)), get(r2, (s, d, j))]))
                p_1(s, d, z).start()

        @pl.when(s + 3 < SLOTS)
        def _():
            for z in others:
                z_arrived(s + 3, z)

        @pl.when(jnp.logical_or(s == 0, s == 2))
        def _():
            send_z(lax.div(s, 2) + 2)

    def stage_h(s):
        for d in range(2):
            wait_into(r1.at[s, d], p1_recv.at[s, d])
        for k, z in enumerate((*others, mz)):
            put(part, (s, my, z), *merge([get(part, (s, my, z)), get(r1, (s, 0, z)), get(r1, (s, 1, z))]))
            if k < NZ - 1:
                p_z(s, k).start()

    def fresh(s):
        q = qbuf[s, my, mz]
        rows = nkv[owner(s), tokens(which(s)), :]
        j = lax.broadcasted_iota(jnp.int32, (NEW, NEW), 0)
        i = lax.broadcasted_iota(jnp.int32, (NEW, NEW), 1) % (4 * PART)
        i = i + i // PART * PART + share(s) * PART
        t = jnp.where(j <= i, nt(rows[:, :HEAD], q) * LOG2_SCALE, -jnp.inf)
        m = jnp.max(t, axis=0, keepdims=True).astype(jnp.bfloat16).astype(jnp.float32)
        e = jnp.exp2(t - m)
        o = jnp.dot(rows[:, HEAD:].T, e.astype(jnp.bfloat16), preferred_element_type=jnp.float32)
        return o, m, jnp.sum(e, axis=0, keepdims=True)

    def a_copy(s):
        mine = att.at[s, :, half(core)]
        return remote(mine, mine, at_send, at_recv.at[s], pool=here)

    def stage_f(s):
        parts = [fresh(s), get(part, (s, my, mz))]
        wait_into(rz.at[s], pz_recv.at[s])
        parts += [get(rz, (s, k)) for k in range(NZ - 1)]
        o, _, l = merge(parts)
        o = o / l
        o = o.T
        att[s, :, half(core)] = jnp.concatenate([o[: 4 * PART], o[4 * PART :]], axis=1).astype(jnp.bfloat16)
        a_copy(s).start()

    def is_dest(s):
        return lax.div(mx, 2) == which(s)

    def sent_half(s):
        return jnp.where(is_dest(s), 1 - lax.rem(mx, 2), lax.rem(mx, 2))

    def rows(h):
        return pl.ds(pl.multiple_of(h * 2 * PART, 2 * PART), 2 * PART)

    def part_of(h, z):
        return pl.ds(pl.multiple_of((2 * h + z) * PART, PART), PART)

    def cols(n):
        return pl.ds(pl.multiple_of(n * chunk, chunk), chunk)

    def x_1(s, n):
        return remote(
            proj.at[s, rows(sent_half(s)), cols(n)], x1.at[s, :, cols(n)],
            x1_send, x1_recv.at[s, n], tp=tp_of(pair, zh),
        )

    def x_2(s, n):
        return remote(
            proj.at[s, rows(1 - sent_half(s)), cols(n)], x2.at[s, :, cols(n)],
            x2_send, x2_recv.at[lax.div(s, 2), n], tp=tp_of(facing, zh),
        )

    def z_h(s, n):
        return remote(
            zout.at[s, :, cols(n)], zin.at[s, core, :, cols(n)], zh_send, zh_recv.at[share(s), core, n],
            pool=dev(my, mz, owner(s)), tp=tp_of(mx, 1 - zh),
        )

    def s_in(s, n):
        return remote(sout.at[s, :, cols(n)], sin.at[s, :, cols(n)], si_send, si_recv.at[share(s), n], pool=here)

    def stage_o(s):
        @pl.when(s == 0)
        def _():
            w_own.wait()

        theirs = att.at[s, :, half(sib)]
        wait_into(theirs, at_recv.at[s])

        @pl.loop(0, CHUNKS)
        def _(n):
            proj[s, :, cols(n)] = jnp.dot(
                att[s], w[:, cols(n)], preferred_element_type=jnp.float32
            ).astype(jnp.bfloat16)
            x_1(s, n).start()

    def f32(x):
        return x.astype(jnp.float32)

    def stage_x(s):
        @pl.when(jnp.logical_not(is_dest(s)))
        def _():
            keep = 1 - sent_half(s)

            @pl.loop(0, CHUNKS)
            def _(n):
                wait_into(x1.at[s, :, cols(n)], x1_recv.at[s, n])
                total = f32(proj[s, rows(keep), cols(n)]) + f32(x1[s, :, cols(n)])
                proj[s, rows(keep), cols(n)] = total.astype(jnp.bfloat16)
                x_2(s, n).start()

    def stage_d(s):
        @pl.when(is_dest(s))
        def _():
            keep = 1 - sent_half(s)

            def total(n, z):
                t = f32(proj[s, part_of(keep, z), cols(n)])
                return t + f32(x1[s, part_of(0, z), cols(n)]) + f32(x2[s, part_of(0, z), cols(n)])

            @pl.loop(0, CHUNKS)
            def _(n):
                wait_into(x1.at[s, :, cols(n)], x1_recv.at[s, n])
                wait_into(x2.at[s, :, cols(n)], x2_recv.at[lax.div(s, 2), n])
                zout[s, :, cols(n)] = total(n, 1 - zh).astype(jnp.bfloat16)
                z_h(s, n).start()

                @pl.when(owner(s) != core)
                def _():
                    sout[s, :, cols(n)] = total(n, zh).astype(jnp.bfloat16)
                    s_in(s, n).start()

    def stage_e(s):
        @pl.when(jnp.logical_and(is_dest(s), owner(s) == core))
        def _():
            keep = 1 - sent_half(s)
            out_rows = pl.ds(pl.multiple_of(share(s) * PART, PART), PART)

            @pl.loop(0, CHUNKS)
            def _(n):
                own = f32(proj[s, part_of(keep, zh), cols(n)])
                own += f32(x1[s, part_of(0, zh), cols(n)]) + f32(x2[s, part_of(0, zh), cols(n)])
                wait_into(sin.at[s, :, cols(n)], si_recv.at[share(s), n])
                for c, t in ((core, own), (sib, f32(sin[s, :, cols(n)]))):
                    wait_into(zin.at[s, c, :, cols(n)], zh_recv.at[share(s), c, n])
                    at = pl.ds(pl.multiple_of(c * width + n * chunk, chunk), chunk)
                    t += f32(zin[s, c, :, cols(n)]) + f32(res_ref[out_rows, at])
                    out_ref[out_rows, at] = t.astype(jnp.bfloat16)

    nk_own.wait()
    for copy in (k_copy, nk_copy, v_copy):
        copy.wait_send()
    wait_into(nkv.at[sib], kv_recv.at[0])
    wait_into(k_sib, kv_recv.at[1])
    wait_into(vt_sib, kv_recv.at[2])

    @pl.loop(0, SLOTS + 2)
    def _(t):
        def stage(f, s):
            @pl.when(jnp.logical_and(s >= 0, s < SLOTS))
            def _():
                f(s)

        stage(stage_c, t)
        stage(stage_h, t - 1)
        stage(stage_f, jnp.where(t < SLOTS - 1, t - 2, -1))
        stage(stage_o, jnp.where(t < SLOTS - 1, t - 2, -1))
        stage(stage_m, t)
        stage(stage_f, jnp.where(t < SLOTS - 1, -1, t - 2))
        stage(stage_o, jnp.where(t < SLOTS - 1, -1, t - 2))
        stage(stage_d, jnp.where(t < SLOTS, t - 4, jnp.where(t > SLOTS, SLOTS - 4, -1)))
        stage(stage_x, t - 3)
        stage(stage_e, t - 7)

    stage_d(SLOTS - 3)
    stage_x(SLOTS - 1)
    for s in range(SLOTS - 2, SLOTS):
        stage_d(s)

    @pl.loop(SLOTS - 5, SLOTS)
    def _(s):
        stage_e(s)

    for ref, sem in (
        (qbuf.at[pl.ds(0, 6), 0], qz_send),
        (qbuf.at[0, 0], qs_send),
        (qbuf.at[pl.ds(0, 4)], qy_send),
        (qbuf.at[pl.ds(0, 2)], qr_send),
        (part.at[pl.ds(0, 2)], p2_send),
        (part.at[pl.ds(0, 4)], p1_send),
        (part.at[pl.ds(0, 6), 0], pz_send),
        (att.at[:, :, pl.ds(0, 2 * HEAD)], at_send),
        (x1, x1_send),
        (x2.at[pl.ds(0, SLOTS // 2)], x2_send),
        (zout.at[pl.ds(0, SLOTS // 2)], zh_send),
        (sout.at[pl.ds(0, SLOTS // 4)], si_send),
    ):
        wait_into(ref, sem)

def layer(tab, queries, nkv, store, residual, weight):
    bf = jnp.bfloat16
    blocks = store.shape[0]
    depth, width = weight.shape[0], weight.shape[1] // 2
    vmem = pl.BlockSpec(memory_space=pltpu.VMEM)
    dma = pltpu.SemaphoreType.DMA
    unit = (ROWS, NEW)
    one = dma(())
    return pl.pallas_call(
        layer_kernel,
        out_shape=jax.ShapeDtypeStruct(residual.shape, bf),
        in_specs=[pl.BlockSpec(memory_space=pltpu.SMEM)] + [vmem] * 3 + [pl.BlockSpec(memory_space=pl.ANY)] * 2,
        out_specs=vmem,
        scratch_shapes=[
            pltpu.VMEM(store.shape, bf),
            pltpu.VMEM((2, 2, 2, NEW, HEAD), bf),
            pltpu.VMEM((SLOTS, NY, NZ, NEW, HEAD), bf),
            pltpu.VMEM((blocks, BLOCK, HEAD), bf),
            pltpu.VMEM((blocks, HEAD, BLOCK), bf),
            pltpu.VMEM((blocks, HEAD, BLOCK), bf),
            pltpu.VMEM((2, 2 * NEW, 2 * HEAD), bf),
            pltpu.VMEM((SLOTS, NY, NZ) + unit, bf),
            pltpu.VMEM((SLOTS, 2, 2) + unit, bf),
            pltpu.VMEM((SLOTS, 2, NZ) + unit, bf),
            pltpu.VMEM((SLOTS, NZ - 1) + unit, bf),
            pltpu.VMEM((SLOTS, 4 * PART, 4 * HEAD), bf),
            pltpu.VMEM((depth, width), bf),
            pltpu.VMEM((SLOTS, 4 * PART, width), bf),
            pltpu.VMEM((SLOTS, 2 * PART, width), bf),
            pltpu.VMEM((SLOTS, 2 * PART, width), bf),
            pltpu.VMEM((SLOTS, PART, width), bf),
            pltpu.VMEM((SLOTS, 2, PART, width), bf),
            pltpu.VMEM((SLOTS, PART, width), bf),
            pltpu.VMEM((SLOTS, PART, width), bf),
            dma((3,)), dma((3,)), dma((3,)),
            one, one, dma((SLOTS, NZ)),
            one, dma((SLOTS, 2, 2)), one, dma((SLOTS,)),
            one, dma((SLOTS, 2)), one, dma((SLOTS, 2)),
            one, dma((SLOTS,)), one, dma((SLOTS,)),
            one, dma((SLOTS, CHUNKS)), one, dma((SLOTS // 2, CHUNKS)),
            one, dma((2, 2, CHUNKS)), one, dma((2, CHUNKS)),
        ],
        compiler_params=pltpu.CompilerParams(
            collective_id=0, has_side_effects=True, vmem_limit_bytes=56 * 1024 * 1024
        ),
    )(tab, queries, nkv, residual, store, weight)


def hit_table(hit_dev, hit_blk, prefix_len):
    me = lax.axis_index("pool")
    there = jnp.stack([me, me + 1 - 2 * (me % 2)])[:, None, None]
    start = jnp.arange(MAXB, dtype=jnp.int32) * BLOCK
    count = jnp.clip(prefix_len[:, None] - start[None, :], 0, BLOCK)
    return jnp.sum(jnp.where(hit_dev[None] == there, (hit_blk + 32 * count)[None], 0), axis=2)


def shards(queries, new_key_values, key_value_store, o_weight, residual, hit_dev, hit_blk, prefix_len):
    tab = hit_table(hit_dev, hit_blk, prefix_len)
    return layer(tab, queries, new_key_values, key_value_store, residual, o_weight)


def solution(mesh):
    placed = (
        P("pool", "tp"),
        P("pool", "tp"),
        P("pool", None, "tp"),
        P("tp", None),
        P(("pool", "tp"), None),
        P(),
        P(),
        P(),
    )
    return jax.shard_map(
        shards, mesh=mesh, in_specs=placed, out_specs=P(("pool", "tp"), None), check_vma=False
    )
```
